32 devices in a mesh: pitch: 8 (over z, x), span: 2 (over y), row: 2 (over core).
Axes of the slice: x: 2, y: 2, z: 4, core: 2. Of those that a mesh axis runs over, the one named last changes fastest.
Arguments:
- fields: float32 [3, 128, 32, 512], P(None, 'pitch', 'span', 'row'), may hold values from -6 to 6
- diffusivity: float32 [128, 32, 512], P('pitch', 'span', 'row'), may hold values from 0.01 to 0.1
- mean_flow: bfloat16 [32, 2, 512], P('span', None, 'row'), may hold values from -6 to 6
- radial_kernel: bfloat16 [32, 32], replicated
- tracer_values: float32 [10, 65536], P(None, ('pitch', 'span', 'row')), may hold values from -6 to 6
- tracer_cells: int32 [65536], P(('pitch', 'span', 'row')), may hold values from 0 to 65535
- tracer_dest: int32 [65536, 1], P(('pitch', 'span', 'row')), may hold values from 0 to 7; in each aligned block of 2048 rows (0 to 2047, 2048 to 4095, ...) at most 512 rows name the same one
- interface_map: int32 [2, 128], P('row', 'pitch'), may hold values from 0 to 127, as said below
Outputs:
- advected: float32 [3, 128, 32, 512], P(None, 'pitch', 'span', 'row')
- arrived: float32 [10, 131072], P(None, ('pitch', 'span', 'row'))
The draws below stay inside these ranges and needn't reach their ends.
Inputs may be any that keep to these rules, and one draw needn't show every extreme that they name: `tracer_cells`: the local index of the owning cell within the block of the device that holds the tracer, i * 16 * 256 + r * 256 + a for local indices i, r, a. `tracer_dest`: at most 512 of the tracers of one device go to one pitch index. `interface_map`: for one offset o of each draw, row 0 holds (i + o) mod 128 and row 1 holds (i - o) mod 128, so the two rows are inverse permutations.
All inputs are finite; a program needn't handle non-finite values.
Results may differ from the reference program's by a relative error of at most 0.0015.
Values may be sent and summed in bfloat16 or wider, within the bound.
No kernel may reach another device: no remote copies, remote signals or barrier semaphores. Data moves between devices by JAX's collectives and lax.ppermute only.
A program may use at most 128 MiB of HBM per device.

```python
import math
import jax
import jax.numpy as jnp
import numpy as np

CP = 16
CR = 16
CA = 256
TRACERS_DEV = 2048
FIELDS = 3
TRACER_VALUES = 10
SUB = 2
NPITCH = 128
NR = 32
NA = 512
CAP = 512
RECV = 4096
TRACERS = 65536
N_PITCH = 8
N_SPAN = 2
N_ROW = 2
DEVICES = 32


def draw_radial_kernel(key, part):
    index_rows = jnp.arange(NR, dtype=jnp.int32)
    identity = (index_rows[:, None] == index_rows[None, :]).astype(jnp.float32)
    noise = jax.random.normal(key, (NR, NR), jnp.float32)
    return (0.7 * identity + 0.7 * noise / math.sqrt(NR)).astype(jnp.bfloat16)


def draw_interface_map(key, part):
    block_key, cell_key = jax.random.split(jax.random.fold_in(key, 7))
    block_count = NPITCH // CP
    offset = CP * jax.random.randint(block_key, (), 1, block_count) + jax.random.randint(cell_key, (), 0, CP)
    pitch_index = jnp.arange(NPITCH, dtype=jnp.int32)
    return jnp.stack([(pitch_index + offset) % NPITCH, (pitch_index - offset) % NPITCH]).astype(jnp.int32)


def touch_ends(values, stream_key, smallest, high):
    longest = values.shape.index(max(values.shape))
    spots = []
    for shift in (0, 1):
        where = [jax.random.randint(jax.random.fold_in(stream_key, axis), (), 0, length) for axis, length in enumerate(values.shape)]
        where[longest] = (where[longest] + shift) % values.shape[longest]
        spots.append(tuple(where))
    return values.at[spots[0]].set(smallest).at[spots[1]].set(high)


def shard_levels(key, extent, shards, low, largest):
    loudness = 1.0
    for dim, parts in shards:
        heights = jax.random.uniform(jax.random.fold_in(jax.random.fold_in(key, 6), dim), (parts,), jnp.float32, low / len(shards), largest / len(shards))
        loudness = loudness * jnp.repeat(jnp.exp(heights), extent[dim] // parts).reshape((-1,) + (1,) * (len(extent) - 1 - dim))
    return loudness


def shared_out(key, own, number, rows, number_of, top, most, skew):
    ranking = jax.random.permutation(key, number_of)
    heavy_load, ordinary = portions_of(number_of, rows * top, most, skew, True), portions_of(number_of, rows * top, most, skew, False)
    places = jnp.arange(number_of)

    def named(sizes, offset_by):
        used = int((sizes > 0).sum())
        fixed = max(1, used // 4)
        passed = fixed + (places - fixed + offset_by * (used - fixed)) % max(1, number_of - fixed)
        return jnp.zeros((number_of,), jnp.int32).at[ranking[jnp.where(places < fixed, places, passed)]].set(jnp.asarray(sizes, jnp.int32))

    sizes = jnp.where(number % 4 == 0, named(heavy_load, number // 4), named(ordinary, number - number // 4 - 1))
    mixed = jax.random.permutation(jax.random.fold_in(own, 3), number_of)
    source_of, receiver = mixed[0:number_of // 2 * 2:2], mixed[1:number_of // 2 * 2:2]
    room = jnp.minimum(sizes[source_of] - 1, most - sizes[receiver]) // 2
    room = jnp.where((source_of == ranking[0]) | (receiver == ranking[0]) | (sizes[receiver] == 0), 0, jnp.maximum(room, 0))
    passed = jax.random.randint(jax.random.fold_in(own, 4), (number_of // 2,), 0, 1 << 20) % (room + 1)
    sizes = sizes.at[source_of].add(-passed).at[receiver].add(passed)
    members = jnp.searchsorted(jnp.cumsum(sizes), jnp.arange(rows * top), side="right").astype(jnp.int32)
    table = members.reshape(top, rows).T
    table = table[jax.random.permutation(jax.random.fold_in(own, 1), rows)]
    offset_by = jax.random.randint(jax.random.fold_in(own, 2), (rows, 1), 0, top)
    return jnp.take_along_axis(table, (jnp.arange(top)[None, :] + offset_by) % top, axis=1)


def portions_of(number_of, total, reach, skew, full):
    weights = [(1 << 20) // math.isqrt(rank ** skew) + 1 for rank in range(1, number_of + 1)]
    largest = reach if full else min(reach, max(-(-total // number_of), total * weights[0] // sum(weights)))
    least = 1 if total - largest >= number_of - 1 else 0
    counts, rest = [largest] + [least] * (number_of - 1), total - largest - least * (number_of - 1)
    while rest > 0:
        free = [i for i in range(1, number_of) if counts[i] < largest] or [i for i in range(1, number_of) if counts[i] < reach]
        mass, remaining = sum([weights[i] for i in free]), rest
        for i in free:
            extra = min(reach - counts[i], max(1, remaining * weights[i] // mass), rest)
            counts[i] = counts[i] + extra
            rest = rest - extra
    return np.array(counts)


def gaussian(key, shape, scale, limit, shards=(), held_as=jnp.bfloat16):
    entries = scale * jax.random.normal(key, shape, jnp.float32)
    if shards:
        entries = entries * shard_levels(key, shape, shards, -0.22, 0.18)
    return jnp.clip(entries, -limit, limit).astype(held_as)


def setup_inputs(seed: int = 0) -> dict:
    splits = jax.random.split(jax.random.key(seed), 9)
    fields = gaussian(splits[0], (FIELDS, NPITCH, NR, NA), 1.0, 6.0, ((1, 8), (2, 2), (3, 2)), jnp.float32)
    diffusivity = jnp.clip(jnp.exp(math.log(0.1) - 2.3025851 * jax.random.uniform(splits[1], (NPITCH, NR, NA), jnp.float32) ** shard_levels(splits[1], (NPITCH, NR, NA), ((0, 8), (1, 2), (2, 2)), -0.2, 0.2)), 0.01, 0.1)
    mean_flow = gaussian(splits[2], (NR, 2, NA), 1.0, 6.0, ((0, 2), (2, 2)))
    radial_kernel = draw_radial_kernel(jax.random.fold_in(splits[8], 71), 0)
    tracer_values = gaussian(splits[4], (TRACER_VALUES, TRACERS), 1.0, 6.0, ((1, 32),), jnp.float32)
    tracer_cells = touch_ends(jax.random.randint(splits[5], (TRACERS,), 0, CP * CR * CA), jax.random.fold_in(splits[5], 1), 0, (CP * CR * CA) - 1).astype(jnp.int32)
    tracer_dest_keys = jax.random.split(jax.random.fold_in(splits[6], 1), TRACERS // TRACERS_DEV)
    tracer_dest_turns = jax.random.permutation(jax.random.fold_in(splits[6], 3), TRACERS // TRACERS_DEV)
    tracer_dest = jax.vmap(lambda own, number: shared_out(jax.random.fold_in(splits[6], 2), own, number, TRACERS_DEV, N_PITCH, 1, CAP, 2))(tracer_dest_keys, tracer_dest_turns).reshape((TRACERS, 1))
    interface_map = draw_interface_map(jax.random.fold_in(splits[8], 71), 0)
    return dict(fields=fields, diffusivity=diffusivity, mean_flow=mean_flow, radial_kernel=radial_kernel, tracer_values=tracer_values, tracer_cells=tracer_cells, tracer_dest=tracer_dest, interface_map=interface_map)


TIME_STEP = 0.9
AXIAL_SPEED = 0.15
PITCH_SPEED = 0.15


def face_flux(left_values, right_values, left_kappa, right_kappa, face_speed):
    diffusion = -0.5 * (left_kappa + right_kappa) * (right_values - left_values)
    if face_speed is None:
        return diffusion
    return jnp.maximum(face_speed, 0.0) * left_values + jnp.minimum(face_speed, 0.0) * right_values + diffusion


def axial_line(array, ghost, row_number):
    upstream = (array[..., 0], ghost)[row_number]
    downstream = (ghost, array[..., -1])[row_number]
    return jnp.concatenate([upstream[..., None], array, downstream[..., None]], -1)


def advance_field(values, kappa, speed_axial, speed_pitch, ghost_values, ghost_kappa, ghost_speed, row_number):
    pitch_values = jnp.concatenate([values[-1:], values, values[:1]], 0)
    pitch_kappa = jnp.concatenate([kappa[-1:], kappa, kappa[:1]], 0)
    pitch_flux = face_flux(pitch_values[:-1], pitch_values[1:], pitch_kappa[:-1], pitch_kappa[1:], speed_pitch)
    radial_values = jnp.pad(values, ((0, 0), (1, 1), (0, 0)))
    radial_kappa = jnp.pad(kappa, ((0, 0), (1, 1), (0, 0)))
    face_index = jnp.arange(NR + 1, dtype=jnp.int32)
    wall_mask = ((face_index > 0) & (face_index < NR)).astype(jnp.float32)
    radial_flux = face_flux(radial_values[:, :-1], radial_values[:, 1:], radial_kappa[:, :-1], radial_kappa[:, 1:], None) * wall_mask[:, None]
    speed_full = jnp.broadcast_to(speed_axial[None], values.shape)
    line_values = axial_line(values, ghost_values, row_number)
    line_kappa = axial_line(kappa, ghost_kappa, row_number)
    line_speed = axial_line(speed_full, ghost_speed, row_number)
    face_speed = 0.5 * (line_speed[..., :-1] + line_speed[..., 1:])
    axial_flux = face_flux(line_values[..., :-1], line_values[..., 1:], line_kappa[..., :-1], line_kappa[..., 1:], face_speed)
    divergence = pitch_flux[1:] - pitch_flux[:-1] + radial_flux[:, 1:] - radial_flux[:, :-1] + axial_flux[..., 1:] - axial_flux[..., :-1]
    return values - TIME_STEP * divergence


def reference(fields, diffusivity, mean_flow, radial_kernel, tracer_values, tracer_cells, tracer_dest, interface_map):
    smoothed = jnp.dot(radial_kernel, mean_flow.reshape(NR, 2 * NA), preferred_element_type=jnp.float32).reshape(NR, 2, NA)
    speed_axial = AXIAL_SPEED * (1.0 + 0.5 * jnp.tanh(smoothed[:, 0]))
    speed_pitch = PITCH_SPEED * jnp.tanh(smoothed[:, 1])

    tracer_ids = jnp.arange(TRACERS, dtype=jnp.int32)
    device_ids = tracer_ids // TRACERS_DEV
    pitch_dev = device_ids // (N_SPAN * N_ROW)
    span_dev = (device_ids // N_ROW) % N_SPAN
    row_dev = device_ids % N_ROW
    global_pitch = pitch_dev * CP + tracer_cells // (CR * CA)
    global_radial = span_dev * CR + (tracer_cells // CA) % CR
    global_axial = row_dev * CA + tracer_cells % CA
    sample_fields = fields[:, global_pitch, global_radial, global_axial]
    sample_speed = jnp.stack([speed_axial[global_radial, global_axial], speed_pitch[global_radial, global_axial]])
    sampled = jnp.concatenate([sample_fields, sample_speed], 0)
    head_rows = tracer_values[:5]
    tail_rows = tracer_values[5:]
    updated = jnp.concatenate([head_rows + 0.5 * (sampled - head_rows), tail_rows + 0.8 * sampled], 0)
    targets = tracer_dest[:, 0]
    onehot = (targets.reshape(DEVICES, TRACERS_DEV)[:, :, None] == jnp.arange(N_PITCH, dtype=jnp.int32)[None, None]).astype(jnp.int32)
    slot_index = jnp.sum((jnp.cumsum(onehot, 1) - onehot) * onehot, 2).reshape(TRACERS)
    position = ((targets * N_SPAN + span_dev) * N_ROW + row_dev) * RECV + pitch_dev * CAP + slot_index
    arrived = jnp.zeros((TRACER_VALUES, DEVICES * RECV), jnp.float32).at[:, position].set(updated)

    current = fields
    for substep in range(SUB):
        plane_values = []
        plane_kappa = []
        plane_speed = []
        for row_number in range(2):
            plane = row_number * CA + (CA - 1) * (1 - row_number)
            plane_values.append(current[:, :, :, plane])
            plane_kappa.append(diffusivity[:, :, plane])
            plane_speed.append(jnp.broadcast_to(speed_axial[None, :, plane], (NPITCH, NR)))
        new_rows = []
        for row_number in range(2):
            other_row = 1 - row_number
            facing = interface_map[row_number]
            ghost_values = plane_values[other_row][:, facing, :]
            ghost_kappa = plane_kappa[other_row][facing, :]
            ghost_speed = plane_speed[other_row][facing, :]
            first_cell = row_number * CA
            kappa_row = diffusivity[:, :, first_cell:first_cell + CA]
            axial_row = speed_axial[:, first_cell:first_cell + CA]
            pitch_row = speed_pitch[:, first_cell:first_cell + CA]
            advanced = []
            for field_number in range(FIELDS):
                advanced.append(advance_field(current[field_number, :, :, first_cell:first_cell + CA], kappa_row, axial_row, pitch_row, ghost_values[field_number], ghost_kappa, ghost_speed, row_number))
            new_rows.append(jnp.stack(advanced))
        current = jnp.concatenate(new_rows, -1)
    return current, arrived
```

```python
import jax
import jax.numpy as jnp
from jax import lax
from jax.experimental import pallas as pl
from jax.experimental.pallas import tpu as pltpu
from jax.sharding import PartitionSpec as P

SUB = 2
TIME_STEP = 0.9
AXIAL_SPEED = 0.15
PITCH_SPEED = 0.15
LANES = 128
EXTRA = 8
SLAB = 32
F32 = jnp.float32
BF16 = jnp.bfloat16
VMEM = pl.BlockSpec(memory_space=pltpu.VMEM)
SMEM = pl.BlockSpec(memory_space=pltpu.SMEM)
VMEM_LIMIT = 48 * 1024 * 1024


def iota(shape, dim):
    return lax.broadcasted_iota(jnp.int32, shape, dim)


def split(x):
    high = x.astype(BF16)
    return high, (x - high.astype(F32)).astype(BF16)


def power(n):
    assert n & (n - 1) == 0
    return n.bit_length() - 1


def call(body, outs, args, specs, scratch=(), flops=0, nbytes=0):
    return pl.pallas_call(
        body,
        out_shape=tuple(jax.ShapeDtypeStruct(s, d) for s, d in outs),
        in_specs=list(specs),
        out_specs=tuple(VMEM for _ in outs),
        scratch_shapes=list(scratch),
        compiler_params=pltpu.CompilerParams(vmem_limit_bytes=VMEM_LIMIT),
        cost_estimate=pl.CostEstimate(flops=flops, bytes_accessed=nbytes, transcendentals=0),
    )(*args)


def edge_rows(f_ref, k_ref, rows):
    parts = []
    for r in rows:
        parts.append(f_ref[:, :, r, :].reshape(-1, f_ref.shape[3]))
        parts.append(k_ref[:, r, :])
    return jnp.concatenate(parts, 0)


def pack_span(f_ref, k_ref, m_ref, *outs):
    radial = f_ref.shape[2]
    top = edge_rows(f_ref, k_ref, (radial - 2, radial - 1))
    bottom = edge_rows(f_ref, k_ref, (0, 1))
    flow = m_ref[...].astype(F32)
    flow = jnp.concatenate([flow[:, 0, :], flow[:, 1, :]], 0).astype(BF16)
    if len(outs) == 1:
        edge = top.shape[0]
        first = lax.axis_index("span") == 0
        outs[0][:edge] = jnp.where(first, top, bottom).astype(BF16)
        outs[0][edge:] = flow
    else:
        outs[0][...] = top.astype(BF16)
        outs[1][...] = bottom.astype(BF16)
        outs[2][...] = flow


def sample_fields(npitch, f_ref, cell_ref, dest_ref, samp_ref, slot_ref):
    nfield, pitch, radial, axial = f_ref.shape
    lines = pitch * radial
    chunks = cell_ref.shape[0]
    table = f_ref[...].reshape(nfield * lines, axial)
    high, low = split(table)
    samp_ref[...] = jnp.zeros(samp_ref.shape, F32)
    for c in range(0, chunks, 2):
        cells = jnp.concatenate([cell_ref[c : c + 1, :], cell_ref[c + 1 : c + 2, :]], 1)
        width = cells.shape[1]
        lane = cells & (axial - 1)
        line = lax.shift_right_logical(cells, power(axial))
        pick = (iota((axial, width), 0) == lane).astype(F32).astype(BF16)
        got = jnp.dot(high, pick, preferred_element_type=F32) + jnp.dot(
            low, pick, preferred_element_type=F32
        )
        mine = iota((lines, width), 0) == line
        for f in range(nfield):
            part = jnp.where(mine, got[f * lines : (f + 1) * lines], 0.0)
            samp_ref[f : f + 1, c * LANES : c * LANES + width] = jnp.sum(part, 0, keepdims=True)
    ones = []
    for c in range(chunks):
        ones.append((iota((npitch, LANES), 0) == dest_ref[c : c + 1, :]).astype(F32))
    stacked = jnp.concatenate(ones, 0)
    before = (iota((LANES, LANES), 0) < iota((LANES, LANES), 1)).astype(F32).astype(BF16)
    prefix = jnp.dot(stacked.astype(BF16), before, preferred_element_type=F32)
    carry = jnp.zeros((npitch, 1), F32)
    for c in range(chunks):
        rank = prefix[c * npitch : (c + 1) * npitch] + carry
        slot = jnp.sum(rank * ones[c], 0, keepdims=True)
        slot_ref[:, c * LANES : (c + 1) * LANES] = slot.astype(jnp.int32)
        carry = carry + jnp.sum(ones[c], 1, keepdims=True)


def dispatch(
    npitch,
    nspan,
    f_ref,
    k_ref,
    m_ref,
    kern_ref,
    tv_ref,
    cell_ref,
    dest_ref,
    samp_ref,
    slot_ref,
    *refs,
):
    nfield, pitch, radial, axial = f_ref.shape
    planes = nfield + 1
    edge = planes * pitch
    if nspan == 2:
        (got_ref,) = refs[:1]
        refs = refs[1:]
        low_ref = high_ref = got_ref
    else:
        low_ref, high_ref, all_ref = refs[:3]
        refs = refs[3:]
    buf_ref, a_ref, b_ref, speed_ref, halo_ref, kern_s, upd_s, lhs_s, face_s = refs
    s = lax.axis_index("span")
    q = lax.axis_index("row")
    even = lax.rem(lax.axis_index("pitch"), 2) == 0

    total = kern_ref.shape[0]
    kern_s[...] = kern_ref[...].astype(F32)
    main = kern_s[pl.ds(pl.multiple_of(s * radial, 8), radial), :]
    above = kern_s[pl.ds(pl.multiple_of(jnp.minimum((s + 1) * radial, total - 8), 8), 8), :]
    below = kern_s[pl.ds(pl.multiple_of(jnp.maximum(s * radial - 8, 0), 8), 8), :]
    wide = jnp.concatenate([main, jnp.where(iota((EXTRA, total), 0) < 4, above, below)], 0).astype(BF16)
    smoothed = []
    flow = m_ref[...].astype(F32)
    for c in range(2):
        if nspan == 2:
            own = flow[:, c, :]
            other = got_ref[2 * edge + c * radial : 2 * edge + (c + 1) * radial, :].astype(F32)
            rows = [jnp.where(s == 0, own, other), jnp.where(s == 0, other, own)]
        else:
            rows = [all_ref[n, c * radial : (c + 1) * radial, :].astype(F32) for n in range(nspan)]
        smoothed.append(
            jnp.dot(wide, jnp.concatenate(rows, 0).astype(BF16), preferred_element_type=F32)
        )
    sa = AXIAL_SPEED * (1.0 + 0.5 * jnp.tanh(smoothed[0]))
    sp = PITCH_SPEED * jnp.tanh(smoothed[1])
    speed_ref[0] = sa
    speed_ref[1] = sp

    chunks = cell_ref.shape[0]
    high, low = split(jnp.concatenate([sa[:radial], sp[:radial]], 0))
    upd_s[...] = jnp.zeros(upd_s.shape, F32)
    for c in range(0, chunks, 2):
        cells = jnp.concatenate([cell_ref[c : c + 1, :], cell_ref[c + 1 : c + 2, :]], 1)
        width = cells.shape[1]
        span = slice(c * LANES, c * LANES + width)
        lane = cells & (axial - 1)
        line = lax.shift_right_logical(cells, power(axial)) & (radial - 1)
        pick = (iota((axial, width), 0) == lane).astype(F32).astype(BF16)
        got = jnp.dot(high, pick, preferred_element_type=F32) + jnp.dot(
            low, pick, preferred_element_type=F32
        )
        mine = iota((radial, width), 0) == line
        sampled = [samp_ref[f : f + 1, span] for f in range(nfield)]
        for n in range(2):
            part = jnp.where(mine, got[n * radial : (n + 1) * radial], 0.0)
            sampled.append(jnp.sum(part, 0, keepdims=True))
        count = len(sampled)
        for v, value in enumerate(sampled):
            head = tv_ref[v : v + 1, span]
            upd_s[v : v + 1, span] = head + 0.5 * (value - head)
            upd_s[count + v : count + v + 1, span] = tv_ref[count + v : count + v + 1, span] + 0.8 * value

    values = tv_ref.shape[0]
    tracers = tv_ref.shape[1]
    capacity = 2 * tracers // npitch
    pad = upd_s.shape[0]
    both = upd_s[...]
    rounded = both.astype(BF16).astype(F32)
    both = jnp.concatenate([rounded, both - rounded], 0)
    dest = jnp.concatenate([dest_ref[c : c + 1, :] for c in range(chunks)], 1)
    for d in range(npitch):
        lhs_s[d * 2 * pad : (d + 1) * 2 * pad, :] = jnp.where(dest == d, both, 0.0).astype(BF16)
    place = (iota((capacity, tracers), 0) == slot_ref[...]).astype(F32).astype(BF16)
    out = lax.dot_general(
        lhs_s[...], place, (((1,), (1,)), ((), ())), preferred_element_type=F32
    )
    for d in range(npitch):
        both = out[d * 2 * pad : (d + 1) * 2 * pad]
        mine = both[:pad] + both[pad:]
        for j in range(capacity // LANES):
            buf_ref[d, q, j * values : (j + 1) * values, :] = mine[
                :values, j * LANES : (j + 1) * LANES
            ]

    sub = iota((EXTRA, axial), 0)
    up0, up1 = high_ref[:edge].astype(F32), high_ref[edge : 2 * edge].astype(F32)
    dn0, dn1 = low_ref[:edge].astype(F32), low_ref[edge : 2 * edge].astype(F32)
    for n in range(edge):
        tile = jnp.where(sub == 0, up0[n : n + 1], 0.0)
        tile = jnp.where(sub == 1, up1[n : n + 1], tile)
        tile = jnp.where(sub == 6, dn0[n : n + 1], tile)
        halo_ref[n] = jnp.where(sub == 7, dn1[n : n + 1], tile)

    stator = q == 0
    tile = pl.ds(pl.multiple_of((1 - q) * (axial - LANES), LANES), LANES)
    blank = jnp.zeros((SLAB - radial - EXTRA, LANES), F32)
    face_s[...] = jnp.zeros(face_s.shape, F32)

    def near(block):
        turned = block.T
        return (
            jnp.where(stator, turned[LANES - 1 : LANES], turned[0:1]),
            jnp.where(stator, turned[LANES - 2 : LANES - 1], turned[1:2]),
        )

    for i in range(pitch):
        parts = []
        for f in range(planes):
            parts.append(f_ref[f, i, :, tile] if f < nfield else k_ref[i, :, tile])
            parts += [halo_ref[f * pitch + i, :, tile], blank]
        first, second = near(jnp.concatenate(parts, 0))
        face_s[i : i + 1] = first
        face_s[pitch + i : pitch + i + 1] = second
    rest = jnp.zeros((LANES - 2 * SLAB, LANES), F32)
    first, second = near(
        jnp.concatenate([speed_ref[0, :, tile], blank, speed_ref[1, :, tile], blank, rest], 0)
    )
    face_s[2 * pitch : 2 * pitch + 1] = first
    face_s[2 * pitch + 1 : 2 * pitch + 2] = second
    face = face_s[...]
    for d in range(npitch):
        buf_ref[d, 1 - q] = face

    def layers(indices, nearest):
        rows = []
        for f in range(planes):
            for i in indices:
                rows.append(f_ref[f, i] if f < nfield else k_ref[i])
        for f in range(planes):
            corner = halo_ref[f * pitch + nearest]
            rows += [corner[0:1], corner[7:8]]
        rows.append(jnp.zeros((8, axial), F32))
        return jnp.concatenate(rows, 0)

    top = layers((pitch - 2, pitch - 1), pitch - 1)
    bottom = layers((0, 1), 0)
    a_ref[...] = jnp.where(even, top, bottom).astype(BF16)
    b_ref[...] = jnp.where(even, bottom, top).astype(BF16)


def transport(
    npitch,
    nspan,
    map_ref,
    f_ref,
    k_ref,
    speed_ref,
    halo_ref,
    a_ref,
    b_ref,
    buf_ref,
    o_ref,
    arr_ref,
    x_s,
    y_s,
    c_s,
    p_s,
):
    nfield, pitch, radial, axial = f_ref.shape
    planes = nfield + 1
    rows = radial + EXTRA
    lanes = axial + LANES
    s = lax.axis_index("span")
    q = lax.axis_index("row")
    even = lax.rem(lax.axis_index("pitch"), 2) == 0
    stator = q == 0

    values = arr_ref.shape[0]
    capacity = arr_ref.shape[1] // npitch
    for p in range(npitch):
        for j in range(capacity // LANES):
            at = p * capacity + j * LANES
            arr_ref[:, at : at + LANES] = buf_ref[p, q, j * values : (j + 1) * values, :]

    x_s[...] = jnp.zeros(x_s.shape, F32)
    ext_hi = jnp.where(even, a_ref[...].astype(F32), b_ref[...].astype(F32))
    ext_lo = jnp.where(even, b_ref[...].astype(F32), a_ref[...].astype(F32))
    sub = iota((EXTRA, axial), 0)
    corner_at = 2 * planes * radial
    for f in range(planes):
        x_s[f, 2 : 2 + pitch, :radial, :axial] = f_ref[f] if f < nfield else k_ref[...]
        x_s[f, 2 : 2 + pitch, radial:, :axial] = halo_ref[f * pitch : (f + 1) * pitch]
        for n in range(2):
            at = (2 * f + n) * radial
            x_s[f, n, :radial, :axial] = ext_lo[at : at + radial]
            x_s[f, 2 + pitch + n, :radial, :axial] = ext_hi[at : at + radial]
        at = corner_at + 2 * f
        for where, ext in ((1, ext_lo), (2 + pitch, ext_hi)):
            tile = jnp.where(sub == 0, ext[at : at + 1], 0.0)
            x_s[f, where, radial:, :axial] = jnp.where(sub == 7, ext[at + 1 : at + 2], tile)

    row = iota((LANES, LANES), 0)
    near_row = jnp.where(stator, 0, LANES - 1)
    far_row = jnp.where(stator, 1, LANES - 2)
    whole = npitch * pitch
    begin = map_ref[0, 0] - 1

    def turned(near, far):
        return jnp.where(row == near_row, near, jnp.where(row == far_row, far, 0.0)).T

    for n in range(pitch + 2):
        j = begin + n
        j = jnp.where(j < 0, j + whole, j)
        j = jnp.where(j >= whole, j - whole, j)
        p = lax.shift_right_logical(j, power(pitch))
        i = j & (pitch - 1)
        block = turned(
            buf_ref[p, 1 - q, pl.ds(i, 1), :], buf_ref[p, 1 - q, pl.ds(pitch + i, 1), :]
        )
        for f in range(planes):
            x_s[f, 1 + n, :, axial:] = block[f * SLAB : f * SLAB + rows]
    block = turned(
        buf_ref[0, 1 - q, 2 * pitch : 2 * pitch + 1, :],
        buf_ref[0, 1 - q, 2 * pitch + 1 : 2 * pitch + 2, :],
    )
    sa = jnp.concatenate([speed_ref[0], block[:rows]], 1)
    sp = jnp.concatenate([speed_ref[1], block[SLAB : SLAB + rows]], 1)

    lane = iota((rows, lanes), 1)
    radius = iota((rows, lanes), 0)
    sa_next = pltpu.roll(sa, lanes - 1, 1)
    wa = 0.5 * TIME_STEP * (sa + sa_next)
    wa_up, wa_dn = jnp.maximum(wa, 0.0), jnp.minimum(wa, 0.0)
    sp = TIME_STEP * sp
    wp_up, wp_dn = jnp.maximum(sp, 0.0), jnp.minimum(sp, 0.0)
    inlet = stator & (lane == lanes - 1)
    outlet = jnp.logical_not(stator) & (lane == axial - 1)
    end = inlet | outlet
    end_a = jnp.where(outlet, TIME_STEP * sa, 0.0)
    end_b = jnp.where(inlet, TIME_STEP * sa_next, 0.0)
    wall = ((radius == radial - 1) & (s == nspan - 1)) | ((radius == rows - 1) & (s == 0))
    half = 0.5 * TIME_STEP

    def pitch_coefficients(k, k_next):
        kappa = half * (k + k_next)
        return wp_up + kappa, wp_dn - kappa

    def stencil(v, v_next, f, aa, ab, kr, pa, pb):
        axial_flux = aa * v + ab * pltpu.roll(v, lanes - 1, 1)
        radial_flux = kr * (v - pltpu.roll(v, rows - 1, 0))
        pitch_flux = pa * v + pb * v_next
        change = (
            axial_flux
            - pltpu.roll(axial_flux, 1, 1)
            + radial_flux
            - pltpu.roll(radial_flux, 1, 0)
            + pitch_flux
            - p_s[f]
        )
        p_s[f] = pitch_flux
        return v - change

    pa, pb = pitch_coefficients(x_s[nfield, 0], x_s[nfield, 1])
    for f in range(nfield):
        p_s[f] = pa * x_s[f, 0] + pb * x_s[f, 1]

    @pl.loop(1, pitch + 3)
    def _(i):
        k = x_s[nfield, i]
        kappa = half * (k + pltpu.roll(k, lanes - 1, 1))
        aa = jnp.where(end, end_a, wa_up + kappa)
        ab = jnp.where(end, end_b, wa_dn - kappa)
        kr = jnp.where(wall, 0.0, half * (k + pltpu.roll(k, rows - 1, 0)))
        pa, pb = pitch_coefficients(k, x_s[nfield, i + 1])
        for n, value in enumerate((aa, ab, kr, pa, pb)):
            c_s[n, i] = value
        for f in range(nfield):
            y_s[f, i] = stencil(x_s[f, i], x_s[f, i + 1], f, aa, ab, kr, pa, pb)

    for f in range(nfield):
        p_s[f] = c_s[3, 1] * y_s[f, 1] + c_s[4, 1] * y_s[f, 2]

    @pl.loop(2, pitch + 2)
    def _(i):
        coefficients = [c_s[n, i] for n in range(5)]
        for f in range(nfield):
            new = stencil(y_s[f, i], y_s[f, i + 1], f, *coefficients)
            o_ref[f, i - 2] = new[:radial, :axial]


def local(
    fields,
    diffusivity,
    mean_flow,
    radial_kernel,
    tracer_values,
    tracer_cells,
    tracer_dest,
    interface_map,
):
    npitch = lax.axis_size("pitch")
    nspan = lax.axis_size("span")
    nfield, pitch, radial, axial = fields.shape
    planes = nfield + 1
    values, tracers = tracer_values.shape
    chunks = tracers // LANES
    capacity = 2 * tracers // npitch
    edge = planes * pitch
    cells = tracer_cells.reshape(chunks, LANES)
    dest = tracer_dest.reshape(chunks, LANES)

    mean_rows = 2 * radial
    if nspan == 2:
        (packed,) = call(
            pack_span,
            [((2 * edge + mean_rows, axial), BF16)],
            (fields, diffusivity, mean_flow),
            [VMEM] * 3,
            nbytes=2**20,
        )
        span_got = (lax.ppermute(packed, "span", [(0, 1), (1, 0)]),)
    else:
        up, down, mean = call(
            pack_span,
            [((2 * edge, axial), BF16)] * 2 + [((mean_rows, axial), BF16)],
            (fields, diffusivity, mean_flow),
            [VMEM] * 3,
            nbytes=2**20,
        )
        span_got = (
            lax.ppermute(up, "span", [(n, n + 1) for n in range(nspan - 1)]),
            lax.ppermute(down, "span", [(n + 1, n) for n in range(nspan - 1)]),
            lax.all_gather(mean, "span"),
        )

    samp, slot = call(
        lambda *refs: sample_fields(npitch, *refs),
        [((8, tracers), F32), ((1, tracers), jnp.int32)],
        (fields, cells, dest),
        [VMEM] * 3,
        flops=4 * nfield * pitch * radial * axial * tracers,
        nbytes=2**20,
    )

    rows = radial + EXTRA
    per_slot = max(values * capacity // LANES, 2 * pitch + 2)
    per_slot = -(-per_slot // 8) * 8
    halo_rows = 2 * planes * radial + 16
    pad = 16
    buf, a_send, b_send, speeds, halo = call(
        lambda *refs: dispatch(npitch, nspan, *refs),
        [
            ((npitch, 2, per_slot, LANES), F32),
            ((halo_rows, axial), BF16),
            ((halo_rows, axial), BF16),
            ((2, rows, axial), F32),
            ((edge, EXTRA, axial), F32),
        ],
        (
            fields,
            diffusivity,
            mean_flow,
            radial_kernel,
            tracer_values,
            cells,
            dest,
            samp,
            slot,
        )
        + span_got,
        [VMEM] * (9 + len(span_got)),
        [
            pltpu.VMEM(radial_kernel.shape, F32),
            pltpu.VMEM((pad, tracers), F32),
            pltpu.VMEM((npitch * 2 * pad, tracers), BF16),
            pltpu.VMEM((per_slot, LANES), F32),
        ],
        flops=2 * npitch * 2 * pad * tracers * capacity,
        nbytes=2**21,
    )
    buf = lax.all_to_all(
        buf.reshape(npitch * 2, per_slot, LANES), ("pitch", "row"), 0, 0
    ).reshape(buf.shape)
    swap = [(n, n ^ 1) for n in range(npitch)]
    turn = [((n + 1) % npitch, ((n ^ 1) + 1) % npitch) for n in range(npitch)]
    a_got = lax.ppermute(a_send, "pitch", swap)
    b_got = lax.ppermute(b_send, "pitch", turn)

    lanes = axial + LANES
    return call(
        lambda *refs: transport(npitch, nspan, *refs),
        [(fields.shape, F32), ((values, npitch * capacity), F32)],
        (interface_map, fields, diffusivity, speeds, halo, a_got, b_got, buf),
        [SMEM] + [VMEM] * 7,
        [
            pltpu.VMEM((planes, pitch + 4, rows, lanes), F32),
            pltpu.VMEM((nfield, pitch + 4, rows, lanes), F32),
            pltpu.VMEM((5, pitch + 4, rows, lanes), F32),
            pltpu.VMEM((nfield, rows, lanes), F32),
        ],
        flops=2**24,
        nbytes=2**22,
    )


def solution(mesh):
    placed = (
        P(None, "pitch", "span", "row"),
        P("pitch", "span", "row"),
        P("span", None, "row"),
        P(),
        P(None, ("pitch", "span", "row")),
        P(("pitch", "span", "row")),
        P(("pitch", "span", "row"), None),
        P("row", "pitch"),
    )
    return jax.shard_map(
        local,
        mesh=mesh,
        in_specs=placed,
        out_specs=(P(None, "pitch", "span", "row"), P(None, ("pitch", "span", "row"))),
        check_vma=False,
    )
```

```python
import jax
import jax.numpy as jnp
from jax import lax
from jax.experimental import pallas as pl
from jax.experimental.pallas import tpu as pltpu
from jax.sharding import PartitionSpec as P

SUB = 2
TIME_STEP = 0.9
AXIAL_SPEED = 0.15
PITCH_SPEED = 0.15
LANES = 128
EXTRA = 8
SLAB = 32
F32 = jnp.float32
BF16 = jnp.bfloat16
VMEM = pl.BlockSpec(memory_space=pltpu.VMEM)
ANY = pl.BlockSpec(memory_space=pl.ANY)
HBM = pl.BlockSpec(memory_space=pltpu.HBM)
VMEM_LIMIT = 48 * 1024 * 1024


def iota(shape, dim):
    return lax.broadcasted_iota(jnp.int32, shape, dim)


def split(x):
    high = x.astype(BF16)
    return high, (x - high.astype(F32)).astype(BF16)


def power(n):
    assert n & (n - 1) == 0
    return n.bit_length() - 1


def call(body, outs, args, specs, scratch=(), flops=0, nbytes=0, place=VMEM):
    return pl.pallas_call(
        body,
        out_shape=tuple(jax.ShapeDtypeStruct(s, d) for s, d in outs),
        in_specs=list(specs),
        out_specs=tuple(place for _ in outs),
        scratch_shapes=list(scratch),
        compiler_params=pltpu.CompilerParams(vmem_limit_bytes=VMEM_LIMIT),
        cost_estimate=pl.CostEstimate(flops=flops, bytes_accessed=nbytes, transcendentals=0),
    )(*args)


def pack_span(nspan, f_ref, k_ref, m_ref, *refs):
    radial, axial = f_ref.shape[2:]
    *outs, f_s, k_s, m_s, sems = refs
    s = lax.axis_index("span")
    copies = [pltpu.make_async_copy(m_ref, m_s, sems.at[0])]
    sides = 1 if nspan == 2 else 2
    for n in range(sides):
        first = (1 - s if nspan == 2 else 1 - n) * (radial - 8)
        rows = pl.ds(pl.multiple_of(first, 8), 8)
        copies.append(pltpu.make_async_copy(f_ref.at[:, :, rows, :], f_s.at[n], sems.at[1 + 2 * n]))
        copies.append(pltpu.make_async_copy(k_ref.at[:, rows, :], k_s.at[n], sems.at[2 + 2 * n]))
    for copy in copies:
        copy.start()
    for copy in copies:
        copy.wait()

    def edge(n, rows):
        parts = []
        for r in rows:
            parts += [f_s[n, :, :, r, :].reshape(-1, axial), k_s[n, :, r, :]]
        return jnp.concatenate(parts, 0)

    flow = m_s[...].astype(F32)
    flow = jnp.concatenate([flow[:, 0, :], flow[:, 1, :]], 0).astype(BF16)
    if nspan == 2:
        packed = jnp.where(s == 0, edge(0, (6, 7)), edge(0, (0, 1)))
        outs[0][: packed.shape[0]] = packed.astype(BF16)
        outs[0][packed.shape[0] :] = flow
    else:
        outs[0][...] = edge(0, (6, 7)).astype(BF16)
        outs[1][...] = edge(1, (0, 1)).astype(BF16)
        outs[2][...] = flow


def sample_fields(npitch, f_ref, cell_ref, dest_ref, samp_ref, slot_ref):
    nfield, pitch, radial, axial = f_ref.shape
    lines = pitch * radial
    chunks = cell_ref.shape[0]
    table = f_ref[...].reshape(nfield * lines, axial)
    high, low = split(table)
    samp_ref[...] = jnp.zeros(samp_ref.shape, F32)
    for c in range(0, chunks, 2):
        cells = jnp.concatenate([cell_ref[c : c + 1, :], cell_ref[c + 1 : c + 2, :]], 1)
        width = cells.shape[1]
        lane = cells & (axial - 1)
        line = lax.shift_right_logical(cells, power(axial))
        pick = (iota((axial, width), 0) == lane).astype(F32).astype(BF16)
        got = jnp.dot(high, pick, preferred_element_type=F32) + jnp.dot(
            low, pick, preferred_element_type=F32
        )
        mine = iota((lines, width), 0) == line
        for f in range(nfield):
            part = jnp.where(mine, got[f * lines : (f + 1) * lines], 0.0)
            samp_ref[f : f + 1, c * LANES : c * LANES + width] = jnp.sum(part, 0, keepdims=True)
    ones = []
    for c in range(chunks):
        ones.append((iota((npitch, LANES), 0) == dest_ref[c : c + 1, :]).astype(F32))
    stacked = jnp.concatenate(ones, 0)
    before = (iota((LANES, LANES), 0) < iota((LANES, LANES), 1)).astype(F32).astype(BF16)
    prefix = jnp.dot(stacked.astype(BF16), before, preferred_element_type=F32)
    carry = jnp.zeros((npitch, 1), F32)
    for c in range(chunks):
        rank = prefix[c * npitch : (c + 1) * npitch] + carry
        slot = jnp.sum(rank * ones[c], 0, keepdims=True)
        slot_ref[:, c * LANES : (c + 1) * LANES] = slot.astype(jnp.int32)
        carry = carry + jnp.sum(ones[c], 1, keepdims=True)


def slab(core, extra):
    return [extra, core, extra]


def near(stator, parts):
    turned = jnp.concatenate(parts, 0).T
    return (
        jnp.where(stator, turned[LANES - 1 : LANES], turned[0:1]),
        jnp.where(stator, turned[LANES - 2 : LANES - 1], turned[1:2]),
    )


def dispatch(
    npitch,
    nspan,
    f_ref,
    k_ref,
    m_ref,
    kern_ref,
    tv_ref,
    cell_ref,
    dest_ref,
    samp_ref,
    slot_ref,
    map_ref,
    *refs,
):
    nfield, pitch, radial, axial = f_ref.shape
    planes = nfield + 1
    edge = planes * pitch
    if nspan == 2:
        (got_ref,) = refs[:1]
        refs = refs[1:]
        low_ref = high_ref = got_ref
    else:
        low_ref, high_ref, all_ref = refs[:3]
        refs = refs[3:]
    buf_ref, a_ref, b_ref, speed_ref, halo_ref, face_ref, kern_s, upd_s, lhs_s, face_s = refs
    s = lax.axis_index("span")
    q = lax.axis_index("row")
    even = lax.rem(lax.axis_index("pitch"), 2) == 0

    total = kern_ref.shape[0]
    kern_s[...] = kern_ref[...].astype(F32)
    main = kern_s[pl.ds(pl.multiple_of(s * radial, 8), radial), :]
    above = kern_s[pl.ds(pl.multiple_of(jnp.minimum((s + 1) * radial, total - 8), 8), 8), :]
    below = kern_s[pl.ds(pl.multiple_of(jnp.maximum(s * radial - 8, 0), 8), 8), :]
    wide = jnp.concatenate([main, jnp.where(iota((EXTRA, total), 0) < 4, above, below)], 0).astype(BF16)
    smoothed = []
    flow = m_ref[...].astype(F32)
    for c in range(2):
        if nspan == 2:
            own = flow[:, c, :]
            other = got_ref[2 * edge + c * radial : 2 * edge + (c + 1) * radial, :].astype(F32)
            rows = [jnp.where(s == 0, own, other), jnp.where(s == 0, other, own)]
        else:
            rows = [all_ref[n, c * radial : (c + 1) * radial, :].astype(F32) for n in range(nspan)]
        smoothed.append(
            jnp.dot(wide, jnp.concatenate(rows, 0).astype(BF16), preferred_element_type=F32)
        )
    sa = AXIAL_SPEED * (1.0 + 0.5 * jnp.tanh(smoothed[0]))
    sp = PITCH_SPEED * jnp.tanh(smoothed[1])
    speed_ref[0] = sa
    speed_ref[1] = sp

    chunks = cell_ref.shape[0]
    high, low = split(jnp.concatenate([sa[:radial], sp[:radial]], 0))
    upd_s[...] = jnp.zeros(upd_s.shape, F32)
    for c in range(0, chunks, 2):
        cells = jnp.concatenate([cell_ref[c : c + 1, :], cell_ref[c + 1 : c + 2, :]], 1)
        width = cells.shape[1]
        span = slice(c * LANES, c * LANES + width)
        lane = cells & (axial - 1)
        line = lax.shift_right_logical(cells, power(axial)) & (radial - 1)
        pick = (iota((axial, width), 0) == lane).astype(F32).astype(BF16)
        got = jnp.dot(high, pick, preferred_element_type=F32) + jnp.dot(
            low, pick, preferred_element_type=F32
        )
        mine = iota((radial, width), 0) == line
        sampled = [samp_ref[f : f + 1, span] for f in range(nfield)]
        for n in range(2):
            part = jnp.where(mine, got[n * radial : (n + 1) * radial], 0.0)
            sampled.append(jnp.sum(part, 0, keepdims=True))
        count = len(sampled)
        for v, value in enumerate(sampled):
            head = tv_ref[v : v + 1, span]
            upd_s[v : v + 1, span] = head + 0.5 * (value - head)
            upd_s[count + v : count + v + 1, span] = tv_ref[count + v : count + v + 1, span] + 0.8 * value

    values = tv_ref.shape[0]
    tracers = tv_ref.shape[1]
    capacity = 2 * tracers // npitch
    pad = upd_s.shape[0]
    both = upd_s[...]
    rounded = both.astype(BF16).astype(F32)
    both = jnp.concatenate([rounded, both - rounded], 0)
    dest = jnp.concatenate([dest_ref[c : c + 1, :] for c in range(chunks)], 1)
    for d in range(npitch):
        lhs_s[d * 2 * pad : (d + 1) * 2 * pad, :] = jnp.where(dest == d, both, 0.0).astype(BF16)
    place = (iota((capacity, tracers), 0) == slot_ref[...]).astype(F32).astype(BF16)
    out = lax.dot_general(
        lhs_s[...], place, (((1,), (1,)), ((), ())), preferred_element_type=F32
    )
    for d in range(npitch):
        both = out[d * 2 * pad : (d + 1) * 2 * pad]
        mine = both[:pad] + both[pad:]
        for j in range(capacity // LANES):
            buf_ref[d, q, j * values : (j + 1) * values, :] = mine[
                :values, j * LANES : (j + 1) * LANES
            ]

    sub = iota((EXTRA, axial), 0)
    up0, up1 = high_ref[:edge].astype(F32), high_ref[edge : 2 * edge].astype(F32)
    dn0, dn1 = low_ref[:edge].astype(F32), low_ref[edge : 2 * edge].astype(F32)
    for n in range(edge):
        tile = jnp.where(sub == 0, up0[n : n + 1], 0.0)
        tile = jnp.where(sub == 1, up1[n : n + 1], tile)
        tile = jnp.where(sub == 6, dn0[n : n + 1], tile)
        halo_ref[n] = jnp.where(sub == 7, dn1[n : n + 1], tile)

    stator = q == 0
    tile = pl.ds(pl.multiple_of((1 - q) * (axial - LANES), LANES), LANES)
    face_s[...] = jnp.zeros(face_s.shape, F32)

    for i in range(pitch):
        parts = []
        for f in range(planes):
            core = f_ref[f, i, :, tile] if f < nfield else k_ref[i, :, tile]
            parts += slab(core, halo_ref[f * pitch + i, :, tile])
        first, second = near(stator, parts)
        face_s[i : i + 1] = first
        face_s[pitch + i : pitch + i + 1] = second
    for n in range(2):
        speed = speed_ref[n, :, tile]
        first, second = near(stator, slab(speed[:radial], speed[radial:]) * planes)
        at = 2 * pitch + 2 * n
        face_s[at : at + 1] = first
        face_s[at + 1 : at + 2] = second
    face = face_s[...]
    face_ref[...] = face
    first = map_ref[...].astype(F32)
    face_ref[2 * pitch + 3 : 2 * pitch + 4] = jnp.broadcast_to(first[:, :1], (1, LANES))
    for d in range(npitch):
        buf_ref[d, 1 - q] = face

    def layers(indices, nearest):
        rows = []
        for f in range(planes):
            for i in indices:
                rows.append(f_ref[f, i] if f < nfield else k_ref[i])
        for f in range(planes):
            corner = halo_ref[f * pitch + nearest]
            rows += [corner[0:1], corner[7:8]]
        rows.append(jnp.zeros((8, axial), F32))
        return jnp.concatenate(rows, 0)

    top = layers((pitch - 2, pitch - 1), pitch - 1)
    bottom = layers((0, 1), 0)
    a_ref[...] = jnp.where(even, top, bottom).astype(BF16)
    b_ref[...] = jnp.where(even, bottom, top).astype(BF16)


class Faces:
    def __init__(self, nspan, speed_ref, radial):
        self.rows, self.lanes = speed_ref.shape[1:]
        shape = (self.rows, self.lanes)
        s = lax.axis_index("span")
        stator = lax.axis_index("row") == 0
        lane, radius = iota(shape, 1), iota(shape, 0)
        sa = TIME_STEP * speed_ref[0]
        sp = TIME_STEP * speed_ref[1]
        wa = 0.5 * (sa + pltpu.roll(sa, self.lanes - 1, 1))
        self.last = lane == self.lanes - 1
        self.wa_up, self.wa_dn = jnp.maximum(wa, 0.0), jnp.minimum(wa, 0.0)
        self.wp_up, self.wp_dn = jnp.maximum(sp, 0.0), jnp.minimum(sp, 0.0)
        self.wall = ((radius == radial - 1) & (s == nspan - 1)) | (
            (radius == self.rows - 1) & (s == 0)
        )
        inlet = jnp.where(stator & (lane == 0), sa, 0.0)
        self.keep = 1.0 + inlet - jnp.where(jnp.logical_not(stator) & self.last, sa, 0.0)
        self.half = 0.5 * TIME_STEP

    def plane(self, k):
        kappa = self.half * (k + pltpu.roll(k, self.lanes - 1, 1))
        aa = jnp.where(self.last, 0.0, self.wa_up + kappa)
        ab = jnp.where(self.last, 0.0, self.wa_dn - kappa)
        kr = jnp.where(self.wall, 0.0, self.half * (k + pltpu.roll(k, self.rows - 1, 0)))
        return aa, ab, kr

    def pitch(self, k, k_next):
        kappa = self.half * (k + k_next)
        return self.wp_up + kappa, self.wp_dn - kappa

    def step(self, v, coefficients, flux_up, flux_dn):
        aa, ab, kr = coefficients
        along = aa * v + ab * pltpu.roll(v, self.lanes - 1, 1)
        radial = kr * (v - pltpu.roll(v, self.rows - 1, 0))
        change = along - pltpu.roll(along, 1, 1) + radial - pltpu.roll(radial, 1, 0)
        return self.keep * v - (change + (flux_up - flux_dn))


def middle(nspan, f_ref, k_ref, speed_ref, halo_ref, o_ref, y4_ref, row_ref, y_s, c_s, p_s):
    nfield, pitch, radial, axial = f_ref.shape
    stator = lax.axis_index("row") == 0
    faces = Faces(nspan, speed_ref, radial)

    def state(f, i):
        return jnp.concatenate([f_ref[f, i], halo_ref[f * pitch + i]], 0)

    def kappa(i):
        return jnp.concatenate([k_ref[i], halo_ref[nfield * pitch + i]], 0)

    pa, pb = faces.pitch(kappa(0), kappa(1))
    for f in range(nfield):
        p_s[f] = pa * state(f, 0) + pb * state(f, 1)

    @pl.loop(1, pitch - 1)
    def _(i):
        k = kappa(i)
        plane = faces.plane(k)
        pa, pb = faces.pitch(k, kappa(i + 1))
        for n, value in enumerate((*plane, pa, pb)):
            c_s[n, i] = value
        for f in range(nfield):
            v = state(f, i)
            flux = pa * v + pb * state(f, i + 1)
            y_s[f, i] = faces.step(v, plane, flux, p_s[f])
            p_s[f] = flux

    for f in range(nfield):
        p_s[f] = c_s[3, 1] * y_s[f, 1] + c_s[4, 1] * y_s[f, 2]

    @pl.loop(2, pitch - 2)
    def _(i):
        aa, ab, kr, pa, pb = [c_s[n, i] for n in range(5)]
        for f in range(nfield):
            v = y_s[f, i]
            flux = pa * v + pb * y_s[f, i + 1]
            o_ref[f, i - 2] = faces.step(v, (aa, ab, kr), flux, p_s[f])[:radial]
            p_s[f] = flux

    for f in range(nfield):
        for n, i in enumerate((1, 2, pitch - 3, pitch - 2)):
            y4_ref[f, n] = y_s[f, i]
    row_ref[...] = jnp.zeros(row_ref.shape, F32)
    tile = pl.ds(pl.multiple_of(lax.axis_index("row") * (LANES - axial) + axial - LANES, LANES), LANES)
    blank = jnp.zeros((SLAB, LANES), F32)
    for i in range(1, pitch - 1):
        parts = []
        for f in range(nfield):
            parts += slab(y_s[f, i, :radial, tile], y_s[f, i, radial:, tile])
        row_ref[i : i + 1] = near(stator, parts + [blank])[0]


def edges(
    nspan, f_ref, k_ref, speed_ref, halo_ref, a_ref, b_ref, y4_ref, row_ref, o_ref, row_out, beyond_ref, y_s
):
    nfield, pitch, radial, axial = f_ref.shape
    planes = nfield + 1
    stator = lax.axis_index("row") == 0
    even = lax.rem(lax.axis_index("pitch"), 2) == 0
    faces = Faces(nspan, speed_ref, radial)
    ext = {
        -1: jnp.where(even, b_ref[...].astype(F32), a_ref[...].astype(F32)),
        1: jnp.where(even, a_ref[...].astype(F32), b_ref[...].astype(F32)),
    }
    sub = iota((EXTRA, axial), 0)
    corner_at = 2 * planes * radial

    def state(f, i):
        if 0 <= i < pitch:
            core = f_ref[f, i] if f < nfield else k_ref[i]
            return jnp.concatenate([core, halo_ref[f * pitch + i]], 0)
        side = ext[-1 if i < 0 else 1]
        at = (2 * f + (i + 2 if i < 0 else i - pitch)) * radial
        extra = jnp.zeros((EXTRA, axial), F32)
        if i in (-1, pitch):
            corner = corner_at + 2 * f
            extra = jnp.where(sub == 0, side[corner : corner + 1], 0.0)
            extra = jnp.where(sub == 7, side[corner + 1 : corner + 2], extra)
        return jnp.concatenate([side[at : at + radial], extra], 0)

    row_out[...] = row_ref[...]
    beyond_ref[...] = jnp.zeros(beyond_ref.shape, F32)
    tile = pl.ds(pl.multiple_of(lax.axis_index("row") * (LANES - axial) + axial - LANES, LANES), LANES)

    def edge_lanes(value):
        return jnp.where(stator, value[:, axial - LANES :], value[:, :LANES])

    blank = jnp.zeros((SLAB, LANES), F32)
    for side, new, done in ((0, (-1, 0), (0, 1)), (1, (pitch - 1, pitch), (pitch - 2, pitch - 1))):
        k = {i: state(nfield, i) for i in range(new[0] - 1, new[1] + 2)}
        low = min(new[0] - 1, done[0] - 1)
        top = max(new[1] + 1, done[1] + 1)
        k = {i: state(nfield, i) for i in range(low, top + 1)}
        along = {i: faces.pitch(k[i], k[i + 1]) for i in range(low, top)}
        plane = {i: faces.plane(k[i]) for i in sorted({*new, *done})}
        held = {}
        for n, i in enumerate((1, 2, pitch - 3, pitch - 2)):
            held[i] = n
        for f in range(nfield):
            x = {i: state(f, i) for i in range(new[0] - 1, new[1] + 2)}
            flux = {i: along[i][0] * x[i] + along[i][1] * x[i + 1] for i in range(new[0] - 1, new[1] + 1)}
            y = {i: y4_ref[f, held[i]] for i in held if done[0] - 1 <= i <= done[1] + 1}
            for i in new:
                y[i] = faces.step(x[i], plane[i], flux[i], flux[i - 1])
            flux = {i: along[i][0] * y[i] + along[i][1] * y[i + 1] for i in range(done[0] - 1, done[1] + 1)}
            for n, i in enumerate(done):
                o_ref[f, 2 * side + n] = faces.step(y[i], plane[i], flux[i], flux[i - 1])[:radial]
            y_s[f] = y[0 if side == 0 else pitch - 1]
        parts = []
        for f in range(nfield):
            parts += slab(y_s[f, :radial, tile], y_s[f, radial:, tile])
        i = 0 if side == 0 else pitch - 1
        row_out[i : i + 1] = near(stator, parts + [blank])[0]
        parts = []
        for f in range(planes):
            value = edge_lanes(state(f, -1 if side == 0 else pitch))
            parts += slab(value[:radial], value[radial:])
        beyond_ref[side : side + 1] = near(stator, parts)[0]


def interface(
    npitch,
    nspan,
    mid_ref,
    edge_ref,
    face_ref,
    row_ref,
    beyond_ref,
    buf_ref,
    o_ref,
    arr_ref,
    arr_s,
    tile_s,
    ring_s,
    sems,
):
    nfield, pitch, radial, axial = o_ref.shape
    planes = nfield + 1
    s = lax.axis_index("span")
    q = lax.axis_index("row")
    stator = q == 0
    near_tile = pl.ds(pl.multiple_of((1 - q) * (axial - LANES), LANES), LANES)
    copies = []
    if axial > LANES:
        rest = pl.ds(pl.multiple_of(q * LANES, LANES), axial - LANES)
        copies += [
            pltpu.make_async_copy(
                mid_ref.at[:, :, :, rest], o_ref.at[:, 2 : pitch - 2, :, rest], sems.at[0]
            ),
            pltpu.make_async_copy(
                edge_ref.at[:, :2, :, rest], o_ref.at[:, :2, :, rest], sems.at[1]
            ),
            pltpu.make_async_copy(
                edge_ref.at[:, 2:, :, rest], o_ref.at[:, pitch - 2 :, :, rest], sems.at[2]
            ),
        ]
    for copy in copies:
        copy.start()

    values = arr_ref.shape[0]
    capacity = arr_ref.shape[1] // npitch
    for p in range(npitch):
        for j in range(capacity // LANES):
            at = p * capacity + j * LANES
            arr_s[:, at : at + LANES] = buf_ref[p, q, j * values : (j + 1) * values, :]
    copies.append(pltpu.make_async_copy(arr_s, arr_ref, sems.at[3]))
    copies[-1].start()

    whole = npitch * pitch
    count = pitch + 8
    for p in range(npitch):
        ring_s[0, p * pitch : (p + 1) * pitch] = buf_ref[p, 1 - q, :pitch, :]
        ring_s[1, p * pitch : (p + 1) * pitch] = buf_ref[p, 1 - q, pitch : 2 * pitch, :]
    for n in range(2):
        ring_s[n, whole : whole + pitch] = ring_s[n, :pitch]
        ring_s[n, whole + pitch :] = ring_s[n, pitch : pitch + 8]
    begin = jnp.max(face_ref[2 * pitch + 3 : 2 * pitch + 4]).astype(jnp.int32) - 1
    begin = jnp.where(begin < 0, begin + whole, begin)
    ghost = ring_s[0, pl.ds(begin, count), :]
    farther = ring_s[1, pl.ds(begin, count), :]
    tail = jnp.zeros((count - pitch - 2, LANES), F32)
    own = jnp.concatenate(
        [beyond_ref[0:1], face_ref[:pitch], beyond_ref[1:2], tail], 0
    )
    top = jnp.zeros((1, LANES), F32)
    own_k1 = jnp.concatenate([top, face_ref[pitch : 2 * pitch], top, tail], 0)
    own_new = jnp.concatenate([top, row_ref[...], top, tail], 0)
    at = 2 * pitch
    sa0, sa1, sp0 = [TIME_STEP * face_ref[at + n : at + n + 1] for n in range(3)]
    ga0, ga1, gp0 = [TIME_STEP * buf_ref[0, 1 - q, at + n : at + n + 1, :] for n in range(3)]
    shape = (count, LANES)
    lane = iota(shape, 1)
    group = lax.shift_right_logical(lane, power(SLAB))
    radius = lane & (SLAB - 1)

    def spread(x):
        out = x
        for f in range(nfield):
            out = jnp.where(group == f, pltpu.roll(x, (f + 1) * SLAB, 1), out)
        return out

    half = 0.5 * TIME_STEP
    k0, k1, g0, g1 = spread(own), spread(own_k1), spread(ghost), spread(farther)
    wall = ((radius == 7 + radial) & (s == nspan - 1)) | ((radius == 7) & (s == 0))

    def ahead(x):
        return pltpu.roll(x, count - 1, 0)

    def outward(x):
        return pltpu.roll(x, LANES - 1, 1)

    def change(v, k, speed):
        kappa = half * (k + ahead(k))
        up, dn = jnp.maximum(speed, 0.0), jnp.minimum(speed, 0.0)
        along = (up + kappa) * v + (dn - kappa) * ahead(v)
        kappa = jnp.where(wall, 0.0, half * (k + outward(k)))
        across = kappa * (v - outward(v))
        return along - pltpu.roll(along, 1, 0) + across - pltpu.roll(across, 1, 1)

    def face(first, second, speed, kappa):
        lower = jnp.where(stator, first, second)
        upper = jnp.where(stator, second, first)
        return (jnp.maximum(speed, 0.0) + kappa) * lower + (jnp.minimum(speed, 0.0) - kappa) * upper

    sign = jnp.where(stator, 1.0, -1.0)
    speed = 0.5 * (sa0 + ga0)
    kappa = half * (k0 + g0)
    flux = sign * face(own, ghost, speed, kappa)
    shift = -flux
    ghost_new = (
        ghost
        + flux
        - sign * face(ghost, farther, 0.5 * (ga0 + ga1), half * (g0 + g1))
        - change(ghost, g0, gp0)
    )
    flux = sign * face(own_new + shift, ghost_new, speed, kappa)
    inner = 0.5 * (sa0 + sa1)
    kappa = half * (k0 + k1)
    inner = sign * jnp.where(
        stator, jnp.minimum(inner, 0.0) - kappa, jnp.maximum(inner, 0.0) + kappa
    ) * shift
    add0 = shift - change(shift, k0, sp0) + inner - flux
    add1 = -inner

    row = iota((LANES, LANES), 0)
    near_row = jnp.where(stator, LANES - 1, 0)
    far_row = jnp.where(stator, LANES - 2, 1)
    for i in range(pitch):
        block = jnp.where(
            row == near_row,
            add0[i + 1 : i + 2],
            jnp.where(row == far_row, add1[i + 1 : i + 2], 0.0),
        ).T
        for f in range(nfield):
            if 2 <= i < pitch - 2:
                old = mid_ref[f, i - 2, :, near_tile]
            else:
                old = edge_ref[f, i if i < 2 else i - pitch + 4, :, near_tile]
            tile_s[f, i] = old + block[f * SLAB + 8 : f * SLAB + 8 + radial]
    copies.append(pltpu.make_async_copy(tile_s, o_ref.at[:, :, :, near_tile], sems.at[4]))
    copies[-1].start()
    for copy in copies:
        copy.wait()


def local(
    fields,
    diffusivity,
    mean_flow,
    radial_kernel,
    tracer_values,
    tracer_cells,
    tracer_dest,
    interface_map,
):
    npitch = lax.axis_size("pitch")
    nspan = lax.axis_size("span")
    nfield, pitch, radial, axial = fields.shape
    planes = nfield + 1
    values, tracers = tracer_values.shape
    chunks = tracers // LANES
    capacity = 2 * tracers // npitch
    edge = planes * pitch
    cells = tracer_cells.reshape(chunks, LANES)
    dest = tracer_dest.reshape(chunks, LANES)

    mean_rows = 2 * radial
    sides = 1 if nspan == 2 else 2
    if nspan == 2:
        outs = [((2 * edge + mean_rows, axial), BF16)]
    else:
        outs = [((2 * edge, axial), BF16)] * 2 + [((mean_rows, axial), BF16)]
    packed = call(
        lambda *refs: pack_span(nspan, *refs),
        outs,
        [pltpu.with_memory_space_constraint(x, pltpu.HBM) for x in (fields, diffusivity, mean_flow)],
        [HBM] * 3,
        [
            pltpu.VMEM((sides, nfield, pitch, 8, axial), F32),
            pltpu.VMEM((sides, pitch, 8, axial), F32),
            pltpu.VMEM(mean_flow.shape, mean_flow.dtype),
            pltpu.SemaphoreType.DMA((1 + 2 * sides,)),
        ],
        nbytes=2**20,
    )
    if nspan == 2:
        span_got = (lax.ppermute(packed[0], "span", [(0, 1), (1, 0)]),)
    else:
        span_got = (
            lax.ppermute(packed[0], "span", [(n, n + 1) for n in range(nspan - 1)]),
            lax.ppermute(packed[1], "span", [(n + 1, n) for n in range(nspan - 1)]),
            lax.all_gather(packed[2], "span"),
        )

    samp, slot = call(
        lambda *refs: sample_fields(npitch, *refs),
        [((8, tracers), F32), ((1, tracers), jnp.int32)],
        (fields, cells, dest),
        [VMEM] * 3,
        flops=4 * nfield * pitch * radial * axial * tracers,
        nbytes=2**20,
    )

    rows = radial + EXTRA
    per_slot = max(values * capacity // LANES, 2 * pitch + 4)
    per_slot = -(-per_slot // 8) * 8
    halo_rows = 2 * planes * radial + 16
    pad = 16
    buf, a_send, b_send, speeds, halo, face = call(
        lambda *refs: dispatch(npitch, nspan, *refs),
        [
            ((npitch, 2, per_slot, LANES), F32),
            ((halo_rows, axial), BF16),
            ((halo_rows, axial), BF16),
            ((2, rows, axial), F32),
            ((edge, EXTRA, axial), F32),
            ((per_slot, LANES), F32),
        ],
        (
            fields,
            diffusivity,
            mean_flow,
            radial_kernel,
            tracer_values,
            cells,
            dest,
            samp,
            slot,
            interface_map,
        )
        + span_got,
        [VMEM] * (10 + len(span_got)),
        [
            pltpu.VMEM(radial_kernel.shape, F32),
            pltpu.VMEM((pad, tracers), F32),
            pltpu.VMEM((npitch * 2 * pad, tracers), BF16),
            pltpu.VMEM((per_slot, LANES), F32),
        ],
        flops=2 * npitch * 2 * pad * tracers * capacity,
        nbytes=2**21,
    )
    buf = lax.all_to_all(
        buf.reshape(npitch * 2, per_slot, LANES), ("pitch", "row"), 0, 0
    ).reshape(buf.shape)
    swap = [(n, n ^ 1) for n in range(npitch)]
    turn = [((n + 1) % npitch, ((n ^ 1) + 1) % npitch) for n in range(npitch)]
    a_got = lax.ppermute(a_send, "pitch", swap)
    b_got = lax.ppermute(b_send, "pitch", turn)

    mid, near_edge, new_rows = call(
        lambda *refs: middle(nspan, *refs),
        [
            ((nfield, pitch - 4, radial, axial), F32),
            ((nfield, 4, rows, axial), F32),
            ((pitch, LANES), F32),
        ],
        (fields, diffusivity, speeds, halo),
        [VMEM] * 4,
        [
            pltpu.VMEM((nfield, pitch, rows, axial), F32),
            pltpu.VMEM((5, pitch, rows, axial), F32),
            pltpu.VMEM((nfield, rows, axial), F32),
        ],
        flops=2**24,
        nbytes=2**22,
    )
    outer, new_rows, beyond = call(
        lambda *refs: edges(nspan, *refs),
        [
            ((nfield, 4, radial, axial), F32),
            ((pitch, LANES), F32),
            ((8, LANES), F32),
        ],
        (fields, diffusivity, speeds, halo, a_got, b_got, near_edge, new_rows),
        [VMEM] * 8,
        [pltpu.VMEM((nfield, rows, axial), F32)],
        flops=2**23,
        nbytes=2**21,
    )
    return call(
        lambda *refs: interface(npitch, nspan, *refs),
        [(fields.shape, F32), ((values, npitch * capacity), F32)],
        (mid, outer, face, new_rows, beyond, buf),
        [VMEM] * 6,
        [
            pltpu.VMEM((values, npitch * capacity), F32),
            pltpu.VMEM((nfield, pitch, radial, LANES), F32),
            pltpu.VMEM((2, npitch * pitch + pitch + 8, LANES), F32),
            pltpu.SemaphoreType.DMA((5,)),
        ],
        flops=2**22,
        nbytes=2**21,
        place=ANY,
    )


def solution(mesh):
    placed = (
        P(None, "pitch", "span", "row"),
        P("pitch", "span", "row"),
        P("span", None, "row"),
        P(),
        P(None, ("pitch", "span", "row")),
        P(("pitch", "span", "row")),
        P(("pitch", "span", "row"), None),
        P("row", "pitch"),
    )
    return jax.shard_map(
        local,
        mesh=mesh,
        in_specs=placed,
        out_specs=(P(None, "pitch", "span", "row"), P(None, ("pitch", "span", "row"))),
        check_vma=False,
    )
```

```python
import jax
import jax.numpy as jnp
from jax import lax
from jax.experimental import pallas as pl
from jax.experimental.pallas import tpu as pltpu
from jax.sharding import PartitionSpec as P

SUB = 2
TIME_STEP = 0.9
AXIAL_SPEED = 0.15
PITCH_SPEED = 0.15
LANES = 128
EXTRA = 8
SLAB = 32
F32 = jnp.float32
BF16 = jnp.bfloat16
VMEM = pl.BlockSpec(memory_space=pltpu.VMEM)
ANY = pl.BlockSpec(memory_space=pl.ANY)
HBM = pl.BlockSpec(memory_space=pltpu.HBM)
CODE = 10.0
FINE = 18.0
VMEM_LIMIT = 48 * 1024 * 1024


def iota(shape, dim):
    return lax.broadcasted_iota(jnp.int32, shape, dim)


def split(x):
    high = x.astype(BF16)
    return high, (x - high.astype(F32)).astype(BF16)


def power(n):
    assert n & (n - 1) == 0
    return n.bit_length() - 1


def call(body, outs, args, specs, scratch=(), flops=0, nbytes=0, place=VMEM, fixed=False):
    shape = pltpu.VMEM if fixed else jax.ShapeDtypeStruct
    return pl.pallas_call(
        body,
        out_shape=tuple(shape(s, d) for s, d in outs),
        in_specs=list(specs),
        out_specs=tuple(place for _ in outs),
        scratch_shapes=list(scratch),
        compiler_params=pltpu.CompilerParams(vmem_limit_bytes=VMEM_LIMIT),
        cost_estimate=pl.CostEstimate(flops=flops, bytes_accessed=nbytes, transcendentals=0),
    )(*args)


def pack_span(nspan, n_in, *refs):
    ins, rest = refs[:n_in], refs[n_in:]
    outs, kept, (m_s, sems) = rest[: -n_in - 1], rest[-n_in - 1 : -2], rest[-2:]
    f_ref, k_ref = kept[:2]
    radial, axial = f_ref.shape[2:]
    s = lax.axis_index("span")
    half = radial - 8
    early = [pltpu.make_async_copy(ins[-1], m_s, sems.at[0])]
    late = []
    for n, first, size in ((0, (1 - s) * half, 8), (1, s * 8, half)):
        rows = pl.ds(pl.multiple_of(first, 8), size)
        copies = [
            pltpu.make_async_copy(
                ins[0].at[:, :, rows, :], f_ref.at[:, :, rows, :], sems.at[1 + 2 * n]
            ),
            pltpu.make_async_copy(ins[1].at[:, rows, :], k_ref.at[:, rows, :], sems.at[2 + 2 * n]),
        ]
        if n == 0 or nspan > 2:
            early += copies
        else:
            late += copies
    for n in range(2, n_in - 1):
        late.append(pltpu.make_async_copy(ins[n], kept[n], sems.at[n + 3]))
    for copy in early + late:
        copy.start()
    for copy in early:
        copy.wait()

    def edge(first):
        parts = []
        for r in range(2):
            row = pl.ds(first + r, 1)
            parts += [f_ref[:, :, row, :].reshape(-1, axial), k_ref[:, row, :].reshape(-1, axial)]
        return jnp.concatenate(parts, 0).astype(BF16)

    flow = m_s[...].astype(F32)
    flow = jnp.concatenate([flow[:, 0, :], flow[:, 1, :]], 0).astype(BF16)
    if nspan == 2:
        packed = edge((1 - s) * (radial - 2))
        outs[0][: packed.shape[0]] = packed
        outs[0][packed.shape[0] :] = flow
    else:
        outs[0][...] = edge(radial - 2)
        outs[1][...] = edge(0)
        outs[2][...] = flow
    for copy in late:
        copy.wait()


def tracer_chunk(ref, c):
    both = [ref[pl.ds(2 * c + n, 1), :] for n in range(2)]
    return jnp.concatenate(both, 1), pl.ds(pl.multiple_of(c * 2 * LANES, 2 * LANES), 2 * LANES)


def one_hot(rows, index):
    return (iota((rows, index.shape[1]), 0) == index).astype(F32).astype(BF16)


def sample_fields(npitch, f_ref, cell_ref, dest_ref, samp_ref, place_ref, key_ref, pick_ref, table_s):
    nfield, pitch, radial, axial = f_ref.shape
    lines = pitch * radial
    chunks = cell_ref.shape[0]

    @pl.loop(0, nfield, unroll=True)
    def _(f):
        table_s[f] = jnp.exp2(FINE * f_ref[f].reshape(lines, axial)).astype(BF16)

    table = table_s[...].reshape(nfield * lines, axial)
    samp_ref[...] = jnp.zeros(samp_ref.shape, F32)

    @pl.loop(0, chunks // 2, unroll=True)
    def _(c):
        cells, span = tracer_chunk(cell_ref, c)
        pick = one_hot(axial, cells & (axial - 1))
        pick_ref[:, span] = pick
        got = jnp.dot(table, pick, preferred_element_type=F32)
        mine = iota((lines, cells.shape[1]), 0) == lax.shift_right_logical(cells, power(axial))
        for f in range(nfield):
            part = jnp.where(mine, got[f * lines : (f + 1) * lines], 0.0)
            part = jnp.sum(part, 0, keepdims=True)
            samp_ref[f : f + 1, span] = jnp.log2(part) * (1.0 / FINE)

    ones = []
    for c in range(chunks):
        ones.append((iota((npitch, LANES), 0) == dest_ref[c : c + 1, :]).astype(F32))
    stacked = jnp.concatenate(ones, 0)
    before = (iota((LANES, LANES), 0) < iota((LANES, LANES), 1)).astype(F32).astype(BF16)
    prefix = jnp.dot(stacked.astype(BF16), before, preferred_element_type=F32)
    carry = jnp.zeros((npitch, 1), F32)
    for c in range(chunks):
        rank = prefix[c * npitch : (c + 1) * npitch] + carry
        slot = jnp.sum(rank * ones[c], 0, keepdims=True).astype(jnp.int32)
        span = slice(c * LANES, (c + 1) * LANES)
        width = place_ref.shape[0]
        place_ref[:, span] = one_hot(width, slot & (width - 1))
        groups = 2 * chunks * LANES // npitch // width
        key_ref[:, span] = dest_ref[c : c + 1, :] * groups + lax.shift_right_logical(slot, power(width))
        carry = carry + jnp.sum(ones[c], 1, keepdims=True)


def slab(core, extra):
    return [extra, core, extra]


def near(stator, parts):
    turned = jnp.concatenate(parts, 0).T
    return (
        jnp.where(stator, turned[LANES - 1 : LANES], turned[0:1]),
        jnp.where(stator, turned[LANES - 2 : LANES - 1], turned[1:2]),
    )


def dispatch(
    npitch,
    nspan,
    f_ref,
    k_ref,
    kern_ref,
    tv_ref,
    cell_ref,
    map_ref,
    samp_ref,
    place_ref,
    key_ref,
    pick_ref,
    *refs,
):
    nfield, pitch, radial, axial = f_ref.shape
    planes = nfield + 1
    edge = planes * pitch
    if nspan == 2:
        sent_ref, got_ref = refs[:2]
        refs = refs[2:]
        low_ref = high_ref = got_ref
    else:
        low_ref, high_ref, all_ref = refs[:3]
        refs = refs[3:]
    buf_ref, up_ref, down_ref, speed_ref, halo_ref, face_ref, kern_s, upd_s, lhs_s, acc_s, face_s, near_s = refs
    s = lax.axis_index("span")
    q = lax.axis_index("row")

    total = kern_ref.shape[0]
    kern_s[...] = kern_ref[...].astype(F32)
    main = kern_s[pl.ds(pl.multiple_of(s * radial, 8), radial), :]
    above = kern_s[pl.ds(pl.multiple_of(jnp.minimum((s + 1) * radial, total - 8), 8), 8), :]
    below = kern_s[pl.ds(pl.multiple_of(jnp.maximum(s * radial - 8, 0), 8), 8), :]
    wide = jnp.concatenate([main, jnp.where(iota((EXTRA, total), 0) < 4, above, below)], 0).astype(BF16)
    smoothed = []
    for c in range(2):
        if nspan == 2:
            at = slice(2 * edge + c * radial, 2 * edge + (c + 1) * radial)
            own, other = sent_ref[at, :].astype(F32), got_ref[at, :].astype(F32)
            rows = [jnp.where(s == 0, own, other), jnp.where(s == 0, other, own)]
        else:
            rows = [all_ref[n, c * radial : (c + 1) * radial, :].astype(F32) for n in range(nspan)]
        smoothed.append(
            jnp.dot(wide, jnp.concatenate(rows, 0).astype(BF16), preferred_element_type=F32)
        )
    sa = AXIAL_SPEED * (1.0 + 0.5 * jnp.tanh(smoothed[0]))
    sp = PITCH_SPEED * jnp.tanh(smoothed[1])
    speed_ref[0] = sa
    speed_ref[1] = sp

    chunks = cell_ref.shape[0]
    values, tracers = tv_ref.shape
    capacity = 2 * tracers // npitch
    count = nfield + 2
    table = jnp.concatenate(split(jnp.concatenate([sa[:radial], sp[:radial]], 0)), 0)

    @pl.loop(0, chunks // 2, unroll=True)
    def _(c):
        cells, span = tracer_chunk(cell_ref, c)
        line = lax.shift_right_logical(cells, power(axial)) & (radial - 1)
        got = jnp.dot(table, pick_ref[:, span], preferred_element_type=F32)
        got = got[: 2 * radial] + got[2 * radial :]
        mine = iota((radial, cells.shape[1]), 0) == line
        sampled = [samp_ref[f : f + 1, span] for f in range(nfield)]
        for n in range(2):
            part = jnp.where(mine, got[n * radial : (n + 1) * radial], 0.0)
            sampled.append(jnp.sum(part, 0, keepdims=True))
        for v, value in enumerate(sampled):
            head = tv_ref[v : v + 1, span]
            upd_s[v : v + 1, span] = head + 0.5 * (value - head)
            upd_s[count + v : count + v + 1, span] = tv_ref[count + v : count + v + 1, span] + 0.8 * value

    width = place_ref.shape[0]
    groups = capacity // width
    keys = npitch * groups
    coded = jnp.exp2(CODE * upd_s[:values])
    mine = iota((keys, tracers), 0) == key_ref[...]
    for v in range(values):
        lhs_s[v * keys : (v + 1) * keys, :] = jnp.where(mine, coded[v : v + 1], 0.0).astype(BF16)
    acc_s[...] = lax.dot_general(
        lhs_s[...], place_ref[...], (((1,), (1,)), ((), ())), preferred_element_type=F32
    ).reshape(acc_s.shape)
    room = buf_ref.shape[2] - values * capacity // LANES
    filler = [jnp.zeros((room, LANES), F32)] if room else []
    for d in range(npitch):
        pieces = []
        for g in range(groups):
            for n in range(width // LANES):
                pieces.append(acc_s[:, d * groups + g, n * LANES : (n + 1) * LANES])
        buf_ref[d, q] = jnp.concatenate(pieces + filler, 0).astype(BF16)

    sub = iota((EXTRA, axial), 0)
    near_s[0] = high_ref[: 2 * edge].astype(F32)
    near_s[1] = low_ref[: 2 * edge].astype(F32)

    @pl.loop(0, edge, unroll=True)
    def _(n):
        tile = jnp.where(sub == 0, near_s[0, pl.ds(n, 1), :], 0.0)
        tile = jnp.where(sub == 1, near_s[0, pl.ds(edge + n, 1), :], tile)
        tile = jnp.where(sub == 6, near_s[1, pl.ds(n, 1), :], tile)
        halo_ref[n] = jnp.where(sub == 7, near_s[1, pl.ds(edge + n, 1), :], tile)

    stator = q == 0
    tile = pl.ds(pl.multiple_of((1 - q) * (axial - LANES), LANES), LANES)
    face_s[...] = jnp.zeros(face_s.shape, F32)

    @pl.loop(0, pitch, unroll=True)
    def _(i):
        parts = []
        for f in range(planes):
            core = f_ref[f, i, :, tile] if f < nfield else k_ref[i, :, tile]
            parts += slab(core, halo_ref[f * pitch + i, :, tile])
        first, second = near(stator, parts)
        face_s[pl.ds(i, 1), :] = first
        face_s[pl.ds(pitch + i, 1), :] = second

    parts = []
    for n in range(2):
        speed = speed_ref[n, :, tile]
        parts += slab(speed[:radial], speed[radial:])
    first, second = near(stator, parts + [jnp.zeros((LANES - 2 * SLAB, LANES), F32)])
    face_s[2 * pitch : 2 * pitch + 1] = first
    face_s[2 * pitch + 1 : 2 * pitch + 2] = second
    face = face_s[...]
    face_ref[...] = face
    offset = map_ref[...].astype(F32)
    face_ref[2 * pitch + 2 : 2 * pitch + 3] = jnp.broadcast_to(offset[:, :1], (1, LANES))
    face = face.astype(BF16)

    @pl.loop(0, npitch, unroll=True)
    def _(d):
        buf_ref[d, 1 - q] = face

    def layers(ref, top):
        rows = []
        for f in range(planes):
            for n in range(2):
                i = top * (pitch - 2) + n
                rows.append(f_ref[f, i] if f < nfield else k_ref[i])
        for f in range(planes):
            corner = halo_ref[f * pitch + top * (pitch - 1)]
            rows += [corner[0:1], corner[7:8]]
        rows.append(jnp.zeros((8, axial), F32))
        ref[...] = jnp.concatenate(rows, 0).astype(BF16)

    layers(up_ref, 1)
    layers(down_ref, 0)


class Faces:
    def __init__(self, nspan, speed_ref, radial):
        self.rows, self.lanes = speed_ref.shape[1:]
        shape = (self.rows, self.lanes)
        s = lax.axis_index("span")
        stator = lax.axis_index("row") == 0
        lane, radius = iota(shape, 1), iota(shape, 0)
        sa = TIME_STEP * speed_ref[0]
        sp = TIME_STEP * speed_ref[1]
        wa = 0.5 * (sa + pltpu.roll(sa, self.lanes - 1, 1))
        self.first, self.last = lane == 0, lane == self.lanes - 1
        up, dn = jnp.maximum(wa, 0.0), jnp.minimum(wa, 0.0)
        self.axial = (
            jnp.where(self.last, 0.0, up),
            jnp.where(self.last, 0.0, dn),
            pltpu.roll(jnp.where(self.last, 0.0, up), 1, 1),
            pltpu.roll(jnp.where(self.last, 0.0, dn), 1, 1),
        )
        self.pitch_up, self.pitch_dn = jnp.maximum(sp, 0.0), jnp.minimum(sp, 0.0)
        top, bottom = s == nspan - 1, s == 0
        end = self.rows - 1
        self.wall_up = ((radius == radial - 1) & top) | ((radius == end) & bottom)
        self.wall_dn = ((radius == radial) & top) | ((radius == 0) & bottom)
        inlet = jnp.where(stator & self.first, sa, 0.0)
        keep = 1.0 + inlet - jnp.where(jnp.logical_not(stator) & self.last, sa, 0.0)
        self.keep = keep - self.axial[0] + self.axial[3] - self.pitch_up + self.pitch_dn

    def weights(self, k_before, k, k_after):
        half = 0.5 * TIME_STEP
        k = half * k
        k_up = jnp.where(self.last, 0.0, k + pltpu.roll(k, self.lanes - 1, 1))
        k_dn = jnp.where(self.first, 0.0, k + pltpu.roll(k, 1, 1))
        r_up = jnp.where(self.wall_up, 0.0, k + pltpu.roll(k, self.rows - 1, 0))
        r_dn = jnp.where(self.wall_dn, 0.0, k + pltpu.roll(k, 1, 0))
        p_up, p_dn = k + half * k_after, k + half * k_before
        return (
            self.keep - (k_up + k_dn) - (r_up + r_dn) - (p_up + p_dn),
            k_up - self.axial[1],
            k_dn + self.axial[2],
            r_up,
            r_dn,
            p_up - self.pitch_dn,
            p_dn + self.pitch_up,
        )

    def step(self, w, before, v, after):
        a = w[0] * v + w[1] * pltpu.roll(v, self.lanes - 1, 1)
        b = w[2] * pltpu.roll(v, 1, 1) + w[3] * pltpu.roll(v, self.rows - 1, 0)
        c = w[4] * pltpu.roll(v, 1, 0) + w[5] * after
        return (a + b) + (c + w[6] * before)


def middle(nspan, f_ref, k_ref, speed_ref, halo_ref, o_ref, y4_ref, row_ref, y_s, w_s):
    nfield, pitch, radial, axial = f_ref.shape
    stator = lax.axis_index("row") == 0
    faces = Faces(nspan, speed_ref, radial)

    def state(f, i):
        return jnp.concatenate([f_ref[f, i], halo_ref[f * pitch + i]], 0)

    def kappa(i):
        return jnp.concatenate([k_ref[i], halo_ref[nfield * pitch + i]], 0)

    @pl.loop(1, pitch - 1, unroll=True)
    def _(i):
        w = faces.weights(kappa(i - 1), kappa(i), kappa(i + 1))
        for n, value in enumerate(w):
            w_s[n, i] = value
        for f in range(nfield):
            y_s[f, i] = faces.step(w, state(f, i - 1), state(f, i), state(f, i + 1))

    @pl.loop(2, pitch - 2, unroll=True)
    def _(i):
        w = [w_s[n, i] for n in range(7)]
        for f in range(nfield):
            o_ref[f, i - 2] = faces.step(w, y_s[f, i - 1], y_s[f, i], y_s[f, i + 1])[:radial]

    for f in range(nfield):
        for n, i in enumerate((1, 2, pitch - 3, pitch - 2)):
            y4_ref[f, n] = y_s[f, i]
    row_ref[...] = jnp.zeros(row_ref.shape, F32)
    q = lax.axis_index("row")
    tile = pl.ds(pl.multiple_of((1 - q) * (axial - LANES), LANES), LANES)
    blank = jnp.zeros((SLAB, LANES), F32)

    @pl.loop(1, pitch - 1, unroll=True)
    def _(i):
        parts = []
        for f in range(nfield):
            parts += slab(y_s[f, i, :radial, tile], y_s[f, i, radial:, tile])
        row_ref[pl.ds(i, 1), :] = near(stator, parts + [blank])[0]


def edges(
    nspan, f_ref, k_ref, speed_ref, halo_ref, lower_ref, upper_ref, y4_ref, row_ref, o_ref, row_out, beyond_ref, y_s
):
    nfield, pitch, radial, axial = f_ref.shape
    planes = nfield + 1
    stator = lax.axis_index("row") == 0
    faces = Faces(nspan, speed_ref, radial)
    ext = {-1: lower_ref[...].astype(F32), 1: upper_ref[...].astype(F32)}
    sub = iota((EXTRA, axial), 0)
    corner_at = 2 * planes * radial

    def state(f, i):
        if 0 <= i < pitch:
            core = f_ref[f, i] if f < nfield else k_ref[i]
            return jnp.concatenate([core, halo_ref[f * pitch + i]], 0)
        side = ext[-1 if i < 0 else 1]
        at = (2 * f + (i + 2 if i < 0 else i - pitch)) * radial
        extra = jnp.zeros((EXTRA, axial), F32)
        if i in (-1, pitch):
            corner = corner_at + 2 * f
            extra = jnp.where(sub == 0, side[corner : corner + 1], 0.0)
            extra = jnp.where(sub == 7, side[corner + 1 : corner + 2], extra)
        return jnp.concatenate([side[at : at + radial], extra], 0)

    row_out[...] = row_ref[...]
    beyond_ref[...] = jnp.zeros(beyond_ref.shape, F32)
    tile = pl.ds(pl.multiple_of(lax.axis_index("row") * (LANES - axial) + axial - LANES, LANES), LANES)

    def edge_lanes(value):
        return jnp.where(stator, value[:, axial - LANES :], value[:, :LANES])

    blank = jnp.zeros((SLAB, LANES), F32)
    held = {i: n for n, i in enumerate((1, 2, pitch - 3, pitch - 2))}
    for side, new, done in ((0, (-1, 0), (0, 1)), (1, (pitch - 1, pitch), (pitch - 2, pitch - 1))):
        touched = sorted({*new, *done})
        k = {i: state(nfield, i) for i in range(touched[0] - 1, touched[-1] + 2)}
        w = {i: faces.weights(k[i - 1], k[i], k[i + 1]) for i in touched}
        for f in range(nfield):
            x = {i: state(f, i) for i in range(new[0] - 1, new[1] + 2)}
            y = {i: y4_ref[f, held[i]] for i in held if done[0] - 1 <= i <= done[1] + 1}
            for i in new:
                y[i] = faces.step(w[i], x[i - 1], x[i], x[i + 1])
            for n, i in enumerate(done):
                o_ref[f, 2 * side + n] = faces.step(w[i], y[i - 1], y[i], y[i + 1])[:radial]
            y_s[f] = y[0 if side == 0 else pitch - 1]
        parts = []
        for f in range(nfield):
            parts += slab(y_s[f, :radial, tile], y_s[f, radial:, tile])
        i = 0 if side == 0 else pitch - 1
        row_out[i : i + 1] = near(stator, parts + [blank])[0]
        parts = []
        for f in range(planes):
            value = edge_lanes(state(f, -1 if side == 0 else pitch))
            parts += slab(value[:radial], value[radial:])
        beyond_ref[side : side + 1] = near(stator, parts)[0]


def interface(
    npitch,
    nspan,
    mid_ref,
    edge_ref,
    face_ref,
    row_ref,
    beyond_ref,
    buf_ref,
    o_ref,
    arr_ref,
    arr_s,
    tile_s,
    ring_s,
    add_s,
    sems,
):
    nfield, pitch, radial, axial = o_ref.shape
    planes = nfield + 1
    s = lax.axis_index("span")
    q = lax.axis_index("row")
    stator = q == 0
    near_tile = pl.ds(pl.multiple_of((1 - q) * (axial - LANES), LANES), LANES)
    copies = []
    if axial > LANES:
        rest = pl.ds(pl.multiple_of(q * LANES, LANES), axial - LANES)
        copies += [
            pltpu.make_async_copy(
                mid_ref.at[:, :, :, rest], o_ref.at[:, 2 : pitch - 2, :, rest], sems.at[0]
            ),
            pltpu.make_async_copy(
                edge_ref.at[:, :2, :, rest], o_ref.at[:, :2, :, rest], sems.at[1]
            ),
            pltpu.make_async_copy(
                edge_ref.at[:, 2:, :, rest], o_ref.at[:, pitch - 2 :, :, rest], sems.at[2]
            ),
        ]
    for copy in copies:
        copy.start()

    values = arr_ref.shape[0]
    capacity = arr_ref.shape[1] // npitch

    @pl.loop(0, npitch, unroll=True)
    def _(p):
        coded = buf_ref[p, q].astype(F32)
        plain = jnp.where(coded > 0.0, jnp.log2(coded) * (1.0 / CODE), 0.0)
        for j in range(capacity // LANES):
            at = pl.ds(pl.multiple_of(p * capacity + j * LANES, LANES), LANES)
            arr_s[:, at] = plain[j * values : (j + 1) * values]

    copies.append(pltpu.make_async_copy(arr_s, arr_ref, sems.at[3]))
    copies[-1].start()

    whole = npitch * pitch
    count = pitch + 8

    @pl.loop(0, npitch, unroll=True)
    def _(p):
        at = pl.ds(pl.multiple_of(p * pitch, pitch), pitch)
        both = buf_ref[p, 1 - q].astype(F32)
        ring_s[0, at, :] = both[:pitch]
        ring_s[1, at, :] = both[pitch : 2 * pitch]

    for n in range(2):
        ring_s[n, whole : whole + pitch] = ring_s[n, :pitch]
        ring_s[n, whole + pitch :] = ring_s[n, pitch : pitch + 8]
    begin = jnp.max(face_ref[2 * pitch + 2 : 2 * pitch + 3]).astype(jnp.int32) - 1
    begin = jnp.where(begin < 0, begin + whole, begin)
    ghost = ring_s[0, pl.ds(begin, count), :]
    farther = ring_s[1, pl.ds(begin, count), :]
    tail = jnp.zeros((count - pitch - 2, LANES), F32)
    own = jnp.concatenate(
        [beyond_ref[0:1], face_ref[:pitch], beyond_ref[1:2], tail], 0
    )
    top = jnp.zeros((1, LANES), F32)
    own_k1 = jnp.concatenate([top, face_ref[pitch : 2 * pitch], top, tail], 0)
    own_new = jnp.concatenate([top, row_ref[...], top, tail], 0)
    at = 2 * pitch

    def groups(row, g):
        out = row
        for f in range(planes):
            if f != g:
                out = jnp.where(iota(row.shape, 1) // SLAB == f, pltpu.roll(row, (f - g) * SLAB % LANES, 1), out)
        return out

    def speeds(rows):
        rows = TIME_STEP * rows
        return groups(rows[0:1], 0), groups(rows[1:2], 0), groups(rows[0:1], 1)

    sa0, sa1, sp0 = speeds(face_ref[at : at + 2])
    ga0, ga1, gp0 = speeds(buf_ref[0, 1 - q].astype(F32)[at : at + 2])
    shape = (count, LANES)
    lane = iota(shape, 1)
    group = lax.shift_right_logical(lane, power(SLAB))
    radius = lane & (SLAB - 1)

    def spread(x):
        out = x
        for f in range(nfield):
            out = jnp.where(group == f, pltpu.roll(x, (f + 1) * SLAB, 1), out)
        return out

    half = 0.5 * TIME_STEP
    k0, k1, g0, g1 = spread(own), spread(own_k1), spread(ghost), spread(farther)
    wall = ((radius == 7 + radial) & (s == nspan - 1)) | ((radius == 7) & (s == 0))

    def ahead(x):
        return pltpu.roll(x, count - 1, 0)

    def outward(x):
        return pltpu.roll(x, LANES - 1, 1)

    def change(v, k, speed):
        kappa = half * (k + ahead(k))
        up, dn = jnp.maximum(speed, 0.0), jnp.minimum(speed, 0.0)
        along = (up + kappa) * v + (dn - kappa) * ahead(v)
        kappa = jnp.where(wall, 0.0, half * (k + outward(k)))
        across = kappa * (v - outward(v))
        return along - pltpu.roll(along, 1, 0) + across - pltpu.roll(across, 1, 1)

    def face(first, second, speed, kappa):
        lower = jnp.where(stator, first, second)
        upper = jnp.where(stator, second, first)
        return (jnp.maximum(speed, 0.0) + kappa) * lower + (jnp.minimum(speed, 0.0) - kappa) * upper

    sign = jnp.where(stator, 1.0, -1.0)
    speed = 0.5 * (sa0 + ga0)
    kappa = half * (k0 + g0)
    flux = sign * face(own, ghost, speed, kappa)
    shift = -flux
    ghost_new = (
        ghost
        + flux
        - sign * face(ghost, farther, 0.5 * (ga0 + ga1), half * (g0 + g1))
        - change(ghost, g0, gp0)
    )
    flux = sign * face(own_new + shift, ghost_new, speed, kappa)
    inner = 0.5 * (sa0 + sa1)
    kappa = half * (k0 + k1)
    inner = sign * jnp.where(
        stator, jnp.minimum(inner, 0.0) - kappa, jnp.maximum(inner, 0.0) + kappa
    ) * shift
    add0 = shift - change(shift, k0, sp0) + inner - flux
    add1 = -inner

    row = iota((LANES, LANES), 0)
    near_row = jnp.where(stator, LANES - 1, 0)
    far_row = jnp.where(stator, LANES - 2, 1)
    add_s[0], add_s[1] = add0, add1

    def column(i, old):
        block = jnp.where(
            row == near_row,
            add_s[0, pl.ds(i + 1, 1), :],
            jnp.where(row == far_row, add_s[1, pl.ds(i + 1, 1), :], 0.0),
        ).T
        for f in range(nfield):
            tile_s[f, i] = old(f) + block[f * SLAB + 8 : f * SLAB + 8 + radial]

    @pl.loop(2, pitch - 2, unroll=True)
    def _(i):
        column(i, lambda f: mid_ref[f, i - 2, :, near_tile])

    @pl.loop(0, 4, unroll=True)
    def _(n):
        column(jnp.where(n < 2, n, n + pitch - 4), lambda f: edge_ref[f, n, :, near_tile])

    copies.append(pltpu.make_async_copy(tile_s, o_ref.at[:, :, :, near_tile], sems.at[4]))
    copies[-1].start()
    for copy in copies:
        copy.wait()


def local(
    fields,
    diffusivity,
    mean_flow,
    radial_kernel,
    tracer_values,
    tracer_cells,
    tracer_dest,
    interface_map,
):
    npitch = lax.axis_size("pitch")
    nspan = lax.axis_size("span")
    nfield, pitch, radial, axial = fields.shape
    planes = nfield + 1
    values, tracers = tracer_values.shape
    chunks = tracers // LANES
    capacity = 2 * tracers // npitch
    edge = planes * pitch
    cells = tracer_cells.reshape(chunks, LANES)
    dest = tracer_dest.reshape(chunks, LANES)

    mean_rows = 2 * radial
    if nspan == 2:
        outs = [((2 * edge + mean_rows, axial), BF16)]
    else:
        outs = [((2 * edge, axial), BF16)] * 2 + [((mean_rows, axial), BF16)]
    inputs = [fields, diffusivity, radial_kernel, tracer_values, cells, dest, interface_map, mean_flow]
    *packed, fields, diffusivity, radial_kernel, tracer_values, cells, dest, interface_map = call(
        lambda *refs: pack_span(nspan, len(inputs), *refs),
        outs + [(x.shape, x.dtype) for x in inputs[:-1]],
        [pltpu.with_memory_space_constraint(x, pltpu.HBM) for x in inputs],
        [HBM] * len(inputs),
        [
            pltpu.VMEM(mean_flow.shape, mean_flow.dtype),
            pltpu.SemaphoreType.DMA((len(inputs) + 2,)),
        ],
        nbytes=2**20,
        fixed=True,
    )
    if nspan == 2:
        span_got = (packed[0], lax.ppermute(packed[0], "span", [(0, 1), (1, 0)]))
    else:
        span_got = (
            lax.ppermute(packed[0], "span", [(n, n + 1) for n in range(nspan - 1)]),
            lax.ppermute(packed[1], "span", [(n + 1, n) for n in range(nspan - 1)]),
            lax.all_gather(packed[2], "span"),
        )

    width = min(2 * LANES, capacity)
    sampled = call(
        lambda *refs: sample_fields(npitch, *refs),
        [
            ((8, tracers), F32),
            ((width, tracers), BF16),
            ((1, tracers), jnp.int32),
            ((axial, tracers), BF16),
        ],
        (fields, cells, dest),
        [VMEM] * 3,
        [pltpu.VMEM((nfield, pitch * radial, axial), BF16)],
        flops=4 * nfield * pitch * radial * axial * tracers,
        nbytes=2**20,
    )

    rows = radial + EXTRA
    per_slot = max(values * capacity // LANES, 2 * pitch + 3)
    per_slot = -(-per_slot // 8) * 8
    halo_rows = 2 * planes * radial + 16
    buf, up, down, speeds, halo, face = call(
        lambda *refs: dispatch(npitch, nspan, *refs),
        [
            ((npitch, 2, per_slot, LANES), BF16),
            ((halo_rows, axial), BF16),
            ((halo_rows, axial), BF16),
            ((2, rows, axial), F32),
            ((edge, EXTRA, axial), F32),
            ((per_slot, LANES), F32),
        ],
        (
            fields,
            diffusivity,
            radial_kernel,
            tracer_values,
            cells,
            interface_map,
        )
        + tuple(sampled)
        + span_got,
        [VMEM] * (10 + len(span_got)),
        [
            pltpu.VMEM(radial_kernel.shape, F32),
            pltpu.VMEM((16, tracers), F32),
            pltpu.VMEM((values * npitch * capacity // width, tracers), BF16),
            pltpu.VMEM((values, npitch * capacity // width, width), F32),
            pltpu.VMEM((per_slot, LANES), F32),
            pltpu.VMEM((2, 2 * edge, axial), F32),
        ],
        flops=2 * npitch * values * tracers * capacity,
        nbytes=2**21,
    )
    buf = lax.all_to_all(
        buf.reshape(npitch * 2, per_slot, LANES), ("pitch", "row"), 0, 0
    ).reshape(buf.shape)
    ring = [(n, (n + 1) % npitch) for n in range(npitch)]
    lower = lax.ppermute(up, "pitch", ring)
    upper = lax.ppermute(down, "pitch", [(b, a) for a, b in ring])

    mid, near_edge, new_rows = call(
        lambda *refs: middle(nspan, *refs),
        [
            ((nfield, pitch - 4, radial, axial), F32),
            ((nfield, 4, rows, axial), F32),
            ((pitch, LANES), F32),
        ],
        (fields, diffusivity, speeds, halo),
        [VMEM] * 4,
        [
            pltpu.VMEM((nfield, pitch, rows, axial), F32),
            pltpu.VMEM((7, pitch, rows, axial), F32),
        ],
        flops=2**24,
        nbytes=2**22,
    )
    outer, new_rows, beyond = call(
        lambda *refs: edges(nspan, *refs),
        [
            ((nfield, 4, radial, axial), F32),
            ((pitch, LANES), F32),
            ((8, LANES), F32),
        ],
        (fields, diffusivity, speeds, halo, lower, upper, near_edge, new_rows),
        [VMEM] * 8,
        [pltpu.VMEM((nfield, rows, axial), F32)],
        flops=2**23,
        nbytes=2**21,
    )
    return call(
        lambda *refs: interface(npitch, nspan, *refs),
        [(fields.shape, F32), ((values, npitch * capacity), F32)],
        (mid, outer, face, new_rows, beyond, buf),
        [VMEM] * 6,
        [
            pltpu.VMEM((values, npitch * capacity), F32),
            pltpu.VMEM((nfield, pitch, radial, LANES), F32),
            pltpu.VMEM((2, npitch * pitch + pitch + 8, LANES), F32),
            pltpu.VMEM((2, pitch + 8, LANES), F32),
            pltpu.SemaphoreType.DMA((5,)),
        ],
        flops=2**22,
        nbytes=2**21,
        place=ANY,
    )


def solution(mesh):
    placed = (
        P(None, "pitch", "span", "row"),
        P("pitch", "span", "row"),
        P("span", None, "row"),
        P(),
        P(None, ("pitch", "span", "row")),
        P(("pitch", "span", "row")),
        P(("pitch", "span", "row"), None),
        P("row", "pitch"),
    )
    return jax.shard_map(
        local,
        mesh=mesh,
        in_specs=placed,
        out_specs=(P(None, "pitch", "span", "row"), P(None, ("pitch", "span", "row"))),
        check_vma=False,
    )
```

```python
import jax
import jax.numpy as jnp
from jax import lax
from jax.experimental import pallas as pl
from jax.experimental.pallas import tpu as pltpu
from jax.sharding import PartitionSpec as P

SUB = 2
TIME_STEP = 0.9
AXIAL_SPEED = 0.15
PITCH_SPEED = 0.15
LANES = 128
EXTRA = 8
SLAB = 32
F32 = jnp.float32
BF16 = jnp.bfloat16
VMEM = pl.BlockSpec(memory_space=pltpu.VMEM)
ANY = pl.BlockSpec(memory_space=pl.ANY)
HBM = pl.BlockSpec(memory_space=pltpu.HBM)
CODE = 10.0
FINE = 18.0
VMEM_LIMIT = 48 * 1024 * 1024


def iota(shape, dim):
    return lax.broadcasted_iota(jnp.int32, shape, dim)


def split(x):
    high = x.astype(BF16)
    return high, (x - high.astype(F32)).astype(BF16)


def power(n):
    assert n & (n - 1) == 0
    return n.bit_length() - 1


def call(body, outs, args, specs, scratch=(), flops=0, nbytes=0, place=VMEM, fixed=False, passed=()):
    shape = pltpu.VMEM if fixed else jax.ShapeDtypeStruct
    return pl.pallas_call(
        body,
        out_shape=tuple(shape(s, d) for s, d in outs),
        in_specs=list(specs),
        out_specs=place if isinstance(place, tuple) else tuple(ANY if n in passed else place for n in range(len(outs))),
        input_output_aliases={n: n for n in passed},
        scratch_shapes=list(scratch),
        compiler_params=pltpu.CompilerParams(vmem_limit_bytes=VMEM_LIMIT),
        cost_estimate=pl.CostEstimate(flops=flops, bytes_accessed=nbytes, transcendentals=0),
    )(*args)


def pack_span(nspan, n_in, *refs):
    ins, rest = refs[:n_in], refs[n_in:]
    outs, kept, (m_s, sems) = rest[: -n_in - 1], rest[-n_in - 1 : -2], rest[-2:]
    f_ref, k_ref = kept[:2]
    radial, axial = f_ref.shape[2:]
    s = lax.axis_index("span")
    half = radial - 8
    early = [pltpu.make_async_copy(ins[-1], m_s, sems.at[0])]
    late = []
    for n, first, size in ((0, (1 - s) * half, 8), (1, s * 8, half)):
        rows = pl.ds(pl.multiple_of(first, 8), size)
        copies = [
            pltpu.make_async_copy(
                ins[0].at[:, :, rows, :], f_ref.at[:, :, rows, :], sems.at[1 + 2 * n]
            ),
            pltpu.make_async_copy(ins[1].at[:, rows, :], k_ref.at[:, rows, :], sems.at[2 + 2 * n]),
        ]
        if n == 0 or nspan > 2:
            early += copies
        else:
            late += copies
    for n in range(2, n_in - 1):
        late.append(pltpu.make_async_copy(ins[n], kept[n], sems.at[n + 3]))
    for copy in early + late:
        copy.start()
    for copy in early:
        copy.wait()

    def edge(first):
        parts = []
        for r in range(2):
            row = pl.ds(first + r, 1)
            parts += [f_ref[:, :, row, :].reshape(-1, axial), k_ref[:, row, :].reshape(-1, axial)]
        return jnp.concatenate(parts, 0).astype(BF16)

    flow = m_s[...].astype(F32)
    flow = jnp.concatenate([flow[:, 0, :], flow[:, 1, :]], 0).astype(BF16)
    def corner(layer):
        stator = lax.axis_index("row") == 0
        return jnp.where(stator, layer[:, axial - LANES :], layer[:, :LANES]).astype(BF16)

    if nspan == 2:
        packed = edge((1 - s) * (radial - 2))
        outs[1][...] = packed
        both = packed.astype(F32)
        half = both.shape[0] // 2
        near = corner(jnp.where(s == 0, both[half:], both[:half]))
        half = near.shape[0] // 2
        outs[0][: 2 * radial] = flow
        outs[0][2 * radial :, :LANES] = near[:half]
        outs[0][2 * radial :, LANES : 2 * LANES] = near[half:]
    else:
        top, bottom = edge(radial - 2), edge(0)
        half = top.shape[0] // 2
        outs[0][...] = top
        outs[1][...] = bottom
        outs[2][...] = corner(top[half:].astype(F32))
        outs[3][...] = corner(bottom[:half].astype(F32))
        outs[4][...] = flow
    for copy in late:
        copy.wait()


def tracer_chunk(ref, c):
    both = [ref[pl.ds(2 * c + n, 1), :] for n in range(2)]
    return jnp.concatenate(both, 1), pl.ds(pl.multiple_of(c * 2 * LANES, 2 * LANES), 2 * LANES)


def one_hot(rows, index):
    return (iota((rows, index.shape[1]), 0) == index).astype(F32).astype(BF16)


def sample_fields(npitch, f_ref, cell_ref, dest_ref, samp_ref, place_ref, key_ref, pick_ref, table_s):
    nfield, pitch, radial, axial = f_ref.shape
    lines = pitch * radial
    chunks = cell_ref.shape[0]

    @pl.loop(0, nfield, unroll=True)
    def _(f):
        table_s[f] = jnp.exp2(FINE * f_ref[f].reshape(lines, axial)).astype(BF16)

    table = table_s[...].reshape(nfield * lines, axial)
    samp_ref[...] = jnp.zeros(samp_ref.shape, F32)

    @pl.loop(0, chunks // 2, unroll=True)
    def _(c):
        cells, span = tracer_chunk(cell_ref, c)
        pick = one_hot(axial, cells & (axial - 1))
        pick_ref[:, span] = pick
        got = jnp.dot(table, pick, preferred_element_type=F32)
        mine = iota((lines, cells.shape[1]), 0) == lax.shift_right_logical(cells, power(axial))
        for f in range(nfield):
            part = jnp.where(mine, got[f * lines : (f + 1) * lines], 0.0)
            part = jnp.sum(part, 0, keepdims=True)
            samp_ref[f : f + 1, span] = jnp.log2(part) * (1.0 / FINE)

    ones = []
    for c in range(chunks):
        ones.append((iota((npitch, LANES), 0) == dest_ref[c : c + 1, :]).astype(F32))
    stacked = jnp.concatenate(ones, 0)
    before = (iota((LANES, LANES), 0) < iota((LANES, LANES), 1)).astype(F32).astype(BF16)
    prefix = jnp.dot(stacked.astype(BF16), before, preferred_element_type=F32)
    carry = jnp.zeros((npitch, 1), F32)
    for c in range(chunks):
        rank = prefix[c * npitch : (c + 1) * npitch] + carry
        slot = jnp.sum(rank * ones[c], 0, keepdims=True).astype(jnp.int32)
        span = slice(c * LANES, (c + 1) * LANES)
        width = place_ref.shape[0]
        place_ref[:, span] = one_hot(width, slot & (width - 1))
        groups = 2 * chunks * LANES // npitch // width
        key_ref[:, span] = dest_ref[c : c + 1, :] * groups + lax.shift_right_logical(slot, power(width))
        carry = carry + jnp.sum(ones[c], 1, keepdims=True)


def slab(core, extra):
    return [extra, core, extra]


def near(stator, parts):
    turned = jnp.concatenate(parts, 0).T
    return (
        jnp.where(stator, turned[LANES - 1 : LANES], turned[0:1]),
        jnp.where(stator, turned[LANES - 2 : LANES - 1], turned[1:2]),
    )


def dispatch(
    npitch,
    nspan,
    f_ref,
    k_ref,
    kern_ref,
    tv_ref,
    cell_ref,
    map_ref,
    samp_ref,
    place_ref,
    key_ref,
    pick_ref,
    *refs,
):
    nfield, pitch, radial, axial = f_ref.shape
    planes = nfield + 1
    edge = planes * pitch
    if nspan == 2:
        sent_ref, got_ref = refs[:2]
        refs = refs[2:]
    else:
        low_ref, high_ref, all_ref = refs[:3]
        refs = refs[3:]
    buf_ref, speed_ref, face_ref, kern_s, upd_s, lhs_s, acc_s, face_s, near_s = refs
    s = lax.axis_index("span")
    q = lax.axis_index("row")

    total = kern_ref.shape[0]
    kern_s[...] = kern_ref[...].astype(F32)
    main = kern_s[pl.ds(pl.multiple_of(s * radial, 8), radial), :]
    above = kern_s[pl.ds(pl.multiple_of(jnp.minimum((s + 1) * radial, total - 8), 8), 8), :]
    below = kern_s[pl.ds(pl.multiple_of(jnp.maximum(s * radial - 8, 0), 8), 8), :]
    wide = jnp.concatenate([main, jnp.where(iota((EXTRA, total), 0) < 4, above, below)], 0).astype(BF16)
    smoothed = []
    for c in range(2):
        if nspan == 2:
            at = slice(c * radial, (c + 1) * radial)
            own, other = sent_ref[at, :].astype(F32), got_ref[at, :].astype(F32)
            rows = [jnp.where(s == 0, own, other), jnp.where(s == 0, other, own)]
        else:
            rows = [all_ref[n, c * radial : (c + 1) * radial, :].astype(F32) for n in range(nspan)]
        smoothed.append(
            jnp.dot(wide, jnp.concatenate(rows, 0).astype(BF16), preferred_element_type=F32)
        )
    sa = AXIAL_SPEED * (1.0 + 0.5 * jnp.tanh(smoothed[0]))
    sp = PITCH_SPEED * jnp.tanh(smoothed[1])
    speed_ref[0] = sa
    speed_ref[1] = sp

    chunks = cell_ref.shape[0]
    values, tracers = tv_ref.shape
    capacity = 2 * tracers // npitch
    count = nfield + 2
    table = jnp.concatenate(split(jnp.concatenate([sa[:radial], sp[:radial]], 0)), 0)

    @pl.loop(0, chunks // 2, unroll=True)
    def _(c):
        cells, span = tracer_chunk(cell_ref, c)
        line = lax.shift_right_logical(cells, power(axial)) & (radial - 1)
        got = jnp.dot(table, pick_ref[:, span], preferred_element_type=F32)
        got = got[: 2 * radial] + got[2 * radial :]
        mine = iota((radial, cells.shape[1]), 0) == line
        sampled = [samp_ref[f : f + 1, span] for f in range(nfield)]
        for n in range(2):
            part = jnp.where(mine, got[n * radial : (n + 1) * radial], 0.0)
            sampled.append(jnp.sum(part, 0, keepdims=True))
        for v, value in enumerate(sampled):
            head = tv_ref[v : v + 1, span]
            upd_s[v : v + 1, span] = head + 0.5 * (value - head)
            upd_s[count + v : count + v + 1, span] = tv_ref[count + v : count + v + 1, span] + 0.8 * value

    width = place_ref.shape[0]
    groups = capacity // width
    keys = npitch * groups
    coded = jnp.exp2(CODE * upd_s[:values])
    mine = iota((keys, tracers), 0) == key_ref[...]
    for v in range(values):
        lhs_s[v * keys : (v + 1) * keys, :] = jnp.where(mine, coded[v : v + 1], 0.0).astype(BF16)
    acc_s[...] = lax.dot_general(
        lhs_s[...], place_ref[...], (((1,), (1,)), ((), ())), preferred_element_type=F32
    ).reshape(acc_s.shape)
    room = buf_ref.shape[2] - values * capacity // LANES
    filler = [jnp.zeros((room, LANES), F32)] if room else []
    for d in range(npitch):
        pieces = []
        for g in range(groups):
            for n in range(width // LANES):
                pieces.append(acc_s[:, d * groups + g, n * LANES : (n + 1) * LANES])
        buf_ref[d, q] = jnp.concatenate(pieces + filler, 0).astype(BF16)

    if nspan == 2:
        near_s[0, : edge // 2] = got_ref[2 * radial :, :LANES].astype(F32)
        near_s[0, edge // 2 :] = got_ref[2 * radial :, LANES : 2 * LANES].astype(F32)
        near_s[1] = near_s[0]
    else:
        near_s[0] = high_ref[...].astype(F32)
        near_s[1] = low_ref[...].astype(F32)
    sub = iota((EXTRA, LANES), 0)

    def beside(n):
        return jnp.where(
            sub == 0, near_s[0, n : n + 1], jnp.where(sub == 7, near_s[1, n : n + 1], 0.0)
        )

    stator = q == 0
    tile = pl.ds(pl.multiple_of((1 - q) * (axial - LANES), LANES), LANES)
    face_s[...] = jnp.zeros(face_s.shape, F32)

    for i in range(pitch):
        parts = []
        for f in range(planes):
            core = f_ref[f, i, :, tile] if f < nfield else k_ref[i, :, tile]
            parts += slab(core, beside(f * pitch + i))
        first, second = near(stator, parts)
        face_s[i : i + 1] = first
        face_s[pitch + i : pitch + i + 1] = second

    parts = []
    for n in range(2):
        speed = speed_ref[n, :, tile]
        parts += slab(speed[:radial], speed[radial:])
    first, second = near(stator, parts + [jnp.zeros((LANES - 2 * SLAB, LANES), F32)])
    face_s[2 * pitch : 2 * pitch + 1] = first
    face_s[2 * pitch + 1 : 2 * pitch + 2] = second
    face = face_s[...]
    face_ref[...] = face
    offset = map_ref[...].astype(F32)
    face_ref[2 * pitch + 2 : 2 * pitch + 3] = jnp.broadcast_to(offset[:, :1], (1, LANES))
    face = face.astype(BF16)

    @pl.loop(0, npitch, unroll=True)
    def _(d):
        buf_ref[d, 1 - q] = face


def halos(low_ref, high_ref, f_ref, k_ref, halo_ref, up_ref, down_ref, near_s):
    nfield, pitch, radial, axial = f_ref.shape
    planes = nfield + 1
    edge = planes * pitch
    sub = iota((EXTRA, axial), 0)
    near_s[0] = high_ref[: 2 * edge].astype(F32)
    near_s[1] = low_ref[: 2 * edge].astype(F32)

    @pl.loop(0, edge, unroll=True)
    def _(n):
        tile = jnp.where(sub == 0, near_s[0, pl.ds(n, 1), :], 0.0)
        tile = jnp.where(sub == 1, near_s[0, pl.ds(edge + n, 1), :], tile)
        tile = jnp.where(sub == 6, near_s[1, pl.ds(n, 1), :], tile)
        halo_ref[n] = jnp.where(sub == 7, near_s[1, pl.ds(edge + n, 1), :], tile)

    def layers(ref, top):
        rows = []
        for f in range(planes):
            for n in range(2):
                i = top * (pitch - 2) + n
                rows.append(f_ref[f, i] if f < nfield else k_ref[i])
        for f in range(planes):
            corner = halo_ref[f * pitch + top * (pitch - 1)]
            rows += [corner[0:1], corner[7:8]]
        rows.append(jnp.zeros((8, axial), F32))
        ref[...] = jnp.concatenate(rows, 0).astype(BF16)

    layers(up_ref, 1)
    layers(down_ref, 0)


class Faces:
    def __init__(self, nspan, speed_ref, radial):
        self.rows, self.lanes = speed_ref.shape[1:]
        shape = (self.rows, self.lanes)
        s = lax.axis_index("span")
        stator = lax.axis_index("row") == 0
        lane, radius = iota(shape, 1), iota(shape, 0)
        sa = TIME_STEP * speed_ref[0]
        sp = TIME_STEP * speed_ref[1]
        wa = 0.5 * (sa + pltpu.roll(sa, self.lanes - 1, 1))
        self.first, self.last = lane == 0, lane == self.lanes - 1
        up, dn = jnp.maximum(wa, 0.0), jnp.minimum(wa, 0.0)
        self.axial = (
            jnp.where(self.last, 0.0, up),
            jnp.where(self.last, 0.0, dn),
            pltpu.roll(jnp.where(self.last, 0.0, up), 1, 1),
            pltpu.roll(jnp.where(self.last, 0.0, dn), 1, 1),
        )
        self.pitch_up, self.pitch_dn = jnp.maximum(sp, 0.0), jnp.minimum(sp, 0.0)
        top, bottom = s == nspan - 1, s == 0
        end = self.rows - 1
        self.wall_up = ((radius == radial - 1) & top) | ((radius == end) & bottom)
        self.wall_dn = ((radius == radial) & top) | ((radius == 0) & bottom)
        inlet = jnp.where(stator & self.first, sa, 0.0)
        keep = 1.0 + inlet - jnp.where(jnp.logical_not(stator) & self.last, sa, 0.0)
        self.keep = keep - self.axial[0] + self.axial[3] - self.pitch_up + self.pitch_dn

    def weights(self, k_before, k, k_after):
        half = 0.5 * TIME_STEP
        k = half * k
        k_up = jnp.where(self.last, 0.0, k + pltpu.roll(k, self.lanes - 1, 1))
        k_dn = jnp.where(self.first, 0.0, k + pltpu.roll(k, 1, 1))
        r_up = jnp.where(self.wall_up, 0.0, k + pltpu.roll(k, self.rows - 1, 0))
        r_dn = jnp.where(self.wall_dn, 0.0, k + pltpu.roll(k, 1, 0))
        p_up, p_dn = k + half * k_after, k + half * k_before
        return (
            self.keep - (k_up + k_dn) - (r_up + r_dn) - (p_up + p_dn),
            k_up - self.axial[1],
            k_dn + self.axial[2],
            r_up,
            r_dn,
            p_up - self.pitch_dn,
            p_dn + self.pitch_up,
        )

    def step(self, w, before, v, after):
        a = w[0] * v + w[1] * pltpu.roll(v, self.lanes - 1, 1)
        b = w[2] * pltpu.roll(v, 1, 1) + w[3] * pltpu.roll(v, self.rows - 1, 0)
        c = w[4] * pltpu.roll(v, 1, 0) + w[5] * after
        return (a + b) + (c + w[6] * before)


def middle(nspan, f_ref, k_ref, speed_ref, halo_ref, o_ref, y4_ref, row_ref, y_s, w_s):
    nfield, pitch, radial, axial = f_ref.shape
    stator = lax.axis_index("row") == 0
    faces = Faces(nspan, speed_ref, radial)

    def state(f, i):
        return jnp.concatenate([f_ref[f, i], halo_ref[f * pitch + i]], 0)

    def kappa(i):
        return jnp.concatenate([k_ref[i], halo_ref[nfield * pitch + i]], 0)

    @pl.loop(1, pitch - 1, unroll=True)
    def _(i):
        w = faces.weights(kappa(i - 1), kappa(i), kappa(i + 1))
        for n, value in enumerate(w):
            w_s[n, i] = value
        for f in range(nfield):
            y_s[f, i] = faces.step(w, state(f, i - 1), state(f, i), state(f, i + 1))

    @pl.loop(2, pitch - 2, unroll=True)
    def _(i):
        w = [w_s[n, i] for n in range(7)]
        for f in range(nfield):
            o_ref[f, i - 2] = faces.step(w, y_s[f, i - 1], y_s[f, i], y_s[f, i + 1])[:radial]

    for f in range(nfield):
        for n, i in enumerate((1, 2, pitch - 3, pitch - 2)):
            y4_ref[f, n] = y_s[f, i]
    row_ref[...] = jnp.zeros(row_ref.shape, F32)
    q = lax.axis_index("row")
    tile = pl.ds(pl.multiple_of((1 - q) * (axial - LANES), LANES), LANES)
    blank = jnp.zeros((SLAB, LANES), F32)

    @pl.loop(1, pitch - 1, unroll=True)
    def _(i):
        parts = []
        for f in range(nfield):
            parts += slab(y_s[f, i, :radial, tile], y_s[f, i, radial:, tile])
        row_ref[pl.ds(i, 1), :] = near(stator, parts + [blank])[0]


def contribution(nspan, pitch, radial, face_ref, beyond, new_rows, window_ref):
    planes = LANES // SLAB
    nfield = planes - 1
    s = lax.axis_index("span")
    stator = lax.axis_index("row") == 0
    count = window_ref.shape[1]
    ghost, farther = window_ref[0], window_ref[1]
    tail = jnp.zeros((count - pitch - 2, LANES), F32)
    own = jnp.concatenate([beyond[0], face_ref[:pitch], beyond[1], tail], 0)
    top = jnp.zeros((1, LANES), F32)
    own_k1 = jnp.concatenate([top, face_ref[pitch : 2 * pitch], top, tail], 0)
    own_new = jnp.concatenate([top, new_rows, top, tail], 0)
    at = 2 * pitch

    def groups(row, g):
        out = row
        for f in range(planes):
            if f != g:
                out = jnp.where(iota(row.shape, 1) // SLAB == f, pltpu.roll(row, (f - g) * SLAB % LANES, 1), out)
        return out

    def speeds(rows):
        rows = TIME_STEP * rows
        return groups(rows[0:1], 0), groups(rows[1:2], 0), groups(rows[0:1], 1)

    sa0, sa1, sp0 = speeds(face_ref[at : at + 2])
    ga0, ga1, gp0 = speeds(window_ref[2, :2])
    shape = (count, LANES)
    lane = iota(shape, 1)
    group = lax.shift_right_logical(lane, power(SLAB))
    radius = lane & (SLAB - 1)

    def spread(x):
        out = x
        for f in range(nfield):
            out = jnp.where(group == f, pltpu.roll(x, (f + 1) * SLAB, 1), out)
        return out

    half = 0.5 * TIME_STEP
    k0, k1, g0, g1 = spread(own), spread(own_k1), spread(ghost), spread(farther)
    wall = ((radius == 7 + radial) & (s == nspan - 1)) | ((radius == 7) & (s == 0))

    def ahead(x):
        return pltpu.roll(x, count - 1, 0)

    def outward(x):
        return pltpu.roll(x, LANES - 1, 1)

    def change(v, k, speed):
        kappa = half * (k + ahead(k))
        up, dn = jnp.maximum(speed, 0.0), jnp.minimum(speed, 0.0)
        along = (up + kappa) * v + (dn - kappa) * ahead(v)
        kappa = jnp.where(wall, 0.0, half * (k + outward(k)))
        across = kappa * (v - outward(v))
        return along - pltpu.roll(along, 1, 0) + across - pltpu.roll(across, 1, 1)

    def face(first, second, speed, kappa):
        lower = jnp.where(stator, first, second)
        upper = jnp.where(stator, second, first)
        return (jnp.maximum(speed, 0.0) + kappa) * lower + (jnp.minimum(speed, 0.0) - kappa) * upper

    sign = jnp.where(stator, 1.0, -1.0)
    speed = 0.5 * (sa0 + ga0)
    kappa = half * (k0 + g0)
    flux = sign * face(own, ghost, speed, kappa)
    shift = -flux
    ghost_new = (
        ghost
        + flux
        - sign * face(ghost, farther, 0.5 * (ga0 + ga1), half * (g0 + g1))
        - change(ghost, g0, gp0)
    )
    flux = sign * face(own_new + shift, ghost_new, speed, kappa)
    inner = 0.5 * (sa0 + sa1)
    kappa = half * (k0 + k1)
    inner = sign * jnp.where(
        stator, jnp.minimum(inner, 0.0) - kappa, jnp.maximum(inner, 0.0) + kappa
    ) * shift
    add0 = shift - change(shift, k0, sp0) + inner - flux
    add1 = -inner
    return add0, add1


def column(stator, adds, i):
    row = iota((LANES, LANES), 0)
    near_row = jnp.where(stator, LANES - 1, 0)
    far_row = jnp.where(stator, LANES - 2, 1)
    far = jnp.where(row == far_row, adds[1][i + 1 : i + 2], 0.0)
    return jnp.where(row == near_row, adds[0][i + 1 : i + 2], far).T


def centre(npitch, nspan, mid_ref, face_ref, row_ref, buf_ref, tile_ref, arr_ref, window_ref, ring_s):
    nfield, inner, radial, axial = mid_ref.shape
    pitch = inner + 4
    q = lax.axis_index("row")
    stator = q == 0
    near_tile = pl.ds(pl.multiple_of((1 - q) * (axial - LANES), LANES), LANES)

    values = arr_ref.shape[0]
    capacity = arr_ref.shape[1] // npitch
    for p in range(npitch):
        coded = buf_ref[p, q].astype(F32)
        plain = jnp.where(coded > 0.0, jnp.log2(coded) * (1.0 / CODE), 0.0)
        for j in range(capacity // LANES):
            at = p * capacity + j * LANES
            arr_ref[:, at : at + LANES] = plain[j * values : (j + 1) * values]

    whole = npitch * pitch
    count = window_ref.shape[1]
    for p in range(npitch):
        both = buf_ref[p, 1 - q].astype(F32)
        ring_s[0, p * pitch : (p + 1) * pitch] = both[:pitch]
        ring_s[1, p * pitch : (p + 1) * pitch] = both[pitch : 2 * pitch]
        if p == 0:
            window_ref[2, :8] = both[2 * pitch : 2 * pitch + 8]
    for n in range(2):
        ring_s[n, whole : whole + pitch] = ring_s[n, :pitch]
        ring_s[n, whole + pitch :] = ring_s[n, pitch : count]
    begin = jnp.max(face_ref[2 * pitch + 2 : 2 * pitch + 3]).astype(jnp.int32) - 1
    begin = jnp.where(begin < 0, begin + whole, begin)
    window_ref[0] = ring_s[0, pl.ds(begin, count), :]
    window_ref[1] = ring_s[1, pl.ds(begin, count), :]
    blank = jnp.zeros((1, LANES), F32)
    adds = contribution(
        nspan, pitch, radial, face_ref, (blank, blank), row_ref[...], window_ref
    )
    for i in range(inner):
        block = column(stator, adds, i + 2)
        for f in range(nfield):
            at = f * SLAB + 8
            tile_ref[f, i] = mid_ref[f, i, :, near_tile] + block[at : at + radial]


def finish(
    nspan,
    mid_ref,
    tile_ref,
    arr_ref,
    f_ref,
    k_ref,
    speed_ref,
    halo_ref,
    lower_ref,
    upper_ref,
    y4_ref,
    row_ref,
    face_ref,
    window_ref,
    out_ref,
    arr_out,
    y_s,
    o_s,
    row_s,
    sems,
):
    nfield, pitch, radial, axial = f_ref.shape
    planes = nfield + 1
    stator = lax.axis_index("row") == 0
    q = lax.axis_index("row")
    near_tile = pl.ds(pl.multiple_of((1 - q) * (axial - LANES), LANES), LANES)
    copies = [
        pltpu.make_async_copy(arr_ref, arr_out, sems.at[2]),
        pltpu.make_async_copy(
            tile_ref, out_ref.at[:, 2 : pitch - 2, :, near_tile], sems.at[3]
        ),
    ]
    if axial > LANES:
        rest = pl.ds(pl.multiple_of(q * LANES, LANES), axial - LANES)
        copies.append(
            pltpu.make_async_copy(
                mid_ref.at[:, :, :, rest], out_ref.at[:, 2 : pitch - 2, :, rest], sems.at[4]
            )
        )
    for copy in copies:
        copy.start()
    faces = Faces(nspan, speed_ref, radial)
    ext = {-1: lower_ref[...].astype(F32), 1: upper_ref[...].astype(F32)}
    sub = iota((EXTRA, axial), 0)
    corner_at = 2 * planes * radial

    def state(f, i):
        if 0 <= i < pitch:
            core = f_ref[f, i] if f < nfield else k_ref[i]
            return jnp.concatenate([core, halo_ref[f * pitch + i]], 0)
        side = ext[-1 if i < 0 else 1]
        at = (2 * f + (i + 2 if i < 0 else i - pitch)) * radial
        extra = jnp.zeros((EXTRA, axial), F32)
        if i in (-1, pitch):
            corner = corner_at + 2 * f
            extra = jnp.where(sub == 0, side[corner : corner + 1], 0.0)
            extra = jnp.where(sub == 7, side[corner + 1 : corner + 2], extra)
        return jnp.concatenate([side[at : at + radial], extra], 0)

    row_s[...] = row_ref[...]
    beyond = []
    tile = pl.ds(pl.multiple_of(lax.axis_index("row") * (LANES - axial) + axial - LANES, LANES), LANES)

    def edge_lanes(value):
        return jnp.where(stator, value[:, axial - LANES :], value[:, :LANES])

    blank = jnp.zeros((SLAB, LANES), F32)
    held = {i: n for n, i in enumerate((1, 2, pitch - 3, pitch - 2))}
    for side, new, done in ((0, (-1, 0), (0, 1)), (1, (pitch - 1, pitch), (pitch - 2, pitch - 1))):
        touched = sorted({*new, *done})
        k = {i: state(nfield, i) for i in range(touched[0] - 1, touched[-1] + 2)}
        w = {i: faces.weights(k[i - 1], k[i], k[i + 1]) for i in touched}
        for f in range(nfield):
            x = {i: state(f, i) for i in range(new[0] - 1, new[1] + 2)}
            y = {i: y4_ref[f, held[i]] for i in held if done[0] - 1 <= i <= done[1] + 1}
            for i in new:
                y[i] = faces.step(w[i], x[i - 1], x[i], x[i + 1])
            for n, i in enumerate(done):
                o_s[f, 2 * side + n] = faces.step(w[i], y[i - 1], y[i], y[i + 1])[:radial]
            y_s[f] = y[0 if side == 0 else pitch - 1]
        parts = []
        for f in range(nfield):
            parts += slab(y_s[f, :radial, tile], y_s[f, radial:, tile])
        i = 0 if side == 0 else pitch - 1
        row_s[i : i + 1] = near(stator, parts + [blank])[0]
        parts = []
        for f in range(planes):
            value = edge_lanes(state(f, -1 if side == 0 else pitch))
            parts += slab(value[:radial], value[radial:])
        beyond.append(near(stator, parts)[0])
    adds = contribution(nspan, pitch, radial, face_ref, beyond, row_s[...], window_ref)
    for side in range(2):
        first = side * (pitch - 2)
        for n in range(2):
            block = column(stator, adds, first + n)
            for f in range(nfield):
                at = f * SLAB + 8
                o_s[f, 2 * side + n, :, tile] += block[at : at + radial]
        copies.append(
            pltpu.make_async_copy(
                o_s.at[:, 2 * side : 2 * side + 2], out_ref.at[:, first : first + 2], sems.at[side]
            )
        )
        copies[-1].start()
    for copy in copies:
        copy.wait()


def local(
    fields,
    diffusivity,
    mean_flow,
    radial_kernel,
    tracer_values,
    tracer_cells,
    tracer_dest,
    interface_map,
):
    npitch = lax.axis_size("pitch")
    nspan = lax.axis_size("span")
    nfield, pitch, radial, axial = fields.shape
    planes = nfield + 1
    values, tracers = tracer_values.shape
    chunks = tracers // LANES
    capacity = 2 * tracers // npitch
    edge = planes * pitch
    cells = tracer_cells.reshape(chunks, LANES)
    dest = tracer_dest.reshape(chunks, LANES)

    mean_rows = 2 * radial
    if nspan == 2:
        outs = [((mean_rows + edge // 2, axial), BF16), ((2 * edge, axial), BF16)]
    else:
        outs = [((2 * edge, axial), BF16)] * 2 + [((edge, LANES), BF16)] * 2
        outs += [((mean_rows, axial), BF16)]
    inputs = [fields, diffusivity, radial_kernel, tracer_values, cells, dest, interface_map, mean_flow]
    *packed, fields, diffusivity, radial_kernel, tracer_values, cells, dest, interface_map = call(
        lambda *refs: pack_span(nspan, len(inputs), *refs),
        outs + [(x.shape, x.dtype) for x in inputs[:-1]],
        [pltpu.with_memory_space_constraint(x, pltpu.HBM) for x in inputs],
        [HBM] * len(inputs),
        [
            pltpu.VMEM(mean_flow.shape, mean_flow.dtype),
            pltpu.SemaphoreType.DMA((len(inputs) + 2,)),
        ],
        nbytes=2**20,
        fixed=True,
    )
    if nspan == 2:
        swap = [(0, 1), (1, 0)]
        span_got = (packed[0], lax.ppermute(packed[0], "span", swap))
        low = high = lax.ppermute(packed[1], "span", swap)
    else:
        upward = [(n, n + 1) for n in range(nspan - 1)]
        downward = [(n + 1, n) for n in range(nspan - 1)]
        low, high = lax.ppermute(packed[0], "span", upward), lax.ppermute(packed[1], "span", downward)
        span_got = (
            lax.ppermute(packed[2], "span", upward),
            lax.ppermute(packed[3], "span", downward),
            lax.all_gather(packed[4], "span"),
        )

    width = min(2 * LANES, capacity)
    sampled = call(
        lambda *refs: sample_fields(npitch, *refs),
        [
            ((8, tracers), F32),
            ((width, tracers), BF16),
            ((1, tracers), jnp.int32),
            ((axial, tracers), BF16),
        ],
        (fields, cells, dest),
        [VMEM] * 3,
        [pltpu.VMEM((nfield, pitch * radial, axial), BF16)],
        flops=4 * nfield * pitch * radial * axial * tracers,
        nbytes=2**20,
    )

    rows = radial + EXTRA
    per_slot = max(values * capacity // LANES, 2 * pitch + 3)
    per_slot = -(-per_slot // 8) * 8
    halo_rows = 2 * planes * radial + 16
    buf, speeds, face = call(
        lambda *refs: dispatch(npitch, nspan, *refs),
        [
            ((npitch, 2, per_slot, LANES), BF16),
            ((2, rows, axial), F32),
            ((per_slot, LANES), F32),
        ],
        (
            fields,
            diffusivity,
            radial_kernel,
            tracer_values,
            cells,
            interface_map,
        )
        + tuple(sampled)
        + span_got,
        [VMEM] * (10 + len(span_got)),
        [
            pltpu.VMEM(radial_kernel.shape, F32),
            pltpu.VMEM((16, tracers), F32),
            pltpu.VMEM((values * npitch * capacity // width, tracers), BF16),
            pltpu.VMEM((values, npitch * capacity // width, width), F32),
            pltpu.VMEM((per_slot, LANES), F32),
            pltpu.VMEM((2, edge, LANES), F32),
        ],
        flops=2 * npitch * values * tracers * capacity,
        nbytes=2**21,
    )
    buf, halo, up, down = call(
        lambda *refs: halos(*refs[1:5], *refs[6:]),
        [((npitch, 2, per_slot, LANES), BF16), ((edge, EXTRA, axial), F32)]
        + [((halo_rows, axial), BF16)] * 2,
        (buf, low, high, fields, diffusivity),
        [ANY] + [VMEM] * 4,
        [pltpu.VMEM((2, 2 * edge, axial), F32)],
        nbytes=2**18,
        passed=(0,),
    )
    buf = lax.all_to_all(
        buf.reshape(npitch * 2, per_slot, LANES), ("pitch", "row"), 0, 0
    ).reshape(buf.shape)
    ring = [(n, (n + 1) % npitch) for n in range(npitch)]
    lower = lax.ppermute(up, "pitch", ring)
    upper = lax.ppermute(down, "pitch", [(b, a) for a, b in ring])

    mid, near_edge, new_rows = call(
        lambda *refs: middle(nspan, *refs),
        [
            ((nfield, pitch - 4, radial, axial), F32),
            ((nfield, 4, rows, axial), F32),
            ((pitch, LANES), F32),
        ],
        (fields, diffusivity, speeds, halo),
        [VMEM] * 4,
        [
            pltpu.VMEM((nfield, pitch, rows, axial), F32),
            pltpu.VMEM((7, pitch, rows, axial), F32),
        ],
        flops=2**24,
        nbytes=2**22,
    )
    near_mid, arrived, window = call(
        lambda *refs: centre(npitch, nspan, *refs),
        [
            ((nfield, pitch - 4, radial, LANES), F32),
            ((values, npitch * capacity), F32),
            ((3, pitch + 8, LANES), F32),
        ],
        (mid, face, new_rows, buf),
        [VMEM] * 4,
        [pltpu.VMEM((2, npitch * pitch + pitch + 8, LANES), F32)],
        flops=2**22,
        nbytes=2**21,
        fixed=True,
    )
    return call(
        lambda *refs: finish(nspan, *refs),
        [(fields.shape, F32), (arrived.shape, F32)],
        (
            mid,
            near_mid,
            arrived,
            fields,
            diffusivity,
            speeds,
            halo,
            lower,
            upper,
            near_edge,
            new_rows,
            face,
            window,
        ),
        [VMEM] * 13,
        [
            pltpu.VMEM((nfield, rows, axial), F32),
            pltpu.VMEM((nfield, 4, radial, axial), F32),
            pltpu.VMEM((pitch, LANES), F32),
            pltpu.SemaphoreType.DMA((5,)),
        ],
        flops=2**23,
        nbytes=2**21,
        place=ANY,
    )


def solution(mesh):
    placed = (
        P(None, "pitch", "span", "row"),
        P("pitch", "span", "row"),
        P("span", None, "row"),
        P(),
        P(None, ("pitch", "span", "row")),
        P(("pitch", "span", "row")),
        P(("pitch", "span", "row"), None),
        P("row", "pitch"),
    )
    return jax.shard_map(
        local,
        mesh=mesh,
        in_specs=placed,
        out_specs=(P(None, "pitch", "span", "row"), P(None, ("pitch", "span", "row"))),
        check_vma=False,
    )
```

```python
import jax
import jax.numpy as jnp
from jax import lax
from jax.experimental import pallas as pl
from jax.experimental.pallas import tpu as pltpu
from jax.sharding import PartitionSpec as P

SUB = 2
TIME_STEP = 0.9
AXIAL_SPEED = 0.15
PITCH_SPEED = 0.15
LANES = 128
EXTRA = 8
SLAB = 32
F32 = jnp.float32
BF16 = jnp.bfloat16
VMEM = pl.BlockSpec(memory_space=pltpu.VMEM)
ANY = pl.BlockSpec(memory_space=pl.ANY)
HBM = pl.BlockSpec(memory_space=pltpu.HBM)
CODE = 10.0
FINE = 18.0
VMEM_LIMIT = 48 * 1024 * 1024


def iota(shape, dim):
    return lax.broadcasted_iota(jnp.int32, shape, dim)


def split(x):
    high = x.astype(BF16)
    return high, (x - high.astype(F32)).astype(BF16)


def power(n):
    assert n & (n - 1) == 0
    return n.bit_length() - 1


def call(body, outs, args, specs, scratch=(), flops=0, nbytes=0, place=VMEM, fixed=False, passed=()):
    shape = pltpu.VMEM if fixed else jax.ShapeDtypeStruct
    passed = dict(passed)
    return pl.pallas_call(
        body,
        out_shape=tuple(shape(s, d) for s, d in outs),
        in_specs=list(specs),
        out_specs=place if isinstance(place, tuple) else (place,) * len(outs),
        input_output_aliases=passed,
        scratch_shapes=list(scratch),
        compiler_params=pltpu.CompilerParams(vmem_limit_bytes=VMEM_LIMIT),
        cost_estimate=pl.CostEstimate(flops=flops, bytes_accessed=nbytes, transcendentals=0),
    )(*args)


def pack_span(nspan, n_in, *refs):
    ins, rest = refs[:n_in], refs[n_in:]
    outs, kept, (m_s, sems) = rest[: -n_in - 1], rest[-n_in - 1 : -2], rest[-2:]
    f_ref, k_ref = kept[:2]
    radial, axial = f_ref.shape[2:]
    s = lax.axis_index("span")
    half = radial - 8
    early = [pltpu.make_async_copy(ins[-1], m_s, sems.at[0])]
    late = []
    for n, first, size in ((0, (1 - s) * half, 8), (1, s * 8, half)):
        rows = pl.ds(pl.multiple_of(first, 8), size)
        copies = [
            pltpu.make_async_copy(
                ins[0].at[:, :, rows, :], f_ref.at[:, :, rows, :], sems.at[1 + 2 * n]
            ),
            pltpu.make_async_copy(ins[1].at[:, rows, :], k_ref.at[:, rows, :], sems.at[2 + 2 * n]),
        ]
        if n == 0 or nspan > 2:
            early += copies
        else:
            late += copies
    for n in range(2, n_in - 1):
        late.append(pltpu.make_async_copy(ins[n], kept[n], sems.at[n + 3]))
    for copy in early + late:
        copy.start()
    for copy in early:
        copy.wait()

    def edge(first):
        parts = []
        for r in range(2):
            row = pl.ds(first + r, 1)
            parts += [f_ref[:, :, row, :].reshape(-1, axial), k_ref[:, row, :].reshape(-1, axial)]
        return jnp.concatenate(parts, 0).astype(BF16)

    flow = m_s[...].astype(F32)
    flow = jnp.concatenate([flow[:, 0, :], flow[:, 1, :]], 0).astype(BF16)
    def corner(layer):
        stator = lax.axis_index("row") == 0
        return jnp.where(stator, layer[:, axial - LANES :], layer[:, :LANES]).astype(BF16)

    if nspan == 2:
        packed = edge((1 - s) * (radial - 2))
        outs[1][...] = packed
        both = packed.astype(F32)
        half = both.shape[0] // 2
        near = corner(jnp.where(s == 0, both[half:], both[:half]))
        half = near.shape[0] // 2
        outs[0][: 2 * radial] = flow
        outs[0][2 * radial :, :LANES] = near[:half]
        outs[0][2 * radial :, LANES : 2 * LANES] = near[half:]
    else:
        top, bottom = edge(radial - 2), edge(0)
        half = top.shape[0] // 2
        outs[0][...] = top
        outs[1][...] = bottom
        outs[2][...] = corner(top[half:].astype(F32))
        outs[3][...] = corner(bottom[:half].astype(F32))
        outs[4][...] = flow
    for copy in late:
        copy.wait()


def tracer_chunk(ref, c):
    both = [ref[pl.ds(2 * c + n, 1), :] for n in range(2)]
    return jnp.concatenate(both, 1), pl.ds(pl.multiple_of(c * 2 * LANES, 2 * LANES), 2 * LANES)


def one_hot(rows, index):
    return (iota((rows, index.shape[1]), 0) == index).astype(F32).astype(BF16)


def sample_fields(npitch, f_ref, cell_ref, dest_ref, samp_ref, place_ref, key_ref, pick_ref, table_s):
    nfield, pitch, radial, axial = f_ref.shape
    lines = pitch * radial
    chunks = cell_ref.shape[0]

    @pl.loop(0, nfield, unroll=True)
    def _(f):
        table_s[f] = jnp.exp2(FINE * f_ref[f].reshape(lines, axial)).astype(BF16)

    table = table_s[...].reshape(nfield * lines, axial)
    samp_ref[...] = jnp.zeros(samp_ref.shape, F32)

    @pl.loop(0, chunks // 2, unroll=True)
    def _(c):
        cells, span = tracer_chunk(cell_ref, c)
        pick = one_hot(axial, cells & (axial - 1))
        pick_ref[:, span] = pick
        got = jnp.dot(table, pick, preferred_element_type=F32)
        mine = iota((lines, cells.shape[1]), 0) == lax.shift_right_logical(cells, power(axial))
        for f in range(nfield):
            part = jnp.where(mine, got[f * lines : (f + 1) * lines], 0.0)
            part = jnp.sum(part, 0, keepdims=True)
            samp_ref[f : f + 1, span] = jnp.log2(part) * (1.0 / FINE)

    ones = []
    for c in range(chunks):
        ones.append((iota((npitch, LANES), 0) == dest_ref[c : c + 1, :]).astype(F32))
    stacked = jnp.concatenate(ones, 0)
    before = (iota((LANES, LANES), 0) < iota((LANES, LANES), 1)).astype(F32).astype(BF16)
    prefix = jnp.dot(stacked.astype(BF16), before, preferred_element_type=F32)
    carry = jnp.zeros((npitch, 1), F32)
    for c in range(chunks):
        rank = prefix[c * npitch : (c + 1) * npitch] + carry
        slot = jnp.sum(rank * ones[c], 0, keepdims=True).astype(jnp.int32)
        span = slice(c * LANES, (c + 1) * LANES)
        width = place_ref.shape[0]
        place_ref[:, span] = one_hot(width, slot & (width - 1))
        groups = 2 * chunks * LANES // npitch // width
        key_ref[:, span] = dest_ref[c : c + 1, :] * groups + lax.shift_right_logical(slot, power(width))
        carry = carry + jnp.sum(ones[c], 1, keepdims=True)


def slab(core, extra):
    return [extra, core, extra]


def near(stator, parts):
    turned = jnp.concatenate(parts, 0).T
    return (
        jnp.where(stator, turned[LANES - 1 : LANES], turned[0:1]),
        jnp.where(stator, turned[LANES - 2 : LANES - 1], turned[1:2]),
    )


def dispatch(
    npitch,
    nspan,
    f_ref,
    k_ref,
    kern_ref,
    tv_ref,
    cell_ref,
    map_ref,
    samp_ref,
    place_ref,
    key_ref,
    pick_ref,
    *refs,
):
    nfield, pitch, radial, axial = f_ref.shape
    planes = nfield + 1
    edge = planes * pitch
    if nspan == 2:
        sent_ref, got_ref = refs[:2]
        refs = refs[2:]
    else:
        low_ref, high_ref, all_ref = refs[:3]
        refs = refs[3:]
    buf_ref, speed_ref, face_ref, kern_s, upd_s, lhs_s, acc_s, face_s, near_s = refs
    s = lax.axis_index("span")
    q = lax.axis_index("row")

    total = kern_ref.shape[0]
    kern_s[...] = kern_ref[...].astype(F32)
    main = kern_s[pl.ds(pl.multiple_of(s * radial, 8), radial), :]
    above = kern_s[pl.ds(pl.multiple_of(jnp.minimum((s + 1) * radial, total - 8), 8), 8), :]
    below = kern_s[pl.ds(pl.multiple_of(jnp.maximum(s * radial - 8, 0), 8), 8), :]
    wide = jnp.concatenate([main, jnp.where(iota((EXTRA, total), 0) < 4, above, below)], 0).astype(BF16)
    smoothed = []
    for c in range(2):
        if nspan == 2:
            at = slice(c * radial, (c + 1) * radial)
            own, other = sent_ref[at, :].astype(F32), got_ref[at, :].astype(F32)
            rows = [jnp.where(s == 0, own, other), jnp.where(s == 0, other, own)]
        else:
            rows = [all_ref[n, c * radial : (c + 1) * radial, :].astype(F32) for n in range(nspan)]
        smoothed.append(
            jnp.dot(wide, jnp.concatenate(rows, 0).astype(BF16), preferred_element_type=F32)
        )
    sa = AXIAL_SPEED * (1.0 + 0.5 * jnp.tanh(smoothed[0]))
    sp = PITCH_SPEED * jnp.tanh(smoothed[1])
    speed_ref[0] = sa
    speed_ref[1] = sp

    chunks = cell_ref.shape[0]
    values, tracers = tv_ref.shape
    capacity = 2 * tracers // npitch
    count = nfield + 2
    table = jnp.concatenate(split(jnp.concatenate([sa[:radial], sp[:radial]], 0)), 0)

    @pl.loop(0, chunks // 2, unroll=True)
    def _(c):
        cells, span = tracer_chunk(cell_ref, c)
        line = lax.shift_right_logical(cells, power(axial)) & (radial - 1)
        got = jnp.dot(table, pick_ref[:, span], preferred_element_type=F32)
        got = got[: 2 * radial] + got[2 * radial :]
        mine = iota((radial, cells.shape[1]), 0) == line
        sampled = [samp_ref[f : f + 1, span] for f in range(nfield)]
        for n in range(2):
            part = jnp.where(mine, got[n * radial : (n + 1) * radial], 0.0)
            sampled.append(jnp.sum(part, 0, keepdims=True))
        for v, value in enumerate(sampled):
            head = tv_ref[v : v + 1, span]
            upd_s[v : v + 1, span] = head + 0.5 * (value - head)
            upd_s[count + v : count + v + 1, span] = tv_ref[count + v : count + v + 1, span] + 0.8 * value

    width = place_ref.shape[0]
    groups = capacity // width
    keys = npitch * groups
    coded = jnp.exp2(CODE * upd_s[:values])
    mine = iota((keys, tracers), 0) == key_ref[...]
    for v in range(values):
        lhs_s[v * keys : (v + 1) * keys, :] = jnp.where(mine, coded[v : v + 1], 0.0).astype(BF16)
    acc_s[...] = lax.dot_general(
        lhs_s[...], place_ref[...], (((1,), (1,)), ((), ())), preferred_element_type=F32
    ).reshape(acc_s.shape)
    room = buf_ref.shape[2] - values * capacity // LANES
    filler = [jnp.zeros((room, LANES), F32)] if room else []
    for d in range(npitch):
        pieces = []
        for g in range(groups):
            for n in range(width // LANES):
                pieces.append(acc_s[:, d * groups + g, n * LANES : (n + 1) * LANES])
        buf_ref[d, q] = jnp.concatenate(pieces + filler, 0).astype(BF16)

    if nspan == 2:
        near_s[0, : edge // 2] = got_ref[2 * radial :, :LANES].astype(F32)
        near_s[0, edge // 2 :] = got_ref[2 * radial :, LANES : 2 * LANES].astype(F32)
        near_s[1] = near_s[0]
    else:
        near_s[0] = high_ref[...].astype(F32)
        near_s[1] = low_ref[...].astype(F32)
    sub = iota((EXTRA, LANES), 0)

    def beside(n):
        return jnp.where(
            sub == 0, near_s[0, n : n + 1], jnp.where(sub == 7, near_s[1, n : n + 1], 0.0)
        )

    stator = q == 0
    tile = pl.ds(pl.multiple_of((1 - q) * (axial - LANES), LANES), LANES)
    face_s[...] = jnp.zeros(face_s.shape, F32)

    for i in range(pitch):
        parts = []
        for f in range(planes):
            core = f_ref[f, i, :, tile] if f < nfield else k_ref[i, :, tile]
            parts += slab(core, beside(f * pitch + i))
        first, second = near(stator, parts)
        face_s[i : i + 1] = first
        face_s[pitch + i : pitch + i + 1] = second

    parts = []
    for n in range(2):
        speed = speed_ref[n, :, tile]
        parts += slab(speed[:radial], speed[radial:])
    first, second = near(stator, parts + [jnp.zeros((LANES - 2 * SLAB, LANES), F32)])
    face_s[2 * pitch : 2 * pitch + 1] = first
    face_s[2 * pitch + 1 : 2 * pitch + 2] = second
    face = face_s[...]
    face_ref[...] = face
    offset = map_ref[...].astype(F32)
    face_ref[2 * pitch + 2 : 2 * pitch + 3] = jnp.broadcast_to(offset[:, :1], (1, LANES))
    face = face.astype(BF16)

    @pl.loop(0, npitch, unroll=True)
    def _(d):
        buf_ref[d, 1 - q] = face


def halos(low_ref, high_ref, f_ref, k_ref, halo_ref, up_ref, down_ref, near_s):
    nfield, pitch, radial, axial = f_ref.shape
    planes = nfield + 1
    edge = planes * pitch
    sub = iota((EXTRA, axial), 0)
    near_s[0] = high_ref[: 2 * edge].astype(F32)
    near_s[1] = low_ref[: 2 * edge].astype(F32)

    @pl.loop(0, edge, unroll=True)
    def _(n):
        tile = jnp.where(sub == 0, near_s[0, pl.ds(n, 1), :], 0.0)
        tile = jnp.where(sub == 1, near_s[0, pl.ds(edge + n, 1), :], tile)
        tile = jnp.where(sub == 6, near_s[1, pl.ds(n, 1), :], tile)
        halo_ref[n] = jnp.where(sub == 7, near_s[1, pl.ds(edge + n, 1), :], tile)

    def layers(ref, top):
        rows = []
        for f in range(planes):
            for n in range(2):
                i = top * (pitch - 2) + n
                rows.append(f_ref[f, i] if f < nfield else k_ref[i])
        for f in range(planes):
            corner = halo_ref[f * pitch + top * (pitch - 1)]
            rows += [corner[0:1], corner[7:8]]
        rows.append(jnp.zeros((8, axial), F32))
        ref[...] = jnp.concatenate(rows, 0).astype(BF16)

    layers(up_ref, 1)
    layers(down_ref, 0)


class Faces:
    def __init__(self, nspan, speed_ref, radial):
        self.rows, self.lanes = speed_ref.shape[1:]
        shape = (self.rows, self.lanes)
        s = lax.axis_index("span")
        stator = lax.axis_index("row") == 0
        lane, radius = iota(shape, 1), iota(shape, 0)
        sa = TIME_STEP * speed_ref[0]
        sp = TIME_STEP * speed_ref[1]
        wa = 0.5 * (sa + pltpu.roll(sa, self.lanes - 1, 1))
        self.first, self.last = lane == 0, lane == self.lanes - 1
        up, dn = jnp.maximum(wa, 0.0), jnp.minimum(wa, 0.0)
        self.axial = (
            jnp.where(self.last, 0.0, up),
            jnp.where(self.last, 0.0, dn),
            pltpu.roll(jnp.where(self.last, 0.0, up), 1, 1),
            pltpu.roll(jnp.where(self.last, 0.0, dn), 1, 1),
        )
        self.pitch_up, self.pitch_dn = jnp.maximum(sp, 0.0), jnp.minimum(sp, 0.0)
        top, bottom = s == nspan - 1, s == 0
        end = self.rows - 1
        self.wall_up = ((radius == radial - 1) & top) | ((radius == end) & bottom)
        self.wall_dn = ((radius == radial) & top) | ((radius == 0) & bottom)
        inlet = jnp.where(stator & self.first, sa, 0.0)
        keep = 1.0 + inlet - jnp.where(jnp.logical_not(stator) & self.last, sa, 0.0)
        self.keep = keep - self.axial[0] + self.axial[3] - self.pitch_up + self.pitch_dn

    def weights(self, k_before, k, k_after):
        half = 0.5 * TIME_STEP
        k = half * k
        k_up = jnp.where(self.last, 0.0, k + pltpu.roll(k, self.lanes - 1, 1))
        k_dn = jnp.where(self.first, 0.0, k + pltpu.roll(k, 1, 1))
        r_up = jnp.where(self.wall_up, 0.0, k + pltpu.roll(k, self.rows - 1, 0))
        r_dn = jnp.where(self.wall_dn, 0.0, k + pltpu.roll(k, 1, 0))
        p_up, p_dn = k + half * k_after, k + half * k_before
        return (
            self.keep - (k_up + k_dn) - (r_up + r_dn) - (p_up + p_dn),
            k_up - self.axial[1],
            k_dn + self.axial[2],
            r_up,
            r_dn,
            p_up - self.pitch_dn,
            p_dn + self.pitch_up,
        )

    def step(self, w, before, v, after):
        a = w[0] * v + w[1] * pltpu.roll(v, self.lanes - 1, 1)
        b = w[2] * pltpu.roll(v, 1, 1) + w[3] * pltpu.roll(v, self.rows - 1, 0)
        c = w[4] * pltpu.roll(v, 1, 0) + w[5] * after
        return (a + b) + (c + w[6] * before)


def middle(nspan, f_ref, k_ref, speed_ref, halo_ref, out_ref, o_ref, y2_ref, part_ref, outer_ref, row_ref, y_s, w_s, sem):
    nfield, pitch, radial, axial = f_ref.shape
    stator = lax.axis_index("row") == 0
    faces = Faces(nspan, speed_ref, radial)

    def state(f, i):
        return jnp.concatenate([f_ref[f, i], halo_ref[f * pitch + i]], 0)

    def kappa(i):
        return jnp.concatenate([k_ref[i], halo_ref[nfield * pitch + i]], 0)

    @pl.loop(1, pitch - 1, unroll=True)
    def _(i):
        w = faces.weights(kappa(i - 1), kappa(i), kappa(i + 1))
        for n, value in enumerate(w):
            w_s[n, i] = value
        for f in range(nfield):
            y_s[f, i] = faces.step(w, state(f, i - 1), state(f, i), state(f, i + 1))

    @pl.loop(2, pitch - 2, unroll=True)
    def _(i):
        w = [w_s[n, i] for n in range(7)]
        for f in range(nfield):
            o_ref[f, i - 2] = faces.step(w, y_s[f, i - 1], y_s[f, i], y_s[f, i + 1])[:radial]

    copies = []
    if axial > LANES:
        rest = pl.ds(pl.multiple_of(lax.axis_index("row") * LANES, LANES), axial - LANES)
        copies.append(
            pltpu.make_async_copy(
                o_ref.at[:, :, :, rest], out_ref.at[:, 2 : pitch - 2, :, rest], sem.at[0]
            )
        )
        copies[-1].start()
    k = [kappa(i) for i in (0, 1, pitch - 2, pitch - 1)]
    ends = faces.weights(-k[0], k[0], k[1]), faces.weights(k[2], k[3], -k[3])
    for n, value in enumerate(ends[0]):
        outer_ref[0, n] = value
    for n, value in enumerate(ends[1]):
        outer_ref[1, n] = value
    outer_ref[0, 7] = w_s[6, 1]
    outer_ref[1, 7] = w_s[5, pitch - 2]
    none = jnp.zeros((faces.rows, axial), F32)
    inner = [[w_s[n, i] for n in range(7)] for i in (1, pitch - 2)]
    for f in range(nfield):
        y2_ref[f, 0], y2_ref[f, 1] = y_s[f, 1], y_s[f, pitch - 2]
        part_ref[f, 0] = faces.step(ends[0], none, state(f, 0), state(f, 1))
        part_ref[f, 1] = faces.step(ends[1], state(f, pitch - 2), state(f, pitch - 1), none)
        part_ref[f, 2, :radial] = faces.step(inner[0], none, y_s[f, 1], y_s[f, 2])[:radial]
        part_ref[f, 3, :radial] = faces.step(inner[1], y_s[f, pitch - 3], y_s[f, pitch - 2], none)[:radial]
    row_ref[...] = jnp.zeros(row_ref.shape, F32)
    q = lax.axis_index("row")
    tile = pl.ds(pl.multiple_of((1 - q) * (axial - LANES), LANES), LANES)
    blank = jnp.zeros((SLAB, LANES), F32)

    @pl.loop(1, pitch - 1, unroll=True)
    def _(i):
        parts = []
        for f in range(nfield):
            parts += slab(y_s[f, i, :radial, tile], y_s[f, i, radial:, tile])
        row_ref[pl.ds(i, 1), :] = near(stator, parts + [blank])[0]

    for copy in copies:
        copy.wait()


def contribution(nspan, pitch, radial, face_ref, beyond, new_rows, window_ref):
    planes = LANES // SLAB
    nfield = planes - 1
    s = lax.axis_index("span")
    stator = lax.axis_index("row") == 0
    count = window_ref.shape[1]
    ghost, farther = window_ref[0], window_ref[1]
    tail = jnp.zeros((count - pitch - 2, LANES), F32)
    own = jnp.concatenate([beyond[0], face_ref[:pitch], beyond[1], tail], 0)
    top = jnp.zeros((1, LANES), F32)
    own_k1 = jnp.concatenate([top, face_ref[pitch : 2 * pitch], top, tail], 0)
    own_new = jnp.concatenate([top, new_rows, top, tail], 0)
    at = 2 * pitch

    def groups(row, g):
        out = row
        for f in range(planes):
            if f != g:
                out = jnp.where(iota(row.shape, 1) // SLAB == f, pltpu.roll(row, (f - g) * SLAB % LANES, 1), out)
        return out

    def speeds(rows):
        rows = TIME_STEP * rows
        return groups(rows[0:1], 0), groups(rows[1:2], 0), groups(rows[0:1], 1)

    sa0, sa1, sp0 = speeds(face_ref[at : at + 2])
    ga0, ga1, gp0 = speeds(window_ref[2, :2])
    shape = (count, LANES)
    lane = iota(shape, 1)
    group = lax.shift_right_logical(lane, power(SLAB))
    radius = lane & (SLAB - 1)

    def spread(x):
        out = x
        for f in range(nfield):
            out = jnp.where(group == f, pltpu.roll(x, (f + 1) * SLAB, 1), out)
        return out

    half = 0.5 * TIME_STEP
    k0, k1, g0, g1 = spread(own), spread(own_k1), spread(ghost), spread(farther)
    wall = ((radius == 7 + radial) & (s == nspan - 1)) | ((radius == 7) & (s == 0))

    def ahead(x):
        return pltpu.roll(x, count - 1, 0)

    def outward(x):
        return pltpu.roll(x, LANES - 1, 1)

    def change(v, k, speed):
        kappa = half * (k + ahead(k))
        up, dn = jnp.maximum(speed, 0.0), jnp.minimum(speed, 0.0)
        along = (up + kappa) * v + (dn - kappa) * ahead(v)
        kappa = jnp.where(wall, 0.0, half * (k + outward(k)))
        across = kappa * (v - outward(v))
        return along - pltpu.roll(along, 1, 0) + across - pltpu.roll(across, 1, 1)

    def face(first, second, speed, kappa):
        lower = jnp.where(stator, first, second)
        upper = jnp.where(stator, second, first)
        return (jnp.maximum(speed, 0.0) + kappa) * lower + (jnp.minimum(speed, 0.0) - kappa) * upper

    sign = jnp.where(stator, 1.0, -1.0)
    speed = 0.5 * (sa0 + ga0)
    kappa = half * (k0 + g0)
    flux = sign * face(own, ghost, speed, kappa)
    shift = -flux
    ghost_new = (
        ghost
        + flux
        - sign * face(ghost, farther, 0.5 * (ga0 + ga1), half * (g0 + g1))
        - change(ghost, g0, gp0)
    )
    flux = sign * face(own_new + shift, ghost_new, speed, kappa)
    inner = 0.5 * (sa0 + sa1)
    kappa = half * (k0 + k1)
    inner = sign * jnp.where(
        stator, jnp.minimum(inner, 0.0) - kappa, jnp.maximum(inner, 0.0) + kappa
    ) * shift
    add0 = shift - change(shift, k0, sp0) + inner - flux
    add1 = -inner
    return add0, add1


def column(stator, adds, i):
    row = iota((LANES, LANES), 0)
    near_row = jnp.where(stator, LANES - 1, 0)
    far_row = jnp.where(stator, LANES - 2, 1)
    far = jnp.where(row == far_row, adds[1][i + 1 : i + 2], 0.0)
    return jnp.where(row == near_row, adds[0][i + 1 : i + 2], far).T


def centre(npitch, nspan, mid_ref, face_ref, row_ref, buf_ref, tile_ref, arr_out, window_ref, ring_s, arr_ref, sem):
    nfield, inner, radial, axial = mid_ref.shape
    pitch = inner + 4
    q = lax.axis_index("row")
    stator = q == 0
    near_tile = pl.ds(pl.multiple_of((1 - q) * (axial - LANES), LANES), LANES)

    values = arr_ref.shape[0]
    capacity = arr_ref.shape[1] // npitch
    for p in range(npitch):
        coded = buf_ref[p, q].astype(F32)
        plain = jnp.where(coded > 0.0, jnp.log2(coded) * (1.0 / CODE), 0.0)
        for j in range(capacity // LANES):
            at = p * capacity + j * LANES
            arr_ref[:, at : at + LANES] = plain[j * values : (j + 1) * values]

    copy = pltpu.make_async_copy(arr_ref, arr_out, sem.at[0])
    copy.start()

    whole = npitch * pitch
    count = window_ref.shape[1]
    for p in range(npitch):
        both = buf_ref[p, 1 - q].astype(F32)
        ring_s[0, p * pitch : (p + 1) * pitch] = both[:pitch]
        ring_s[1, p * pitch : (p + 1) * pitch] = both[pitch : 2 * pitch]
        if p == 0:
            window_ref[2, :8] = both[2 * pitch : 2 * pitch + 8]
    for n in range(2):
        ring_s[n, whole : whole + pitch] = ring_s[n, :pitch]
        ring_s[n, whole + pitch :] = ring_s[n, pitch : count]
    begin = jnp.max(face_ref[2 * pitch + 2 : 2 * pitch + 3]).astype(jnp.int32) - 1
    begin = jnp.where(begin < 0, begin + whole, begin)
    window_ref[0] = ring_s[0, pl.ds(begin, count), :]
    window_ref[1] = ring_s[1, pl.ds(begin, count), :]
    blank = jnp.zeros((1, LANES), F32)
    adds = contribution(
        nspan, pitch, radial, face_ref, (blank, blank), row_ref[...], window_ref
    )
    for i in range(inner):
        block = column(stator, adds, i + 2)
        for f in range(nfield):
            at = f * SLAB + 8
            tile_ref[f, i] = mid_ref[f, i, :, near_tile] + block[at : at + radial]
    copy.wait()


def finish(
    nspan,
    _,
    tile_ref,
    f_ref,
    k_ref,
    speed_ref,
    halo_ref,
    lower_ref,
    upper_ref,
    y2_ref,
    part_ref,
    outer_ref,
    row_ref,
    face_ref,
    window_ref,
    out_ref,
    o_s,
    sems,
):
    nfield, pitch, radial, axial = f_ref.shape
    planes = nfield + 1
    stator = lax.axis_index("row") == 0
    q = lax.axis_index("row")
    near_tile = pl.ds(pl.multiple_of((1 - q) * (axial - LANES), LANES), LANES)
    copies = [
        pltpu.make_async_copy(
            tile_ref, out_ref.at[:, 2 : pitch - 2, :, near_tile], sems.at[2]
        )
    ]
    for copy in copies:
        copy.start()
    faces = Faces(nspan, speed_ref, radial)
    ext = {-1: lower_ref[...].astype(F32), 1: upper_ref[...].astype(F32)}
    sub = iota((EXTRA, axial), 0)
    corner_at = 2 * planes * radial

    def state(f, i):
        if 0 <= i < pitch:
            core = f_ref[f, i] if f < nfield else k_ref[i]
            return jnp.concatenate([core, halo_ref[f * pitch + i]], 0)
        side = ext[-1 if i < 0 else 1]
        at = (2 * f + (i + 2 if i < 0 else i - pitch)) * radial
        extra = jnp.zeros((EXTRA, axial), F32)
        if i in (-1, pitch):
            corner = corner_at + 2 * f
            extra = jnp.where(sub == 0, side[corner : corner + 1], 0.0)
            extra = jnp.where(sub == 7, side[corner + 1 : corner + 2], extra)
        return jnp.concatenate([side[at : at + radial], extra], 0)

    beyond, ends, results = [], [], {}

    def edge_lanes(value):
        return jnp.where(stator, value[:, axial - LANES :], value[:, :LANES])

    blank = jnp.zeros((SLAB, LANES), F32)
    for side in range(2):
        inside, outside, beyond_it = ((0, -1, -2), (pitch - 1, pitch, pitch + 1))[side]

        def ordered(far, centre, near):
            return (far, centre, near) if side == 0 else (near, centre, far)

        k_in, k_out = state(nfield, inside), state(nfield, outside)
        w_out = faces.weights(*ordered(state(nfield, beyond_it), k_out, k_in))
        kappa = 0.5 * TIME_STEP * (k_in + k_out)
        w_in = [outer_ref[side, n] for n in range(7)]
        w_in[0] = w_in[0] - kappa
        w_in[6 - side] = w_in[6 - side] + kappa
        wind = faces.pitch_up if side == 0 else -faces.pitch_dn
        updated = []
        for f in range(nfield):
            x_in, x_out = state(f, inside), state(f, outside)
            y_out = faces.step(w_out, *ordered(state(f, beyond_it), x_out, x_in))
            y_in = part_ref[f, side] + kappa * (x_out - x_in) + wind * x_out
            new_in = faces.step(w_in, *ordered(y_out, y_in, y2_ref[f, side]))[:radial]
            new_next = part_ref[f, 2 + side, :radial] + (outer_ref[side, 7] * y_in)[:radial]
            results[f, 3 * side] = new_in
            results[f, 1 + side] = new_next
            value = edge_lanes(y_in)
            updated += slab(value[:radial], value[radial:])
        ends.append(near(stator, updated + [blank])[0])
        parts = []
        for f in range(planes):
            value = edge_lanes(state(f, -1 if side == 0 else pitch))
            parts += slab(value[:radial], value[radial:])
        beyond.append(near(stator, parts)[0])
    rows = row_ref[...]
    index = iota(rows.shape, 0)
    rows = jnp.where(index == 0, ends[0], jnp.where(index == pitch - 1, ends[1], rows))
    adds = contribution(nspan, pitch, radial, face_ref, beyond, rows, window_ref)
    none = jnp.zeros((radial, axial - LANES), F32)
    for side in range(2):
        first = side * (pitch - 2)
        for n in range(2):
            block = column(stator, adds, first + n)
            for f in range(nfield):
                add = block[f * SLAB + 8 : f * SLAB + 8 + radial]
                add = jnp.where(
                    stator, jnp.concatenate([none, add], 1), jnp.concatenate([add, none], 1)
                )
                o_s[f, 2 * side + n] = results[f, 2 * side + n] + add
        copies.append(
            pltpu.make_async_copy(
                o_s.at[:, 2 * side : 2 * side + 2], out_ref.at[:, first : first + 2], sems.at[side]
            )
        )
        copies[-1].start()
    for copy in copies:
        copy.wait()


def local(
    fields,
    diffusivity,
    mean_flow,
    radial_kernel,
    tracer_values,
    tracer_cells,
    tracer_dest,
    interface_map,
):
    npitch = lax.axis_size("pitch")
    nspan = lax.axis_size("span")
    nfield, pitch, radial, axial = fields.shape
    planes = nfield + 1
    values, tracers = tracer_values.shape
    chunks = tracers // LANES
    capacity = 2 * tracers // npitch
    edge = planes * pitch
    cells = tracer_cells.reshape(chunks, LANES)
    dest = tracer_dest.reshape(chunks, LANES)

    mean_rows = 2 * radial
    if nspan == 2:
        outs = [((mean_rows + edge // 2, axial), BF16), ((2 * edge, axial), BF16)]
    else:
        outs = [((2 * edge, axial), BF16)] * 2 + [((edge, LANES), BF16)] * 2
        outs += [((mean_rows, axial), BF16)]
    inputs = [fields, diffusivity, radial_kernel, tracer_values, cells, dest, interface_map, mean_flow]
    *packed, fields, diffusivity, radial_kernel, tracer_values, cells, dest, interface_map = call(
        lambda *refs: pack_span(nspan, len(inputs), *refs),
        outs + [(x.shape, x.dtype) for x in inputs[:-1]],
        [pltpu.with_memory_space_constraint(x, pltpu.HBM) for x in inputs],
        [HBM] * len(inputs),
        [
            pltpu.VMEM(mean_flow.shape, mean_flow.dtype),
            pltpu.SemaphoreType.DMA((len(inputs) + 2,)),
        ],
        nbytes=2**20,
        fixed=True,
    )
    if nspan == 2:
        swap = [(0, 1), (1, 0)]
        span_got = (packed[0], lax.ppermute(packed[0], "span", swap))
        low = high = lax.ppermute(packed[1], "span", swap)
    else:
        upward = [(n, n + 1) for n in range(nspan - 1)]
        downward = [(n + 1, n) for n in range(nspan - 1)]
        low, high = lax.ppermute(packed[0], "span", upward), lax.ppermute(packed[1], "span", downward)
        span_got = (
            lax.ppermute(packed[2], "span", upward),
            lax.ppermute(packed[3], "span", downward),
            lax.all_gather(packed[4], "span"),
        )

    width = min(2 * LANES, capacity)
    sampled = call(
        lambda *refs: sample_fields(npitch, *refs),
        [
            ((8, tracers), F32),
            ((width, tracers), BF16),
            ((1, tracers), jnp.int32),
            ((axial, tracers), BF16),
        ],
        (fields, cells, dest),
        [VMEM] * 3,
        [pltpu.VMEM((nfield, pitch * radial, axial), BF16)],
        flops=4 * nfield * pitch * radial * axial * tracers,
        nbytes=2**20,
    )

    rows = radial + EXTRA
    per_slot = max(values * capacity // LANES, 2 * pitch + 3)
    per_slot = -(-per_slot // 8) * 8
    halo_rows = 2 * planes * radial + 16
    buf, speeds, face = call(
        lambda *refs: dispatch(npitch, nspan, *refs),
        [
            ((npitch, 2, per_slot, LANES), BF16),
            ((2, rows, axial), F32),
            ((per_slot, LANES), F32),
        ],
        (
            fields,
            diffusivity,
            radial_kernel,
            tracer_values,
            cells,
            interface_map,
        )
        + tuple(sampled)
        + span_got,
        [VMEM] * (10 + len(span_got)),
        [
            pltpu.VMEM(radial_kernel.shape, F32),
            pltpu.VMEM((16, tracers), F32),
            pltpu.VMEM((values * npitch * capacity // width, tracers), BF16),
            pltpu.VMEM((values, npitch * capacity // width, width), F32),
            pltpu.VMEM((per_slot, LANES), F32),
            pltpu.VMEM((2, edge, LANES), F32),
        ],
        flops=2 * npitch * values * tracers * capacity,
        nbytes=2**21,
    )
    buf, halo, up, down = call(
        lambda *refs: halos(*refs[1:5], *refs[6:]),
        [((npitch, 2, per_slot, LANES), BF16), ((edge, EXTRA, axial), F32)]
        + [((halo_rows, axial), BF16)] * 2,
        (buf, low, high, fields, diffusivity),
        [ANY] + [VMEM] * 4,
        [pltpu.VMEM((2, 2 * edge, axial), F32)],
        nbytes=2**18,
        place=(ANY, VMEM, VMEM, VMEM),
        passed={0: 0},
    )
    buf = lax.all_to_all(
        buf.reshape(npitch * 2, per_slot, LANES), ("pitch", "row"), 0, 0
    ).reshape(buf.shape)
    ring = [(n, (n + 1) % npitch) for n in range(npitch)]
    lower = lax.ppermute(up, "pitch", ring)
    upper = lax.ppermute(down, "pitch", [(b, a) for a, b in ring])

    moved, mid, near_edge, part, outer, new_rows = call(
        lambda *refs: middle(nspan, *refs),
        [
            (fields.shape, F32),
            ((nfield, pitch - 4, radial, axial), F32),
            ((nfield, 2, rows, axial), F32),
            ((nfield, 4, rows, axial), F32),
            ((2, 8, rows, axial), F32),
            ((pitch, LANES), F32),
        ],
        (fields, diffusivity, speeds, halo),
        [VMEM] * 4,
        [
            pltpu.VMEM((nfield, pitch, rows, axial), F32),
            pltpu.VMEM((7, pitch, rows, axial), F32),
            pltpu.SemaphoreType.DMA((1,)),
        ],
        flops=2**24,
        nbytes=2**22,
        place=(ANY,) + (VMEM,) * 5,
    )
    near_mid, arrived, window = call(
        lambda *refs: centre(npitch, nspan, *refs),
        [
            ((nfield, pitch - 4, radial, LANES), F32),
            ((values, npitch * capacity), F32),
            ((3, pitch + 8, LANES), F32),
        ],
        (mid, face, new_rows, buf),
        [VMEM] * 4,
        [
            pltpu.VMEM((2, npitch * pitch + pitch + 8, LANES), F32),
            pltpu.VMEM((values, npitch * capacity), F32),
            pltpu.SemaphoreType.DMA((1,)),
        ],
        flops=2**22,
        nbytes=2**21,
        place=(VMEM, ANY, VMEM),
    )
    (moved,) = call(
        lambda *refs: finish(nspan, *refs),
        [(fields.shape, F32)],
        (
            moved,
            near_mid,
            fields,
            diffusivity,
            speeds,
            halo,
            lower,
            upper,
            near_edge,
            part,
            outer,
            new_rows,
            face,
            window,
        ),
        [ANY] + [VMEM] * 13,
        [
            pltpu.VMEM((nfield, 4, radial, axial), F32),
            pltpu.SemaphoreType.DMA((3,)),
        ],
        flops=2**23,
        nbytes=2**21,
        place=ANY,
        passed={0: 0},
    )
    return moved, arrived


def solution(mesh):
    placed = (
        P(None, "pitch", "span", "row"),
        P("pitch", "span", "row"),
        P("span", None, "row"),
        P(),
        P(None, ("pitch", "span", "row")),
        P(("pitch", "span", "row")),
        P(("pitch", "span", "row"), None),
        P("row", "pitch"),
    )
    return jax.shard_map(
        local,
        mesh=mesh,
        in_specs=placed,
        out_specs=(P(None, "pitch", "span", "row"), P(None, ("pitch", "span", "row"))),
        check_vma=False,
    )
```

```python
import jax
import jax.numpy as jnp
from jax import lax
from jax.experimental import pallas as pl
from jax.experimental.pallas import tpu as pltpu
from jax.sharding import PartitionSpec as P

SUB = 2
TIME_STEP = 0.9
AXIAL_SPEED = 0.15
PITCH_SPEED = 0.15
LANES = 128
EXTRA = 8
SLAB = 32
F32 = jnp.float32
BF16 = jnp.bfloat16
VMEM = pl.BlockSpec(memory_space=pltpu.VMEM)
ANY = pl.BlockSpec(memory_space=pl.ANY)
HBM = pl.BlockSpec(memory_space=pltpu.HBM)
CODE = 10.0
FINE = 18.0
VMEM_LIMIT = 48 * 1024 * 1024


def iota(shape, dim):
    return lax.broadcasted_iota(jnp.int32, shape, dim)


def split(x):
    high = x.astype(BF16)
    return high, (x - high.astype(F32)).astype(BF16)


def power(n):
    assert n & (n - 1) == 0
    return n.bit_length() - 1


def call(body, outs, args, specs, scratch=(), flops=0, nbytes=0, place=VMEM, fixed=False, passed=()):
    shape = pltpu.VMEM if fixed else jax.ShapeDtypeStruct
    passed = dict(passed)
    return pl.pallas_call(
        body,
        out_shape=tuple(shape(s, d) for s, d in outs),
        in_specs=list(specs),
        out_specs=place if isinstance(place, tuple) else (place,) * len(outs),
        input_output_aliases=passed,
        scratch_shapes=list(scratch),
        compiler_params=pltpu.CompilerParams(vmem_limit_bytes=VMEM_LIMIT),
        cost_estimate=pl.CostEstimate(flops=flops, bytes_accessed=nbytes, transcendentals=0),
    )(*args)


def pack_span(nspan, n_in, *refs):
    ins, rest = refs[:n_in], refs[n_in:]
    outs, kept, (m_s, sems) = rest[: -n_in - 1], rest[-n_in - 1 : -2], rest[-2:]
    f_ref, k_ref = kept[:2]
    radial, axial = f_ref.shape[2:]
    s = lax.axis_index("span")
    half = radial - 8
    early = [pltpu.make_async_copy(ins[-1], m_s, sems.at[0])]
    late = []
    for n, first, size in ((0, (1 - s) * half, 8), (1, s * 8, half)):
        rows = pl.ds(pl.multiple_of(first, 8), size)
        copies = [
            pltpu.make_async_copy(
                ins[0].at[:, :, rows, :], f_ref.at[:, :, rows, :], sems.at[1 + 2 * n]
            ),
            pltpu.make_async_copy(ins[1].at[:, rows, :], k_ref.at[:, rows, :], sems.at[2 + 2 * n]),
        ]
        if n == 0 or nspan > 2:
            early += copies
        else:
            late += copies
    for n in range(2, n_in - 1):
        late.append(pltpu.make_async_copy(ins[n], kept[n], sems.at[n + 3]))
    for copy in early + late:
        copy.start()
    for copy in early:
        copy.wait()

    def edge(first):
        parts = []
        for r in range(2):
            row = pl.ds(first + r, 1)
            parts += [f_ref[:, :, row, :].reshape(-1, axial), k_ref[:, row, :].reshape(-1, axial)]
        return jnp.concatenate(parts, 0).astype(BF16)

    flow = m_s[...].astype(F32)
    flow = jnp.concatenate([flow[:, 0, :], flow[:, 1, :]], 0).astype(BF16)
    def corner(layer):
        stator = lax.axis_index("row") == 0
        return jnp.where(stator, layer[:, axial - LANES :], layer[:, :LANES]).astype(BF16)

    if nspan == 2:
        packed = edge((1 - s) * (radial - 2))
        outs[1][...] = packed
        both = packed.astype(F32)
        half = both.shape[0] // 2
        near = corner(jnp.where(s == 0, both[half:], both[:half]))
        half = near.shape[0] // 2
        outs[0][: 2 * radial] = flow
        outs[0][2 * radial :, :LANES] = near[:half]
        outs[0][2 * radial :, LANES : 2 * LANES] = near[half:]
    else:
        top, bottom = edge(radial - 2), edge(0)
        half = top.shape[0] // 2
        outs[0][...] = top
        outs[1][...] = bottom
        outs[2][...] = corner(top[half:].astype(F32))
        outs[3][...] = corner(bottom[:half].astype(F32))
        outs[4][...] = flow
    for copy in late:
        copy.wait()


def tracer_chunk(ref, c):
    both = [ref[pl.ds(2 * c + n, 1), :] for n in range(2)]
    return jnp.concatenate(both, 1), pl.ds(pl.multiple_of(c * 2 * LANES, 2 * LANES), 2 * LANES)


def one_hot(rows, index):
    return (iota((rows, index.shape[1]), 0) == index).astype(F32).astype(BF16)


def sample_fields(npitch, f_ref, cell_ref, dest_ref, samp_ref, place_ref, key_ref, pick_ref, table_s):
    nfield, pitch, radial, axial = f_ref.shape
    lines = pitch * radial
    chunks = cell_ref.shape[0]

    @pl.loop(0, nfield, unroll=True)
    def _(f):
        table_s[f] = jnp.exp2(FINE * f_ref[f].reshape(lines, axial)).astype(BF16)

    table = table_s[...].reshape(nfield * lines, axial)
    samp_ref[...] = jnp.zeros(samp_ref.shape, F32)

    @pl.loop(0, chunks // 2, unroll=True)
    def _(c):
        cells, span = tracer_chunk(cell_ref, c)
        pick = one_hot(axial, cells & (axial - 1))
        pick_ref[:, span] = pick
        got = jnp.dot(table, pick, preferred_element_type=F32)
        mine = iota((lines, cells.shape[1]), 0) == lax.shift_right_logical(cells, power(axial))
        for f in range(nfield):
            part = jnp.where(mine, got[f * lines : (f + 1) * lines], 0.0)
            part = jnp.sum(part, 0, keepdims=True)
            samp_ref[f : f + 1, span] = jnp.log2(part) * (1.0 / FINE)

    ones = []
    for c in range(chunks):
        ones.append((iota((npitch, LANES), 0) == dest_ref[c : c + 1, :]).astype(F32))
    stacked = jnp.concatenate(ones, 0)
    before = (iota((LANES, LANES), 0) < iota((LANES, LANES), 1)).astype(F32).astype(BF16)
    prefix = jnp.dot(stacked.astype(BF16), before, preferred_element_type=F32)
    carry = jnp.zeros((npitch, 1), F32)
    for c in range(chunks):
        rank = prefix[c * npitch : (c + 1) * npitch] + carry
        slot = jnp.sum(rank * ones[c], 0, keepdims=True).astype(jnp.int32)
        span = slice(c * LANES, (c + 1) * LANES)
        width = place_ref.shape[0]
        place_ref[:, span] = one_hot(width, slot & (width - 1))
        groups = 2 * chunks * LANES // npitch // width
        key_ref[:, span] = dest_ref[c : c + 1, :] * groups + lax.shift_right_logical(slot, power(width))
        carry = carry + jnp.sum(ones[c], 1, keepdims=True)


def slab(core, extra):
    return [extra, core, extra]


def near(stator, parts):
    turned = jnp.concatenate(parts, 0).T
    return (
        jnp.where(stator, turned[LANES - 1 : LANES], turned[0:1]),
        jnp.where(stator, turned[LANES - 2 : LANES - 1], turned[1:2]),
    )


def dispatch(
    npitch,
    nspan,
    f_ref,
    k_ref,
    kern_ref,
    tv_ref,
    cell_ref,
    map_ref,
    samp_ref,
    place_ref,
    key_ref,
    pick_ref,
    *refs,
):
    nfield, pitch, radial, axial = f_ref.shape
    planes = nfield + 1
    edge = planes * pitch
    if nspan == 2:
        sent_ref, got_ref = refs[:2]
        refs = refs[2:]
    else:
        low_ref, high_ref, all_ref = refs[:3]
        refs = refs[3:]
    buf_ref, speed_ref, face_ref, kern_s, upd_s, lhs_s, acc_s, face_s, near_s = refs
    s = lax.axis_index("span")
    q = lax.axis_index("row")

    total = kern_ref.shape[0]
    kern_s[...] = kern_ref[...].astype(F32)
    main = kern_s[pl.ds(pl.multiple_of(s * radial, 8), radial), :]
    above = kern_s[pl.ds(pl.multiple_of(jnp.minimum((s + 1) * radial, total - 8), 8), 8), :]
    below = kern_s[pl.ds(pl.multiple_of(jnp.maximum(s * radial - 8, 0), 8), 8), :]
    wide = jnp.concatenate([main, jnp.where(iota((EXTRA, total), 0) < 4, above, below)], 0).astype(BF16)
    smoothed = []
    for c in range(2):
        if nspan == 2:
            at = slice(c * radial, (c + 1) * radial)
            own, other = sent_ref[at, :].astype(F32), got_ref[at, :].astype(F32)
            rows = [jnp.where(s == 0, own, other), jnp.where(s == 0, other, own)]
        else:
            rows = [all_ref[n, c * radial : (c + 1) * radial, :].astype(F32) for n in range(nspan)]
        smoothed.append(
            jnp.dot(wide, jnp.concatenate(rows, 0).astype(BF16), preferred_element_type=F32)
        )
    sa = AXIAL_SPEED * (1.0 + 0.5 * jnp.tanh(smoothed[0]))
    sp = PITCH_SPEED * jnp.tanh(smoothed[1])
    speed_ref[0] = sa
    speed_ref[1] = sp

    chunks = cell_ref.shape[0]
    values, tracers = tv_ref.shape
    capacity = 2 * tracers // npitch
    count = nfield + 2
    table = jnp.concatenate(split(jnp.concatenate([sa[:radial], sp[:radial]], 0)), 0)

    @pl.loop(0, chunks // 2, unroll=True)
    def _(c):
        cells, span = tracer_chunk(cell_ref, c)
        line = lax.shift_right_logical(cells, power(axial)) & (radial - 1)
        got = jnp.dot(table, pick_ref[:, span], preferred_element_type=F32)
        got = got[: 2 * radial] + got[2 * radial :]
        mine = iota((radial, cells.shape[1]), 0) == line
        sampled = [samp_ref[f : f + 1, span] for f in range(nfield)]
        for n in range(2):
            part = jnp.where(mine, got[n * radial : (n + 1) * radial], 0.0)
            sampled.append(jnp.sum(part, 0, keepdims=True))
        for v, value in enumerate(sampled):
            head = tv_ref[v : v + 1, span]
            upd_s[v : v + 1, span] = head + 0.5 * (value - head)
            upd_s[count + v : count + v + 1, span] = tv_ref[count + v : count + v + 1, span] + 0.8 * value

    width = place_ref.shape[0]
    groups = capacity // width
    keys = npitch * groups
    coded = jnp.exp2(CODE * upd_s[:values])
    mine = iota((keys, tracers), 0) == key_ref[...]
    for v in range(values):
        lhs_s[v * keys : (v + 1) * keys, :] = jnp.where(mine, coded[v : v + 1], 0.0).astype(BF16)
    acc_s[...] = lax.dot_general(
        lhs_s[...], place_ref[...], (((1,), (1,)), ((), ())), preferred_element_type=F32
    ).reshape(acc_s.shape)
    room = buf_ref.shape[2] - values * capacity // LANES
    filler = [jnp.zeros((room, LANES), F32)] if room else []
    for d in range(npitch):
        pieces = []
        for g in range(groups):
            for n in range(width // LANES):
                pieces.append(acc_s[:, d * groups + g, n * LANES : (n + 1) * LANES])
        buf_ref[d, 0] = jnp.concatenate(pieces + filler, 0).astype(BF16)

    if nspan == 2:
        near_s[0, : edge // 2] = got_ref[2 * radial :, :LANES].astype(F32)
        near_s[0, edge // 2 :] = got_ref[2 * radial :, LANES : 2 * LANES].astype(F32)
        near_s[1] = near_s[0]
    else:
        near_s[0] = high_ref[...].astype(F32)
        near_s[1] = low_ref[...].astype(F32)
    sub = iota((EXTRA, LANES), 0)

    def beside(n):
        return jnp.where(
            sub == 0, near_s[0, n : n + 1], jnp.where(sub == 7, near_s[1, n : n + 1], 0.0)
        )

    stator = q == 0
    tile = pl.ds(pl.multiple_of((1 - q) * (axial - LANES), LANES), LANES)
    face_s[...] = jnp.zeros(face_s.shape, F32)

    for i in range(pitch):
        parts = []
        for f in range(planes):
            core = f_ref[f, i, :, tile] if f < nfield else k_ref[i, :, tile]
            parts += slab(core, beside(f * pitch + i))
        first, second = near(stator, parts)
        face_s[i : i + 1] = first
        face_s[pitch + i : pitch + i + 1] = second

    parts = []
    for n in range(2):
        speed = speed_ref[n, :, tile]
        parts += slab(speed[:radial], speed[radial:])
    first, second = near(stator, parts + [jnp.zeros((LANES - 2 * SLAB, LANES), F32)])
    face_s[2 * pitch : 2 * pitch + 1] = first
    face_s[2 * pitch + 1 : 2 * pitch + 2] = second
    face = face_s[...]
    face_ref[...] = face
    offset = map_ref[...].astype(F32)
    face_ref[2 * pitch + 2 : 2 * pitch + 3] = jnp.broadcast_to(offset[:, :1], (1, LANES))
    face = face.astype(BF16)

    @pl.loop(0, npitch, unroll=True)
    def _(d):
        buf_ref[d, 1] = face


def halos(low_ref, high_ref, f_ref, k_ref, halo_ref, up_ref, down_ref, near_s):
    nfield, pitch, radial, axial = f_ref.shape
    planes = nfield + 1
    edge = planes * pitch
    sub = iota((EXTRA, axial), 0)
    near_s[0] = high_ref[: 2 * edge].astype(F32)
    near_s[1] = low_ref[: 2 * edge].astype(F32)

    @pl.loop(0, edge, unroll=True)
    def _(n):
        tile = jnp.where(sub == 0, near_s[0, pl.ds(n, 1), :], 0.0)
        tile = jnp.where(sub == 1, near_s[0, pl.ds(edge + n, 1), :], tile)
        tile = jnp.where(sub == 6, near_s[1, pl.ds(n, 1), :], tile)
        halo_ref[n] = jnp.where(sub == 7, near_s[1, pl.ds(edge + n, 1), :], tile)

    def layers(ref, top):
        rows = []
        for f in range(planes):
            for n in range(2):
                i = top * (pitch - 2) + n
                rows.append(f_ref[f, i] if f < nfield else k_ref[i])
        for f in range(planes):
            corner = halo_ref[f * pitch + top * (pitch - 1)]
            rows += [corner[0:1], corner[7:8]]
        rows.append(jnp.zeros((8, axial), F32))
        ref[...] = jnp.concatenate(rows, 0).astype(BF16)

    layers(up_ref, 1)
    layers(down_ref, 0)


class Faces:
    def __init__(self, nspan, speed_ref, radial):
        self.rows, self.lanes = speed_ref.shape[1:]
        shape = (self.rows, self.lanes)
        s = lax.axis_index("span")
        stator = lax.axis_index("row") == 0
        lane, radius = iota(shape, 1), iota(shape, 0)
        sa = TIME_STEP * speed_ref[0]
        sp = TIME_STEP * speed_ref[1]
        wa = 0.5 * (sa + pltpu.roll(sa, self.lanes - 1, 1))
        self.first, self.last = lane == 0, lane == self.lanes - 1
        up, dn = jnp.maximum(wa, 0.0), jnp.minimum(wa, 0.0)
        self.axial = (
            jnp.where(self.last, 0.0, up),
            jnp.where(self.last, 0.0, dn),
            pltpu.roll(jnp.where(self.last, 0.0, up), 1, 1),
            pltpu.roll(jnp.where(self.last, 0.0, dn), 1, 1),
        )
        self.pitch_up, self.pitch_dn = jnp.maximum(sp, 0.0), jnp.minimum(sp, 0.0)
        top, bottom = s == nspan - 1, s == 0
        end = self.rows - 1
        self.wall_up = ((radius == radial - 1) & top) | ((radius == end) & bottom)
        self.wall_dn = ((radius == radial) & top) | ((radius == 0) & bottom)
        inlet = jnp.where(stator & self.first, sa, 0.0)
        keep = 1.0 + inlet - jnp.where(jnp.logical_not(stator) & self.last, sa, 0.0)
        self.keep = keep - self.axial[0] + self.axial[3] - self.pitch_up + self.pitch_dn

    def weights(self, k_before, k, k_after):
        half = 0.5 * TIME_STEP
        k = half * k
        k_up = jnp.where(self.last, 0.0, k + pltpu.roll(k, self.lanes - 1, 1))
        k_dn = jnp.where(self.first, 0.0, k + pltpu.roll(k, 1, 1))
        r_up = jnp.where(self.wall_up, 0.0, k + pltpu.roll(k, self.rows - 1, 0))
        r_dn = jnp.where(self.wall_dn, 0.0, k + pltpu.roll(k, 1, 0))
        p_up, p_dn = k + half * k_after, k + half * k_before
        return (
            self.keep - (k_up + k_dn) - (r_up + r_dn) - (p_up + p_dn),
            k_up - self.axial[1],
            k_dn + self.axial[2],
            r_up,
            r_dn,
            p_up - self.pitch_dn,
            p_dn + self.pitch_up,
        )

    def step(self, w, before, v, after):
        a = w[0] * v + w[1] * pltpu.roll(v, self.lanes - 1, 1)
        b = w[2] * pltpu.roll(v, 1, 1) + w[3] * pltpu.roll(v, self.rows - 1, 0)
        c = w[4] * pltpu.roll(v, 1, 0) + w[5] * after
        return (a + b) + (c + w[6] * before)


def middle(nspan, f_ref, k_ref, speed_ref, halo_ref, out_ref, o_ref, y2_ref, part_ref, outer_ref, row_ref, y_s, w_s, sem):
    nfield, pitch, radial, axial = f_ref.shape
    stator = lax.axis_index("row") == 0
    faces = Faces(nspan, speed_ref, radial)

    def state(f, i):
        return jnp.concatenate([f_ref[f, i], halo_ref[f * pitch + i]], 0)

    def kappa(i):
        return jnp.concatenate([k_ref[i], halo_ref[nfield * pitch + i]], 0)

    @pl.loop(1, pitch - 1, unroll=True)
    def _(i):
        w = faces.weights(kappa(i - 1), kappa(i), kappa(i + 1))
        for n, value in enumerate(w):
            w_s[n, i] = value
        for f in range(nfield):
            y_s[f, i] = faces.step(w, state(f, i - 1), state(f, i), state(f, i + 1))

    @pl.loop(2, pitch - 2, unroll=True)
    def _(i):
        w = [w_s[n, i] for n in range(7)]
        for f in range(nfield):
            o_ref[f, i - 2] = faces.step(w, y_s[f, i - 1], y_s[f, i], y_s[f, i + 1])[:radial]

    copies = []
    if axial > LANES:
        rest = pl.ds(pl.multiple_of(lax.axis_index("row") * LANES, LANES), axial - LANES)
        copies.append(
            pltpu.make_async_copy(
                o_ref.at[:, :, :, rest], out_ref.at[:, 2 : pitch - 2, :, rest], sem.at[0]
            )
        )
        copies[-1].start()
    k = [kappa(i) for i in (0, 1, pitch - 2, pitch - 1)]
    ends = faces.weights(-k[0], k[0], k[1]), faces.weights(k[2], k[3], -k[3])
    for n, value in enumerate(ends[0]):
        outer_ref[0, n] = value
    for n, value in enumerate(ends[1]):
        outer_ref[1, n] = value
    outer_ref[0, 7] = w_s[6, 1]
    outer_ref[1, 7] = w_s[5, pitch - 2]
    none = jnp.zeros((faces.rows, axial), F32)
    inner = [[w_s[n, i] for n in range(7)] for i in (1, pitch - 2)]
    for f in range(nfield):
        y2_ref[f, 0], y2_ref[f, 1] = y_s[f, 1], y_s[f, pitch - 2]
        part_ref[f, 0] = faces.step(ends[0], none, state(f, 0), state(f, 1))
        part_ref[f, 1] = faces.step(ends[1], state(f, pitch - 2), state(f, pitch - 1), none)
        part_ref[f, 2, :radial] = faces.step(inner[0], none, y_s[f, 1], y_s[f, 2])[:radial]
        part_ref[f, 3, :radial] = faces.step(inner[1], y_s[f, pitch - 3], y_s[f, pitch - 2], none)[:radial]
    row_ref[...] = jnp.zeros(row_ref.shape, F32)
    q = lax.axis_index("row")
    tile = pl.ds(pl.multiple_of((1 - q) * (axial - LANES), LANES), LANES)
    blank = jnp.zeros((SLAB, LANES), F32)

    @pl.loop(1, pitch - 1, unroll=True)
    def _(i):
        parts = []
        for f in range(nfield):
            parts += slab(y_s[f, i, :radial, tile], y_s[f, i, radial:, tile])
        row_ref[pl.ds(i, 1), :] = near(stator, parts + [blank])[0]

    for copy in copies:
        copy.wait()


def contribution(nspan, pitch, radial, face_ref, beyond, new_rows, window_ref):
    planes = LANES // SLAB
    nfield = planes - 1
    s = lax.axis_index("span")
    stator = lax.axis_index("row") == 0
    count = window_ref.shape[1]
    ghost, farther = window_ref[0], window_ref[1]
    tail = jnp.zeros((count - pitch - 2, LANES), F32)
    own = jnp.concatenate([beyond[0], face_ref[:pitch], beyond[1], tail], 0)
    top = jnp.zeros((1, LANES), F32)
    own_k1 = jnp.concatenate([top, face_ref[pitch : 2 * pitch], top, tail], 0)
    own_new = jnp.concatenate([top, new_rows, top, tail], 0)
    at = 2 * pitch

    def groups(row, g):
        out = row
        for f in range(planes):
            if f != g:
                out = jnp.where(iota(row.shape, 1) // SLAB == f, pltpu.roll(row, (f - g) * SLAB % LANES, 1), out)
        return out

    def speeds(rows):
        rows = TIME_STEP * rows
        return groups(rows[0:1], 0), groups(rows[1:2], 0), groups(rows[0:1], 1)

    sa0, sa1, sp0 = speeds(face_ref[at : at + 2])
    ga0, ga1, gp0 = speeds(window_ref[2, :2])
    shape = (count, LANES)
    lane = iota(shape, 1)
    group = lax.shift_right_logical(lane, power(SLAB))
    radius = lane & (SLAB - 1)

    def spread(x):
        out = x
        for f in range(nfield):
            out = jnp.where(group == f, pltpu.roll(x, (f + 1) * SLAB, 1), out)
        return out

    half = 0.5 * TIME_STEP
    k0, k1, g0, g1 = spread(own), spread(own_k1), spread(ghost), spread(farther)
    wall = ((radius == 7 + radial) & (s == nspan - 1)) | ((radius == 7) & (s == 0))

    def ahead(x):
        return pltpu.roll(x, count - 1, 0)

    def outward(x):
        return pltpu.roll(x, LANES - 1, 1)

    def change(v, k, speed):
        kappa = half * (k + ahead(k))
        up, dn = jnp.maximum(speed, 0.0), jnp.minimum(speed, 0.0)
        along = (up + kappa) * v + (dn - kappa) * ahead(v)
        kappa = jnp.where(wall, 0.0, half * (k + outward(k)))
        across = kappa * (v - outward(v))
        return along - pltpu.roll(along, 1, 0) + across - pltpu.roll(across, 1, 1)

    def face(first, second, speed, kappa):
        lower = jnp.where(stator, first, second)
        upper = jnp.where(stator, second, first)
        return (jnp.maximum(speed, 0.0) + kappa) * lower + (jnp.minimum(speed, 0.0) - kappa) * upper

    sign = jnp.where(stator, 1.0, -1.0)
    speed = 0.5 * (sa0 + ga0)
    kappa = half * (k0 + g0)
    flux = sign * face(own, ghost, speed, kappa)
    shift = -flux
    ghost_new = (
        ghost
        + flux
        - sign * face(ghost, farther, 0.5 * (ga0 + ga1), half * (g0 + g1))
        - change(ghost, g0, gp0)
    )
    flux = sign * face(own_new + shift, ghost_new, speed, kappa)
    inner = 0.5 * (sa0 + sa1)
    kappa = half * (k0 + k1)
    inner = sign * jnp.where(
        stator, jnp.minimum(inner, 0.0) - kappa, jnp.maximum(inner, 0.0) + kappa
    ) * shift
    add0 = shift - change(shift, k0, sp0) + inner - flux
    add1 = -inner
    return add0, add1


def column(stator, adds, i):
    row = iota((LANES, LANES), 0)
    near_row = jnp.where(stator, LANES - 1, 0)
    far_row = jnp.where(stator, LANES - 2, 1)
    far = jnp.where(row == far_row, adds[1][i + 1 : i + 2], 0.0)
    return jnp.where(row == near_row, adds[0][i + 1 : i + 2], far).T


def unpack(npitch, buf_ref, arr_out, arr_ref, sem):
    values = arr_ref.shape[0]
    capacity = arr_ref.shape[1] // npitch
    for p in range(npitch):
        coded = buf_ref[p, 0].astype(F32)
        plain = jnp.where(coded > 0.0, jnp.log2(coded) * (1.0 / CODE), 0.0)
        for j in range(capacity // LANES):
            at = p * capacity + j * LANES
            arr_ref[:, at : at + LANES] = plain[j * values : (j + 1) * values]
    copy = pltpu.make_async_copy(arr_ref, arr_out, sem.at[0])
    copy.start()
    copy.wait()


def extract(npitch, pitch, buf_ref, face_ref, window_ref, ring_s):
    whole = npitch * pitch
    count = window_ref.shape[1]
    for p in range(npitch):
        both = buf_ref[p, 1].astype(F32)
        ring_s[0, p * pitch : (p + 1) * pitch] = both[:pitch]
        ring_s[1, p * pitch : (p + 1) * pitch] = both[pitch : 2 * pitch]
        if p == 0:
            window_ref[2, :8] = both[2 * pitch : 2 * pitch + 8]
    for n in range(2):
        ring_s[n, whole : whole + pitch] = ring_s[n, :pitch]
        ring_s[n, whole + pitch :] = ring_s[n, pitch:count]
    facing = jnp.max(face_ref[2 * pitch + 2 : 2 * pitch + 3]).astype(jnp.int32)
    begin = 2 * pitch * lax.axis_index("pitch") - facing - 1 + 2 * whole
    begin = begin & (whole - 1)
    window_ref[0] = ring_s[0, pl.ds(begin, count), :]
    window_ref[1] = ring_s[1, pl.ds(begin, count), :]


def centre(nspan, mid_ref, face_ref, row_ref, window_ref, tile_ref):
    nfield, inner, radial, axial = mid_ref.shape
    pitch = inner + 4
    q = lax.axis_index("row")
    stator = q == 0
    near_tile = pl.ds(pl.multiple_of((1 - q) * (axial - LANES), LANES), LANES)
    blank = jnp.zeros((1, LANES), F32)
    adds = contribution(
        nspan, pitch, radial, face_ref, (blank, blank), row_ref[...], window_ref
    )
    for i in range(inner):
        block = column(stator, adds, i + 2)
        for f in range(nfield):
            at = f * SLAB + 8
            tile_ref[f, i] = mid_ref[f, i, :, near_tile] + block[at : at + radial]


def finish(
    nspan,
    _,
    tile_ref,
    f_ref,
    k_ref,
    speed_ref,
    halo_ref,
    lower_ref,
    upper_ref,
    y2_ref,
    part_ref,
    outer_ref,
    row_ref,
    face_ref,
    window_ref,
    out_ref,
    o_s,
    sems,
):
    nfield, pitch, radial, axial = f_ref.shape
    planes = nfield + 1
    stator = lax.axis_index("row") == 0
    q = lax.axis_index("row")
    near_tile = pl.ds(pl.multiple_of((1 - q) * (axial - LANES), LANES), LANES)
    copies = [
        pltpu.make_async_copy(
            tile_ref, out_ref.at[:, 2 : pitch - 2, :, near_tile], sems.at[2]
        )
    ]
    for copy in copies:
        copy.start()
    faces = Faces(nspan, speed_ref, radial)
    ext = {-1: lower_ref[...].astype(F32), 1: upper_ref[...].astype(F32)}
    sub = iota((EXTRA, axial), 0)
    corner_at = 2 * planes * radial

    def state(f, i):
        if 0 <= i < pitch:
            core = f_ref[f, i] if f < nfield else k_ref[i]
            return jnp.concatenate([core, halo_ref[f * pitch + i]], 0)
        side = ext[-1 if i < 0 else 1]
        at = (2 * f + (i + 2 if i < 0 else i - pitch)) * radial
        extra = jnp.zeros((EXTRA, axial), F32)
        if i in (-1, pitch):
            corner = corner_at + 2 * f
            extra = jnp.where(sub == 0, side[corner : corner + 1], 0.0)
            extra = jnp.where(sub == 7, side[corner + 1 : corner + 2], extra)
        return jnp.concatenate([side[at : at + radial], extra], 0)

    beyond, ends, results = [], [], {}

    def edge_lanes(value):
        return jnp.where(stator, value[:, axial - LANES :], value[:, :LANES])

    blank = jnp.zeros((SLAB, LANES), F32)
    for side in range(2):
        inside, outside, beyond_it = ((0, -1, -2), (pitch - 1, pitch, pitch + 1))[side]

        def ordered(far, centre, near):
            return (far, centre, near) if side == 0 else (near, centre, far)

        k_in, k_out = state(nfield, inside), state(nfield, outside)
        w_out = faces.weights(*ordered(state(nfield, beyond_it), k_out, k_in))
        kappa = 0.5 * TIME_STEP * (k_in + k_out)
        w_in = [outer_ref[side, n] for n in range(7)]
        w_in[0] = w_in[0] - kappa
        w_in[6 - side] = w_in[6 - side] + kappa
        wind = faces.pitch_up if side == 0 else -faces.pitch_dn
        updated = []
        for f in range(nfield):
            x_in, x_out = state(f, inside), state(f, outside)
            y_out = faces.step(w_out, *ordered(state(f, beyond_it), x_out, x_in))
            y_in = part_ref[f, side] + kappa * (x_out - x_in) + wind * x_out
            new_in = faces.step(w_in, *ordered(y_out, y_in, y2_ref[f, side]))[:radial]
            new_next = part_ref[f, 2 + side, :radial] + (outer_ref[side, 7] * y_in)[:radial]
            results[f, 3 * side] = new_in
            results[f, 1 + side] = new_next
            value = edge_lanes(y_in)
            updated += slab(value[:radial], value[radial:])
        ends.append(near(stator, updated + [blank])[0])
        parts = []
        for f in range(planes):
            value = edge_lanes(state(f, -1 if side == 0 else pitch))
            parts += slab(value[:radial], value[radial:])
        beyond.append(near(stator, parts)[0])
    rows = row_ref[...]
    index = iota(rows.shape, 0)
    rows = jnp.where(index == 0, ends[0], jnp.where(index == pitch - 1, ends[1], rows))
    adds = contribution(nspan, pitch, radial, face_ref, beyond, rows, window_ref)
    none = jnp.zeros((radial, axial - LANES), F32)
    for side in range(2):
        first = side * (pitch - 2)
        for n in range(2):
            block = column(stator, adds, first + n)
            for f in range(nfield):
                add = block[f * SLAB + 8 : f * SLAB + 8 + radial]
                add = jnp.where(
                    stator, jnp.concatenate([none, add], 1), jnp.concatenate([add, none], 1)
                )
                o_s[f, 2 * side + n] = results[f, 2 * side + n] + add
        copies.append(
            pltpu.make_async_copy(
                o_s.at[:, 2 * side : 2 * side + 2], out_ref.at[:, first : first + 2], sems.at[side]
            )
        )
        copies[-1].start()
    for copy in copies:
        copy.wait()


def local(
    fields,
    diffusivity,
    mean_flow,
    radial_kernel,
    tracer_values,
    tracer_cells,
    tracer_dest,
    interface_map,
):
    npitch = lax.axis_size("pitch")
    nspan = lax.axis_size("span")
    nfield, pitch, radial, axial = fields.shape
    planes = nfield + 1
    values, tracers = tracer_values.shape
    chunks = tracers // LANES
    capacity = 2 * tracers // npitch
    edge = planes * pitch
    cells = tracer_cells.reshape(chunks, LANES)
    dest = tracer_dest.reshape(chunks, LANES)

    mean_rows = 2 * radial
    if nspan == 2:
        outs = [((mean_rows + edge // 2, axial), BF16), ((2 * edge, axial), BF16)]
    else:
        outs = [((2 * edge, axial), BF16)] * 2 + [((edge, LANES), BF16)] * 2
        outs += [((mean_rows, axial), BF16)]
    inputs = [fields, diffusivity, radial_kernel, tracer_values, cells, dest, interface_map, mean_flow]
    *packed, fields, diffusivity, radial_kernel, tracer_values, cells, dest, interface_map = call(
        lambda *refs: pack_span(nspan, len(inputs), *refs),
        outs + [(x.shape, x.dtype) for x in inputs[:-1]],
        [pltpu.with_memory_space_constraint(x, pltpu.HBM) for x in inputs],
        [HBM] * len(inputs),
        [
            pltpu.VMEM(mean_flow.shape, mean_flow.dtype),
            pltpu.SemaphoreType.DMA((len(inputs) + 2,)),
        ],
        nbytes=2**20,
        fixed=True,
    )
    if nspan == 2:
        swap = [(0, 1), (1, 0)]
        span_got = (packed[0], lax.ppermute(packed[0], "span", swap))
        low = high = lax.ppermute(packed[1], "span", swap)
    else:
        upward = [(n, n + 1) for n in range(nspan - 1)]
        downward = [(n + 1, n) for n in range(nspan - 1)]
        low, high = lax.ppermute(packed[0], "span", upward), lax.ppermute(packed[1], "span", downward)
        span_got = (
            lax.ppermute(packed[2], "span", upward),
            lax.ppermute(packed[3], "span", downward),
            lax.all_gather(packed[4], "span"),
        )

    width = min(2 * LANES, capacity)
    sampled = call(
        lambda *refs: sample_fields(npitch, *refs),
        [
            ((8, tracers), F32),
            ((width, tracers), BF16),
            ((1, tracers), jnp.int32),
            ((axial, tracers), BF16),
        ],
        (fields, cells, dest),
        [VMEM] * 3,
        [pltpu.VMEM((nfield, pitch * radial, axial), BF16)],
        flops=4 * nfield * pitch * radial * axial * tracers,
        nbytes=2**20,
    )

    rows = radial + EXTRA
    per_slot = max(values * capacity // LANES, 2 * pitch + 3)
    per_slot = -(-per_slot // 8) * 8
    halo_rows = 2 * planes * radial + 16
    buf, speeds, face = call(
        lambda *refs: dispatch(npitch, nspan, *refs),
        [
            ((npitch, 2, per_slot, LANES), BF16),
            ((2, rows, axial), F32),
            ((per_slot, LANES), F32),
        ],
        (
            fields,
            diffusivity,
            radial_kernel,
            tracer_values,
            cells,
            interface_map,
        )
        + tuple(sampled)
        + span_got,
        [VMEM] * (10 + len(span_got)),
        [
            pltpu.VMEM(radial_kernel.shape, F32),
            pltpu.VMEM((16, tracers), F32),
            pltpu.VMEM((values * npitch * capacity // width, tracers), BF16),
            pltpu.VMEM((values, npitch * capacity // width, width), F32),
            pltpu.VMEM((per_slot, LANES), F32),
            pltpu.VMEM((2, edge, LANES), F32),
        ],
        flops=2 * npitch * values * tracers * capacity,
        nbytes=2**21,
    )
    buf, halo, up, down = call(
        lambda *refs: halos(*refs[1:5], *refs[6:]),
        [((npitch, 2, per_slot, LANES), BF16), ((edge, EXTRA, axial), F32)]
        + [((halo_rows, axial), BF16)] * 2,
        (buf, low, high, fields, diffusivity),
        [ANY] + [VMEM] * 4,
        [pltpu.VMEM((2, 2 * edge, axial), F32)],
        nbytes=2**18,
        place=(ANY, VMEM, VMEM, VMEM),
        passed={0: 0},
    )
    buf = lax.all_to_all(buf, "pitch", 0, 0)
    ring = [(n, (n + 1) % npitch) for n in range(npitch)]
    lower = lax.ppermute(up, "pitch", ring)
    upper = lax.ppermute(down, "pitch", [(b, a) for a, b in ring])

    moved, mid, near_edge, part, outer, new_rows = call(
        lambda *refs: middle(nspan, *refs),
        [
            (fields.shape, F32),
            ((nfield, pitch - 4, radial, axial), F32),
            ((nfield, 2, rows, axial), F32),
            ((nfield, 4, rows, axial), F32),
            ((2, 8, rows, axial), F32),
            ((pitch, LANES), F32),
        ],
        (fields, diffusivity, speeds, halo),
        [VMEM] * 4,
        [
            pltpu.VMEM((nfield, pitch, rows, axial), F32),
            pltpu.VMEM((7, pitch, rows, axial), F32),
            pltpu.SemaphoreType.DMA((1,)),
        ],
        flops=2**24,
        nbytes=2**22,
        place=(ANY,) + (VMEM,) * 5,
    )
    (window,) = call(
        lambda *refs: extract(npitch, pitch, *refs[1:]),
        [((3, pitch + 8, LANES), F32)],
        (new_rows, buf, face),
        [VMEM] * 3,
        [pltpu.VMEM((2, npitch * pitch + pitch + 8, LANES), F32)],
        nbytes=2**18,
    )
    (arrived,) = call(
        lambda *refs: unpack(npitch, *refs[1:]),
        [((values, npitch * capacity), F32)],
        (window, buf),
        [VMEM] * 2,
        [pltpu.VMEM((values, npitch * capacity), F32), pltpu.SemaphoreType.DMA((1,))],
        nbytes=2**20,
        place=ANY,
    )
    window = lax.ppermute(window, "row", [(0, 1), (1, 0)])
    (near_mid,) = call(
        lambda *refs: centre(nspan, *refs),
        [((nfield, pitch - 4, radial, LANES), F32)],
        (mid, face, new_rows, window),
        [VMEM] * 4,
        flops=2**22,
        nbytes=2**20,
    )
    (moved,) = call(
        lambda *refs: finish(nspan, *refs),
        [(fields.shape, F32)],
        (
            moved,
            near_mid,
            fields,
            diffusivity,
            speeds,
            halo,
            lower,
            upper,
            near_edge,
            part,
            outer,
            new_rows,
            face,
            window,
        ),
        [ANY] + [VMEM] * 13,
        [
            pltpu.VMEM((nfield, 4, radial, axial), F32),
            pltpu.SemaphoreType.DMA((3,)),
        ],
        flops=2**23,
        nbytes=2**21,
        place=ANY,
        passed={0: 0},
    )
    return moved, arrived


def solution(mesh):
    placed = (
        P(None, "pitch", "span", "row"),
        P("pitch", "span", "row"),
        P("span", None, "row"),
        P(),
        P(None, ("pitch", "span", "row")),
        P(("pitch", "span", "row")),
        P(("pitch", "span", "row"), None),
        P("row", "pitch"),
    )
    return jax.shard_map(
        local,
        mesh=mesh,
        in_specs=placed,
        out_specs=(P(None, "pitch", "span", "row"), P(None, ("pitch", "span", "row"))),
        check_vma=False,
    )
```

```python
import jax
import jax.numpy as jnp
from jax import lax
from jax.experimental import pallas as pl
from jax.experimental.pallas import tpu as pltpu
from jax.sharding import PartitionSpec as P

SUB = 2
TIME_STEP = 0.9
AXIAL_SPEED = 0.15
PITCH_SPEED = 0.15
LANES = 128
EXTRA = 8
SLAB = 32
F32 = jnp.float32
BF16 = jnp.bfloat16
VMEM = pl.BlockSpec(memory_space=pltpu.VMEM)
ANY = pl.BlockSpec(memory_space=pl.ANY)
HBM = pl.BlockSpec(memory_space=pltpu.HBM)
CODE = 10.0
FINE = 18.0
VMEM_LIMIT = 48 * 1024 * 1024


def iota(shape, dim):
    return lax.broadcasted_iota(jnp.int32, shape, dim)


def split(x):
    high = x.astype(BF16)
    return high, (x - high.astype(F32)).astype(BF16)


def power(n):
    assert n & (n - 1) == 0
    return n.bit_length() - 1


def call(body, outs, args, specs, scratch=(), flops=0, nbytes=0, place=VMEM, fixed=False, passed=()):
    shape = pltpu.VMEM if fixed else jax.ShapeDtypeStruct
    passed = dict(passed)
    return pl.pallas_call(
        body,
        out_shape=tuple(shape(s, d) for s, d in outs),
        in_specs=list(specs),
        out_specs=place if isinstance(place, tuple) else (place,) * len(outs),
        input_output_aliases=passed,
        scratch_shapes=list(scratch),
        compiler_params=pltpu.CompilerParams(vmem_limit_bytes=VMEM_LIMIT),
        cost_estimate=pl.CostEstimate(flops=flops, bytes_accessed=nbytes, transcendentals=0),
    )(*args)


def pack_span(nspan, n_in, *refs):
    ins, rest = refs[:n_in], refs[n_in:]
    outs, kept, (m_s, sems) = rest[: -n_in - 1], rest[-n_in - 1 : -2], rest[-2:]
    f_ref, k_ref = kept[:2]
    radial, axial = f_ref.shape[2:]
    s = lax.axis_index("span")
    half = radial - 8
    early = [pltpu.make_async_copy(ins[-1], m_s, sems.at[0])]
    late = []
    for n, first, size in ((0, (1 - s) * half, 8), (1, s * 8, half)):
        rows = pl.ds(pl.multiple_of(first, 8), size)
        copies = [
            pltpu.make_async_copy(
                ins[0].at[:, :, rows, :], f_ref.at[:, :, rows, :], sems.at[1 + 2 * n]
            ),
            pltpu.make_async_copy(ins[1].at[:, rows, :], k_ref.at[:, rows, :], sems.at[2 + 2 * n]),
        ]
        if n == 0 or nspan > 2:
            early += copies
        else:
            late += copies
    for n in range(2, n_in - 1):
        late.append(pltpu.make_async_copy(ins[n], kept[n], sems.at[n + 3]))
    for copy in early + late:
        copy.start()
    for copy in early:
        copy.wait()

    def edge(first):
        parts = []
        for r in range(2):
            row = pl.ds(first + r, 1)
            parts += [f_ref[:, :, row, :].reshape(-1, axial), k_ref[:, row, :].reshape(-1, axial)]
        return jnp.concatenate(parts, 0).astype(BF16)

    flow = m_s[...].astype(F32)
    flow = jnp.concatenate([flow[:, 0, :], flow[:, 1, :]], 0).astype(BF16)
    def corner(layer):
        stator = lax.axis_index("row") == 0
        return jnp.where(stator, layer[:, axial - LANES :], layer[:, :LANES]).astype(BF16)

    if nspan == 2:
        packed = edge((1 - s) * (radial - 2))
        outs[1][...] = packed
        both = packed.astype(F32)
        half = both.shape[0] // 2
        near = corner(jnp.where(s == 0, both[half:], both[:half]))
        half = near.shape[0] // 2
        outs[0][: 2 * radial] = flow
        outs[0][2 * radial :, :LANES] = near[:half]
        outs[0][2 * radial :, LANES : 2 * LANES] = near[half:]
    else:
        top, bottom = edge(radial - 2), edge(0)
        half = top.shape[0] // 2
        outs[0][...] = top
        outs[1][...] = bottom
        outs[2][...] = corner(top[half:].astype(F32))
        outs[3][...] = corner(bottom[:half].astype(F32))
        outs[4][...] = flow
    for copy in late:
        copy.wait()


def tracer_chunk(ref, c):
    both = [ref[pl.ds(2 * c + n, 1), :] for n in range(2)]
    return jnp.concatenate(both, 1), pl.ds(pl.multiple_of(c * 2 * LANES, 2 * LANES), 2 * LANES)


def one_hot(rows, index):
    return (iota((rows, index.shape[1]), 0) == index).astype(F32).astype(BF16)


def sample_fields(npitch, f_ref, cell_ref, dest_ref, samp_ref, place_ref, key_ref, pick_ref, table_s):
    nfield, pitch, radial, axial = f_ref.shape
    lines = pitch * radial
    chunks = cell_ref.shape[0]

    @pl.loop(0, nfield, unroll=True)
    def _(f):
        table_s[f] = jnp.exp2(FINE * f_ref[f].reshape(lines, axial)).astype(BF16)

    table = table_s[...].reshape(nfield * lines, axial)
    samp_ref[...] = jnp.zeros(samp_ref.shape, F32)

    @pl.loop(0, chunks // 2, unroll=True)
    def _(c):
        cells, span = tracer_chunk(cell_ref, c)
        pick = one_hot(axial, cells & (axial - 1))
        pick_ref[:, span] = pick
        got = jnp.dot(table, pick, preferred_element_type=F32)
        mine = iota((lines, cells.shape[1]), 0) == lax.shift_right_logical(cells, power(axial))
        for f in range(nfield):
            part = jnp.where(mine, got[f * lines : (f + 1) * lines], 0.0)
            part = jnp.sum(part, 0, keepdims=True)
            samp_ref[f : f + 1, span] = jnp.log2(part) * (1.0 / FINE)

    ones = []
    for c in range(chunks):
        ones.append((iota((npitch, LANES), 0) == dest_ref[c : c + 1, :]).astype(F32))
    stacked = jnp.concatenate(ones, 0)
    before = (iota((LANES, LANES), 0) < iota((LANES, LANES), 1)).astype(F32).astype(BF16)
    prefix = jnp.dot(stacked.astype(BF16), before, preferred_element_type=F32)
    carry = jnp.zeros((npitch, 1), F32)
    for c in range(chunks):
        rank = prefix[c * npitch : (c + 1) * npitch] + carry
        slot = jnp.sum(rank * ones[c], 0, keepdims=True).astype(jnp.int32)
        span = slice(c * LANES, (c + 1) * LANES)
        width = place_ref.shape[0]
        place_ref[:, span] = one_hot(width, slot & (width - 1))
        groups = 2 * chunks * LANES // npitch // width
        key_ref[:, span] = dest_ref[c : c + 1, :] * groups + lax.shift_right_logical(slot, power(width))
        carry = carry + jnp.sum(ones[c], 1, keepdims=True)


def slab(core, extra):
    return [extra, core, extra]


def near(stator, parts):
    turned = jnp.concatenate(parts, 0).T
    return (
        jnp.where(stator, turned[LANES - 1 : LANES], turned[0:1]),
        jnp.where(stator, turned[LANES - 2 : LANES - 1], turned[1:2]),
    )


def dispatch(
    npitch,
    nspan,
    f_ref,
    k_ref,
    kern_ref,
    tv_ref,
    cell_ref,
    map_ref,
    samp_ref,
    place_ref,
    key_ref,
    pick_ref,
    *refs,
):
    nfield, pitch, radial, axial = f_ref.shape
    planes = nfield + 1
    edge = planes * pitch
    if nspan == 2:
        sent_ref, got_ref = refs[:2]
        refs = refs[2:]
    else:
        low_ref, high_ref, all_ref = refs[:3]
        refs = refs[3:]
    buf_ref, speed_ref, face_ref, kern_s, upd_s, lhs_s, acc_s, face_s, near_s = refs
    s = lax.axis_index("span")
    q = lax.axis_index("row")

    total = kern_ref.shape[0]
    kern_s[...] = kern_ref[...].astype(F32)
    main = kern_s[pl.ds(pl.multiple_of(s * radial, 8), radial), :]
    above = kern_s[pl.ds(pl.multiple_of(jnp.minimum((s + 1) * radial, total - 8), 8), 8), :]
    below = kern_s[pl.ds(pl.multiple_of(jnp.maximum(s * radial - 8, 0), 8), 8), :]
    wide = jnp.concatenate([main, jnp.where(iota((EXTRA, total), 0) < 4, above, below)], 0).astype(BF16)
    smoothed = []
    for c in range(2):
        if nspan == 2:
            at = slice(c * radial, (c + 1) * radial)
            own, other = sent_ref[at, :].astype(F32), got_ref[at, :].astype(F32)
            rows = [jnp.where(s == 0, own, other), jnp.where(s == 0, other, own)]
        else:
            rows = [all_ref[n, c * radial : (c + 1) * radial, :].astype(F32) for n in range(nspan)]
        smoothed.append(
            jnp.dot(wide, jnp.concatenate(rows, 0).astype(BF16), preferred_element_type=F32)
        )
    sa = AXIAL_SPEED * (1.0 + 0.5 * jnp.tanh(smoothed[0]))
    sp = PITCH_SPEED * jnp.tanh(smoothed[1])
    speed_ref[0] = sa
    speed_ref[1] = sp

    chunks = cell_ref.shape[0]
    values, tracers = tv_ref.shape
    capacity = 2 * tracers // npitch
    count = nfield + 2
    table = jnp.concatenate(split(jnp.concatenate([sa[:radial], sp[:radial]], 0)), 0)

    @pl.loop(0, chunks // 2, unroll=True)
    def _(c):
        cells, span = tracer_chunk(cell_ref, c)
        line = lax.shift_right_logical(cells, power(axial)) & (radial - 1)
        got = jnp.dot(table, pick_ref[:, span], preferred_element_type=F32)
        got = got[: 2 * radial] + got[2 * radial :]
        mine = iota((radial, cells.shape[1]), 0) == line
        sampled = [samp_ref[f : f + 1, span] for f in range(nfield)]
        for n in range(2):
            part = jnp.where(mine, got[n * radial : (n + 1) * radial], 0.0)
            sampled.append(jnp.sum(part, 0, keepdims=True))
        for v, value in enumerate(sampled):
            head = tv_ref[v : v + 1, span]
            upd_s[v : v + 1, span] = head + 0.5 * (value - head)
            upd_s[count + v : count + v + 1, span] = tv_ref[count + v : count + v + 1, span] + 0.8 * value

    width = place_ref.shape[0]
    groups = capacity // width
    keys = npitch * groups
    coded = jnp.exp2(CODE * upd_s[:values])
    mine = iota((keys, tracers), 0) == key_ref[...]
    for v in range(values):
        lhs_s[v * keys : (v + 1) * keys, :] = jnp.where(mine, coded[v : v + 1], 0.0).astype(BF16)
    acc_s[...] = lax.dot_general(
        lhs_s[...], place_ref[...], (((1,), (1,)), ((), ())), preferred_element_type=F32
    ).reshape(acc_s.shape)
    room = buf_ref.shape[2] - values * capacity // LANES
    filler = [jnp.zeros((room, LANES), F32)] if room else []
    for d in range(npitch):
        pieces = []
        for g in range(groups):
            for n in range(width // LANES):
                pieces.append(acc_s[:, d * groups + g, n * LANES : (n + 1) * LANES])
        buf_ref[d, 0] = jnp.concatenate(pieces + filler, 0).astype(BF16)

    if nspan == 2:
        near_s[0, : edge // 2] = got_ref[2 * radial :, :LANES].astype(F32)
        near_s[0, edge // 2 :] = got_ref[2 * radial :, LANES : 2 * LANES].astype(F32)
        near_s[1] = near_s[0]
    else:
        near_s[0] = high_ref[...].astype(F32)
        near_s[1] = low_ref[...].astype(F32)
    sub = iota((EXTRA, LANES), 0)

    def beside(n):
        return jnp.where(
            sub == 0, near_s[0, n : n + 1], jnp.where(sub == 7, near_s[1, n : n + 1], 0.0)
        )

    stator = q == 0
    tile = pl.ds(pl.multiple_of((1 - q) * (axial - LANES), LANES), LANES)
    face_s[...] = jnp.zeros(face_s.shape, F32)

    for i in range(pitch):
        parts = []
        for f in range(planes):
            core = f_ref[f, i, :, tile] if f < nfield else k_ref[i, :, tile]
            parts += slab(core, beside(f * pitch + i))
        first, second = near(stator, parts)
        face_s[i : i + 1] = first
        face_s[pitch + i : pitch + i + 1] = second

    parts = []
    for n in range(2):
        speed = speed_ref[n, :, tile]
        parts += slab(speed[:radial], speed[radial:])
    first, second = near(stator, parts + [jnp.zeros((LANES - 2 * SLAB, LANES), F32)])
    face_s[2 * pitch : 2 * pitch + 1] = first
    face_s[2 * pitch + 1 : 2 * pitch + 2] = second
    face = face_s[...]
    face_ref[...] = face
    offset = map_ref[...].astype(F32)
    face_ref[2 * pitch + 2 : 2 * pitch + 3] = jnp.broadcast_to(offset[:, :1], (1, LANES))
    face = face.astype(BF16)

    @pl.loop(0, npitch, unroll=True)
    def _(d):
        buf_ref[d, 1] = face


def halos(low_ref, high_ref, f_ref, k_ref, halo_ref, up_ref, down_ref, near_s):
    nfield, pitch, radial, axial = f_ref.shape
    planes = nfield + 1
    edge = planes * pitch
    sub = iota((EXTRA, axial), 0)
    near_s[0] = high_ref[: 2 * edge].astype(F32)
    near_s[1] = low_ref[: 2 * edge].astype(F32)

    @pl.loop(0, edge, unroll=True)
    def _(n):
        tile = jnp.where(sub == 0, near_s[0, pl.ds(n, 1), :], 0.0)
        tile = jnp.where(sub == 1, near_s[0, pl.ds(edge + n, 1), :], tile)
        tile = jnp.where(sub == 6, near_s[1, pl.ds(n, 1), :], tile)
        halo_ref[n] = jnp.where(sub == 7, near_s[1, pl.ds(edge + n, 1), :], tile)

    def layers(ref, top):
        rows = []
        for f in range(planes):
            for n in range(2):
                i = top * (pitch - 2) + n
                rows.append(f_ref[f, i] if f < nfield else k_ref[i])
        for f in range(planes):
            corner = halo_ref[f * pitch + top * (pitch - 1)]
            rows += [corner[0:1], corner[7:8]]
        rows.append(jnp.zeros((8, axial), F32))
        ref[...] = jnp.concatenate(rows, 0).astype(BF16)

    layers(up_ref, 1)
    layers(down_ref, 0)


class Faces:
    def __init__(self, nspan, speed_ref, radial):
        self.rows, self.lanes = speed_ref.shape[1:]
        shape = (self.rows, self.lanes)
        s = lax.axis_index("span")
        stator = lax.axis_index("row") == 0
        lane, radius = iota(shape, 1), iota(shape, 0)
        sa = TIME_STEP * speed_ref[0]
        sp = TIME_STEP * speed_ref[1]
        wa = 0.5 * (sa + pltpu.roll(sa, self.lanes - 1, 1))
        self.first, self.last = lane == 0, lane == self.lanes - 1
        up, dn = jnp.maximum(wa, 0.0), jnp.minimum(wa, 0.0)
        self.axial = (
            jnp.where(self.last, 0.0, up),
            jnp.where(self.last, 0.0, dn),
            pltpu.roll(jnp.where(self.last, 0.0, up), 1, 1),
            pltpu.roll(jnp.where(self.last, 0.0, dn), 1, 1),
        )
        self.pitch_up, self.pitch_dn = jnp.maximum(sp, 0.0), jnp.minimum(sp, 0.0)
        top, bottom = s == nspan - 1, s == 0
        end = self.rows - 1
        self.wall_up = ((radius == radial - 1) & top) | ((radius == end) & bottom)
        self.wall_dn = ((radius == radial) & top) | ((radius == 0) & bottom)
        inlet = jnp.where(stator & self.first, sa, 0.0)
        keep = 1.0 + inlet - jnp.where(jnp.logical_not(stator) & self.last, sa, 0.0)
        self.keep = keep - self.axial[0] + self.axial[3] - self.pitch_up + self.pitch_dn

    def weights(self, k_before, k, k_after):
        half = 0.5 * TIME_STEP
        k = half * k
        k_up = jnp.where(self.last, 0.0, k + pltpu.roll(k, self.lanes - 1, 1))
        k_dn = jnp.where(self.first, 0.0, k + pltpu.roll(k, 1, 1))
        r_up = jnp.where(self.wall_up, 0.0, k + pltpu.roll(k, self.rows - 1, 0))
        r_dn = jnp.where(self.wall_dn, 0.0, k + pltpu.roll(k, 1, 0))
        p_up, p_dn = k + half * k_after, k + half * k_before
        return (
            self.keep - (k_up + k_dn) - (r_up + r_dn) - (p_up + p_dn),
            k_up - self.axial[1],
            k_dn + self.axial[2],
            r_up,
            r_dn,
            p_up - self.pitch_dn,
            p_dn + self.pitch_up,
        )

    def step(self, w, before, v, after):
        a = w[0] * v + w[1] * pltpu.roll(v, self.lanes - 1, 1)
        b = w[2] * pltpu.roll(v, 1, 1) + w[3] * pltpu.roll(v, self.rows - 1, 0)
        c = w[4] * pltpu.roll(v, 1, 0) + w[5] * after
        return (a + b) + (c + w[6] * before)


def middle(nspan, f_ref, k_ref, speed_ref, halo_ref, out_ref, o_ref, y2_ref, part_ref, outer_ref, row_ref, y_s, w_s, sem):
    nfield, pitch, radial, axial = f_ref.shape
    stator = lax.axis_index("row") == 0
    faces = Faces(nspan, speed_ref, radial)

    def state(f, i):
        return jnp.concatenate([f_ref[f, i], halo_ref[f * pitch + i]], 0)

    def kappa(i):
        return jnp.concatenate([k_ref[i], halo_ref[nfield * pitch + i]], 0)

    @pl.loop(1, pitch - 1, unroll=True)
    def _(i):
        w = faces.weights(kappa(i - 1), kappa(i), kappa(i + 1))
        for n, value in enumerate(w):
            w_s[n, i] = value
        for f in range(nfield):
            y_s[f, i] = faces.step(w, state(f, i - 1), state(f, i), state(f, i + 1))

    @pl.loop(2, pitch - 2, unroll=True)
    def _(i):
        w = [w_s[n, i] for n in range(7)]
        for f in range(nfield):
            o_ref[f, i - 2] = faces.step(w, y_s[f, i - 1], y_s[f, i], y_s[f, i + 1])[:radial]

    copies = []
    if axial > LANES:
        rest = pl.ds(pl.multiple_of(lax.axis_index("row") * LANES, LANES), axial - LANES)
        copies.append(
            pltpu.make_async_copy(
                o_ref.at[:, :, :, rest], out_ref.at[:, 2 : pitch - 2, :, rest], sem.at[0]
            )
        )
        copies[-1].start()
    k = [kappa(i) for i in (0, 1, pitch - 2, pitch - 1)]
    ends = faces.weights(-k[0], k[0], k[1]), faces.weights(k[2], k[3], -k[3])
    for n, value in enumerate(ends[0]):
        outer_ref[0, n] = value
    for n, value in enumerate(ends[1]):
        outer_ref[1, n] = value
    outer_ref[0, 7] = w_s[6, 1]
    outer_ref[1, 7] = w_s[5, pitch - 2]
    none = jnp.zeros((faces.rows, axial), F32)
    inner = [[w_s[n, i] for n in range(7)] for i in (1, pitch - 2)]
    for f in range(nfield):
        y2_ref[f, 0], y2_ref[f, 1] = y_s[f, 1], y_s[f, pitch - 2]
        part_ref[f, 0] = faces.step(ends[0], none, state(f, 0), state(f, 1))
        part_ref[f, 1] = faces.step(ends[1], state(f, pitch - 2), state(f, pitch - 1), none)
        part_ref[f, 2, :radial] = faces.step(inner[0], none, y_s[f, 1], y_s[f, 2])[:radial]
        part_ref[f, 3, :radial] = faces.step(inner[1], y_s[f, pitch - 3], y_s[f, pitch - 2], none)[:radial]
    row_ref[...] = jnp.zeros(row_ref.shape, F32)
    q = lax.axis_index("row")
    tile = pl.ds(pl.multiple_of((1 - q) * (axial - LANES), LANES), LANES)
    blank = jnp.zeros((SLAB, LANES), F32)

    @pl.loop(1, pitch - 1, unroll=True)
    def _(i):
        parts = []
        for f in range(nfield):
            parts += slab(y_s[f, i, :radial, tile], y_s[f, i, radial:, tile])
        row_ref[pl.ds(i, 1), :] = near(stator, parts + [blank])[0]

    for copy in copies:
        copy.wait()


def contribution(nspan, pitch, radial, face_ref, beyond, new_rows, window_ref):
    planes = LANES // SLAB
    nfield = planes - 1
    s = lax.axis_index("span")
    stator = lax.axis_index("row") == 0
    count = window_ref.shape[1]
    ghost, farther = window_ref[0], window_ref[1]
    tail = jnp.zeros((count - pitch - 2, LANES), F32)
    own = jnp.concatenate([beyond[0], face_ref[:pitch], beyond[1], tail], 0)
    top = jnp.zeros((1, LANES), F32)
    own_k1 = jnp.concatenate([top, face_ref[pitch : 2 * pitch], top, tail], 0)
    own_new = jnp.concatenate([top, new_rows, top, tail], 0)
    at = 2 * pitch

    def groups(row, g):
        out = row
        for f in range(planes):
            if f != g:
                out = jnp.where(iota(row.shape, 1) // SLAB == f, pltpu.roll(row, (f - g) * SLAB % LANES, 1), out)
        return out

    def speeds(rows):
        rows = TIME_STEP * rows
        return groups(rows[0:1], 0), groups(rows[1:2], 0), groups(rows[0:1], 1)

    sa0, sa1, sp0 = speeds(face_ref[at : at + 2])
    ga0, ga1, gp0 = speeds(window_ref[2, :2])
    shape = (count, LANES)
    lane = iota(shape, 1)
    group = lax.shift_right_logical(lane, power(SLAB))
    radius = lane & (SLAB - 1)

    def spread(x):
        out = x
        for f in range(nfield):
            out = jnp.where(group == f, pltpu.roll(x, (f + 1) * SLAB, 1), out)
        return out

    half = 0.5 * TIME_STEP
    k0, k1, g0, g1 = spread(own), spread(own_k1), spread(ghost), spread(farther)
    wall = ((radius == 7 + radial) & (s == nspan - 1)) | ((radius == 7) & (s == 0))

    def ahead(x):
        return pltpu.roll(x, count - 1, 0)

    def outward(x):
        return pltpu.roll(x, LANES - 1, 1)

    def change(v, k, speed):
        kappa = half * (k + ahead(k))
        up, dn = jnp.maximum(speed, 0.0), jnp.minimum(speed, 0.0)
        along = (up + kappa) * v + (dn - kappa) * ahead(v)
        kappa = jnp.where(wall, 0.0, half * (k + outward(k)))
        across = kappa * (v - outward(v))
        return along - pltpu.roll(along, 1, 0) + across - pltpu.roll(across, 1, 1)

    def face(first, second, speed, kappa):
        lower = jnp.where(stator, first, second)
        upper = jnp.where(stator, second, first)
        return (jnp.maximum(speed, 0.0) + kappa) * lower + (jnp.minimum(speed, 0.0) - kappa) * upper

    sign = jnp.where(stator, 1.0, -1.0)
    speed = 0.5 * (sa0 + ga0)
    kappa = half * (k0 + g0)
    flux = sign * face(own, ghost, speed, kappa)
    shift = -flux
    ghost_new = (
        ghost
        + flux
        - sign * face(ghost, farther, 0.5 * (ga0 + ga1), half * (g0 + g1))
        - change(ghost, g0, gp0)
    )
    flux = sign * face(own_new + shift, ghost_new, speed, kappa)
    inner = 0.5 * (sa0 + sa1)
    kappa = half * (k0 + k1)
    inner = sign * jnp.where(
        stator, jnp.minimum(inner, 0.0) - kappa, jnp.maximum(inner, 0.0) + kappa
    ) * shift
    add0 = shift - change(shift, k0, sp0) + inner - flux
    add1 = -inner
    return add0, add1


def column(stator, adds, i):
    row = iota((LANES, LANES), 0)
    near_row = jnp.where(stator, LANES - 1, 0)
    far_row = jnp.where(stator, LANES - 2, 1)
    far = jnp.where(row == far_row, adds[1][i + 1 : i + 2], 0.0)
    return jnp.where(row == near_row, adds[0][i + 1 : i + 2], far).T


def unpack(npitch, buf_ref, arr_out, arr_ref, sem):
    values = arr_ref.shape[0]
    capacity = arr_ref.shape[1] // npitch
    for p in range(npitch):
        coded = buf_ref[p, 0].astype(F32)
        plain = jnp.where(coded > 0.0, jnp.log2(coded) * (1.0 / CODE), 0.0)
        for j in range(capacity // LANES):
            at = p * capacity + j * LANES
            arr_ref[:, at : at + LANES] = plain[j * values : (j + 1) * values]
    copy = pltpu.make_async_copy(arr_ref, arr_out, sem.at[0])
    copy.start()
    copy.wait()


def extract(npitch, pitch, buf_ref, face_ref, window_ref, ring_s):
    whole = npitch * pitch
    count = window_ref.shape[1]
    for p in range(npitch):
        both = buf_ref[p, 1].astype(F32)
        ring_s[0, p * pitch : (p + 1) * pitch] = both[:pitch]
        ring_s[1, p * pitch : (p + 1) * pitch] = both[pitch : 2 * pitch]
        if p == 0:
            window_ref[2, :8] = both[2 * pitch : 2 * pitch + 8]
    for n in range(2):
        ring_s[n, whole : whole + pitch] = ring_s[n, :pitch]
        ring_s[n, whole + pitch :] = ring_s[n, pitch:count]
    facing = jnp.max(face_ref[2 * pitch + 2 : 2 * pitch + 3]).astype(jnp.int32)
    begin = 2 * pitch * lax.axis_index("pitch") - facing - 1 + 2 * whole
    begin = begin & (whole - 1)
    window_ref[0] = ring_s[0, pl.ds(begin, count), :]
    window_ref[1] = ring_s[1, pl.ds(begin, count), :]


def edges(
    nspan,
    _,
    f_ref,
    k_ref,
    speed_ref,
    halo_ref,
    lower_ref,
    upper_ref,
    y2_ref,
    part_ref,
    outer_ref,
    row_ref,
    o_ref,
    rows_ref,
    beyond_ref,
):
    nfield, pitch, radial, axial = f_ref.shape
    planes = nfield + 1
    stator = lax.axis_index("row") == 0
    faces = Faces(nspan, speed_ref, radial)
    ext = {-1: lower_ref[...].astype(F32), 1: upper_ref[...].astype(F32)}
    sub = iota((EXTRA, axial), 0)
    corner_at = 2 * planes * radial

    def state(f, i):
        if 0 <= i < pitch:
            core = f_ref[f, i] if f < nfield else k_ref[i]
            return jnp.concatenate([core, halo_ref[f * pitch + i]], 0)
        side = ext[-1 if i < 0 else 1]
        at = (2 * f + (i + 2 if i < 0 else i - pitch)) * radial
        extra = jnp.zeros((EXTRA, axial), F32)
        if i in (-1, pitch):
            corner = corner_at + 2 * f
            extra = jnp.where(sub == 0, side[corner : corner + 1], 0.0)
            extra = jnp.where(sub == 7, side[corner + 1 : corner + 2], extra)
        return jnp.concatenate([side[at : at + radial], extra], 0)

    beyond, ends = [], []

    def edge_lanes(value):
        return jnp.where(stator, value[:, axial - LANES :], value[:, :LANES])

    blank = jnp.zeros((SLAB, LANES), F32)
    for side in range(2):
        inside, outside, beyond_it = ((0, -1, -2), (pitch - 1, pitch, pitch + 1))[side]

        def ordered(far, centre, near):
            return (far, centre, near) if side == 0 else (near, centre, far)

        k_in, k_out = state(nfield, inside), state(nfield, outside)
        w_out = faces.weights(*ordered(state(nfield, beyond_it), k_out, k_in))
        kappa = 0.5 * TIME_STEP * (k_in + k_out)
        w_in = [outer_ref[side, n] for n in range(7)]
        w_in[0] = w_in[0] - kappa
        w_in[6 - side] = w_in[6 - side] + kappa
        wind = faces.pitch_up if side == 0 else -faces.pitch_dn
        updated = []
        for f in range(nfield):
            x_in, x_out = state(f, inside), state(f, outside)
            y_out = faces.step(w_out, *ordered(state(f, beyond_it), x_out, x_in))
            y_in = part_ref[f, side] + kappa * (x_out - x_in) + wind * x_out
            new_in = faces.step(w_in, *ordered(y_out, y_in, y2_ref[f, side]))[:radial]
            new_next = part_ref[f, 2 + side, :radial] + (outer_ref[side, 7] * y_in)[:radial]
            o_ref[f, 3 * side] = new_in
            o_ref[f, 1 + side] = new_next
            value = edge_lanes(y_in)
            updated += slab(value[:radial], value[radial:])
        ends.append(near(stator, updated + [blank])[0])
        parts = []
        for f in range(planes):
            value = edge_lanes(state(f, -1 if side == 0 else pitch))
            parts += slab(value[:radial], value[radial:])
        beyond.append(near(stator, parts)[0])
    rows = row_ref[...]
    index = iota(rows.shape, 0)
    rows_ref[...] = jnp.where(index == 0, ends[0], jnp.where(index == pitch - 1, ends[1], rows))
    beyond_ref[...] = jnp.zeros(beyond_ref.shape, F32)
    beyond_ref[0:1] = beyond[0]
    beyond_ref[1:2] = beyond[1]


def finish(nspan, _, mid_ref, edge_ref, face_ref, rows_ref, beyond_ref, window_ref, out_ref, tile_s, sems):
    nfield, pitch, radial, axial = out_ref.shape
    q = lax.axis_index("row")
    near_tile = pl.ds(pl.multiple_of((1 - q) * (axial - LANES), LANES), LANES)
    copies = []
    if axial > LANES:
        rest = pl.ds(pl.multiple_of(q * LANES, LANES), axial - LANES)
        for side in range(2):
            copies.append(
                pltpu.make_async_copy(
                    edge_ref.at[:, 2 * side : 2 * side + 2, :, rest],
                    out_ref.at[:, side * (pitch - 2) : side * (pitch - 2) + 2, :, rest],
                    sems.at[side],
                )
            )
            copies[-1].start()
    beyond = beyond_ref[0:1], beyond_ref[1:2]
    adds = contribution(nspan, pitch, radial, face_ref, beyond, rows_ref[...], window_ref)
    part = pitch // 4
    for n in range(4):
        for i in range(n * part, (n + 1) * part):
            block = column(q == 0, adds, i)
            for f in range(nfield):
                if 2 <= i < pitch - 2:
                    old = mid_ref[f, i - 2, :, near_tile]
                else:
                    old = edge_ref[f, i if i < 2 else i - pitch + 4, :, near_tile]
                tile_s[f, i] = old + block[f * SLAB + 8 : f * SLAB + 8 + radial]
        done = slice(n * part, (n + 1) * part)
        copies.append(
            pltpu.make_async_copy(
                tile_s.at[:, done], out_ref.at[:, done, :, near_tile], sems.at[2 + n]
            )
        )
        copies[-1].start()
    for copy in copies:
        copy.wait()


def local(
    fields,
    diffusivity,
    mean_flow,
    radial_kernel,
    tracer_values,
    tracer_cells,
    tracer_dest,
    interface_map,
):
    npitch = lax.axis_size("pitch")
    nspan = lax.axis_size("span")
    nfield, pitch, radial, axial = fields.shape
    planes = nfield + 1
    values, tracers = tracer_values.shape
    chunks = tracers // LANES
    capacity = 2 * tracers // npitch
    edge = planes * pitch
    cells = tracer_cells.reshape(chunks, LANES)
    dest = tracer_dest.reshape(chunks, LANES)

    mean_rows = 2 * radial
    if nspan == 2:
        outs = [((mean_rows + edge // 2, axial), BF16), ((2 * edge, axial), BF16)]
    else:
        outs = [((2 * edge, axial), BF16)] * 2 + [((edge, LANES), BF16)] * 2
        outs += [((mean_rows, axial), BF16)]
    inputs = [fields, diffusivity, radial_kernel, tracer_values, cells, dest, interface_map, mean_flow]
    *packed, fields, diffusivity, radial_kernel, tracer_values, cells, dest, interface_map = call(
        lambda *refs: pack_span(nspan, len(inputs), *refs),
        outs + [(x.shape, x.dtype) for x in inputs[:-1]],
        [pltpu.with_memory_space_constraint(x, pltpu.HBM) for x in inputs],
        [HBM] * len(inputs),
        [
            pltpu.VMEM(mean_flow.shape, mean_flow.dtype),
            pltpu.SemaphoreType.DMA((len(inputs) + 2,)),
        ],
        nbytes=2**20,
        fixed=True,
    )
    if nspan == 2:
        swap = [(0, 1), (1, 0)]
        span_got = (packed[0], lax.ppermute(packed[0], "span", swap))
        low = high = lax.ppermute(packed[1], "span", swap)
    else:
        upward = [(n, n + 1) for n in range(nspan - 1)]
        downward = [(n + 1, n) for n in range(nspan - 1)]
        low, high = lax.ppermute(packed[0], "span", upward), lax.ppermute(packed[1], "span", downward)
        span_got = (
            lax.ppermute(packed[2], "span", upward),
            lax.ppermute(packed[3], "span", downward),
            lax.all_gather(packed[4], "span"),
        )

    width = min(2 * LANES, capacity)
    sampled = call(
        lambda *refs: sample_fields(npitch, *refs),
        [
            ((8, tracers), F32),
            ((width, tracers), BF16),
            ((1, tracers), jnp.int32),
            ((axial, tracers), BF16),
        ],
        (fields, cells, dest),
        [VMEM] * 3,
        [pltpu.VMEM((nfield, pitch * radial, axial), BF16)],
        flops=4 * nfield * pitch * radial * axial * tracers,
        nbytes=2**20,
    )

    rows = radial + EXTRA
    per_slot = max(values * capacity // LANES, 2 * pitch + 3)
    per_slot = -(-per_slot // 8) * 8
    halo_rows = 2 * planes * radial + 16
    buf, speeds, face = call(
        lambda *refs: dispatch(npitch, nspan, *refs),
        [
            ((npitch, 2, per_slot, LANES), BF16),
            ((2, rows, axial), F32),
            ((per_slot, LANES), F32),
        ],
        (
            fields,
            diffusivity,
            radial_kernel,
            tracer_values,
            cells,
            interface_map,
        )
        + tuple(sampled)
        + span_got,
        [VMEM] * (10 + len(span_got)),
        [
            pltpu.VMEM(radial_kernel.shape, F32),
            pltpu.VMEM((16, tracers), F32),
            pltpu.VMEM((values * npitch * capacity // width, tracers), BF16),
            pltpu.VMEM((values, npitch * capacity // width, width), F32),
            pltpu.VMEM((per_slot, LANES), F32),
            pltpu.VMEM((2, edge, LANES), F32),
        ],
        flops=2 * npitch * values * tracers * capacity,
        nbytes=2**21,
    )
    buf, halo, up, down = call(
        lambda *refs: halos(*refs[1:5], *refs[6:]),
        [((npitch, 2, per_slot, LANES), BF16), ((edge, EXTRA, axial), F32)]
        + [((halo_rows, axial), BF16)] * 2,
        (buf, low, high, fields, diffusivity),
        [ANY] + [VMEM] * 4,
        [pltpu.VMEM((2, 2 * edge, axial), F32)],
        nbytes=2**18,
        place=(ANY, VMEM, VMEM, VMEM),
        passed={0: 0},
    )
    buf = lax.all_to_all(buf, "pitch", 0, 0)
    ring = [(n, (n + 1) % npitch) for n in range(npitch)]
    lower = lax.ppermute(up, "pitch", ring)
    upper = lax.ppermute(down, "pitch", [(b, a) for a, b in ring])

    moved, mid, near_edge, part, outer, new_rows = call(
        lambda *refs: middle(nspan, *refs),
        [
            (fields.shape, F32),
            ((nfield, pitch - 4, radial, axial), F32),
            ((nfield, 2, rows, axial), F32),
            ((nfield, 4, rows, axial), F32),
            ((2, 8, rows, axial), F32),
            ((pitch, LANES), F32),
        ],
        (fields, diffusivity, speeds, halo),
        [VMEM] * 4,
        [
            pltpu.VMEM((nfield, pitch, rows, axial), F32),
            pltpu.VMEM((7, pitch, rows, axial), F32),
            pltpu.SemaphoreType.DMA((1,)),
        ],
        flops=2**24,
        nbytes=2**22,
        place=(ANY,) + (VMEM,) * 5,
    )
    (window,) = call(
        lambda *refs: extract(npitch, pitch, *refs[1:]),
        [((3, pitch + 8, LANES), F32)],
        (new_rows, buf, face),
        [VMEM] * 3,
        [pltpu.VMEM((2, npitch * pitch + pitch + 8, LANES), F32)],
        nbytes=2**18,
    )
    (arrived,) = call(
        lambda *refs: unpack(npitch, *refs[1:]),
        [((values, npitch * capacity), F32)],
        (window, buf),
        [VMEM] * 2,
        [pltpu.VMEM((values, npitch * capacity), F32), pltpu.SemaphoreType.DMA((1,))],
        nbytes=2**20,
        place=ANY,
    )
    near_edge, new_rows, beyond = call(
        lambda *refs: edges(nspan, *refs),
        [
            ((nfield, 4, radial, axial), F32),
            ((pitch, LANES), F32),
            ((8, LANES), F32),
        ],
        (
            window,
            fields,
            diffusivity,
            speeds,
            halo,
            lower,
            upper,
            near_edge,
            part,
            outer,
            new_rows,
        ),
        [VMEM] * 11,
        flops=2**23,
        nbytes=2**21,
    )
    window = lax.ppermute(window, "row", [(0, 1), (1, 0)])
    (moved,) = call(
        lambda *refs: finish(nspan, *refs),
        [(fields.shape, F32)],
        (moved, mid, near_edge, face, new_rows, beyond, window),
        [ANY] + [VMEM] * 6,
        [
            pltpu.VMEM((nfield, pitch, radial, LANES), F32),
            pltpu.SemaphoreType.DMA((6,)),
        ],
        flops=2**22,
        nbytes=2**21,
        place=ANY,
        passed={0: 0},
    )
    return moved, arrived


def solution(mesh):
    placed = (
        P(None, "pitch", "span", "row"),
        P("pitch", "span", "row"),
        P("span", None, "row"),
        P(),
        P(None, ("pitch", "span", "row")),
        P(("pitch", "span", "row")),
        P(("pitch", "span", "row"), None),
        P("row", "pitch"),
    )
    return jax.shard_map(
        local,
        mesh=mesh,
        in_specs=placed,
        out_specs=(P(None, "pitch", "span", "row"), P(None, ("pitch", "span", "row"))),
        check_vma=False,
    )
```

```python
import jax
import jax.numpy as jnp
from jax import lax
from jax.experimental import pallas as pl
from jax.experimental.pallas import tpu as pltpu
from jax.sharding import PartitionSpec as P

SUB = 2
TIME_STEP = 0.9
AXIAL_SPEED = 0.15
PITCH_SPEED = 0.15
LANES = 128
EXTRA = 8
SLAB = 32
F32 = jnp.float32
BF16 = jnp.bfloat16
VMEM = pl.BlockSpec(memory_space=pltpu.VMEM)
ANY = pl.BlockSpec(memory_space=pl.ANY)
HBM = pl.BlockSpec(memory_space=pltpu.HBM)
CODE = 10.0
FINE = 18.0
VMEM_LIMIT = 48 * 1024 * 1024


def iota(shape, dim):
    return lax.broadcasted_iota(jnp.int32, shape, dim)


def split(x):
    high = x.astype(BF16)
    return high, (x - high.astype(F32)).astype(BF16)


def power(n):
    assert n & (n - 1) == 0
    return n.bit_length() - 1


def call(body, outs, args, specs, scratch=(), flops=0, nbytes=0, place=VMEM, fixed=False, passed=()):
    shape = pltpu.VMEM if fixed else jax.ShapeDtypeStruct
    passed = dict(passed)
    return pl.pallas_call(
        body,
        out_shape=tuple(shape(s, d) for s, d in outs),
        in_specs=list(specs),
        out_specs=place if isinstance(place, tuple) else (place,) * len(outs),
        input_output_aliases=passed,
        scratch_shapes=list(scratch),
        compiler_params=pltpu.CompilerParams(vmem_limit_bytes=VMEM_LIMIT),
        cost_estimate=pl.CostEstimate(flops=flops, bytes_accessed=nbytes, transcendentals=0),
    )(*args)


def pack_span(nspan, n_in, *refs):
    ins, rest = refs[:n_in], refs[n_in:]
    outs, kept, (m_s, sems) = rest[: -n_in - 1], rest[-n_in - 1 : -2], rest[-2:]
    f_ref, k_ref = kept[:2]
    radial, axial = f_ref.shape[2:]
    s = lax.axis_index("span")
    half = radial - 8
    early = [pltpu.make_async_copy(ins[-1], m_s, sems.at[0])]
    late = []
    for n, first, size in ((0, (1 - s) * half, 8), (1, s * 8, half)):
        rows = pl.ds(pl.multiple_of(first, 8), size)
        copies = [
            pltpu.make_async_copy(
                ins[0].at[:, :, rows, :], f_ref.at[:, :, rows, :], sems.at[1 + 2 * n]
            ),
            pltpu.make_async_copy(ins[1].at[:, rows, :], k_ref.at[:, rows, :], sems.at[2 + 2 * n]),
        ]
        if n == 0 or nspan > 2:
            early += copies
        else:
            late += copies
    for n in range(2, n_in - 1):
        late.append(pltpu.make_async_copy(ins[n], kept[n], sems.at[n + 3]))
    for copy in early + late:
        copy.start()
    for copy in early:
        copy.wait()

    def edge(first):
        parts = []
        for r in range(2):
            row = pl.ds(first + r, 1)
            parts += [f_ref[:, :, row, :].reshape(-1, axial), k_ref[:, row, :].reshape(-1, axial)]
        return jnp.concatenate(parts, 0).astype(BF16)

    flow = m_s[...].astype(F32)
    flow = jnp.concatenate([flow[:, 0, :], flow[:, 1, :]], 0).astype(BF16)
    def corner(layer):
        stator = lax.axis_index("row") == 0
        return jnp.where(stator, layer[:, axial - LANES :], layer[:, :LANES]).astype(BF16)

    if nspan == 2:
        packed = edge((1 - s) * (radial - 2))
        outs[1][...] = packed
        both = packed.astype(F32)
        half = both.shape[0] // 2
        near = corner(jnp.where(s == 0, both[half:], both[:half]))
        half = near.shape[0] // 2
        outs[0][: 2 * radial] = flow
        outs[0][2 * radial :, :LANES] = near[:half]
        outs[0][2 * radial :, LANES : 2 * LANES] = near[half:]
    else:
        top, bottom = edge(radial - 2), edge(0)
        half = top.shape[0] // 2
        outs[0][...] = top
        outs[1][...] = bottom
        outs[2][...] = corner(top[half:].astype(F32))
        outs[3][...] = corner(bottom[:half].astype(F32))
        outs[4][...] = flow
    for copy in late:
        copy.wait()


def tracer_chunk(ref, c):
    both = [ref[pl.ds(2 * c + n, 1), :] for n in range(2)]
    return jnp.concatenate(both, 1), pl.ds(pl.multiple_of(c * 2 * LANES, 2 * LANES), 2 * LANES)


def one_hot(rows, index):
    return (iota((rows, index.shape[1]), 0) == index).astype(F32).astype(BF16)


def sample_fields(npitch, f_ref, cell_ref, dest_ref, samp_ref, place_ref, key_ref, pick_ref, table_s):
    nfield, pitch, radial, axial = f_ref.shape
    lines = pitch * radial
    chunks = cell_ref.shape[0]

    @pl.loop(0, nfield, unroll=True)
    def _(f):
        table_s[f] = jnp.exp2(FINE * f_ref[f].reshape(lines, axial)).astype(BF16)

    table = table_s[...].reshape(nfield * lines, axial)
    samp_ref[...] = jnp.zeros(samp_ref.shape, F32)

    @pl.loop(0, chunks // 2, unroll=True)
    def _(c):
        cells, span = tracer_chunk(cell_ref, c)
        pick = one_hot(axial, cells & (axial - 1))
        pick_ref[:, span] = pick
        got = jnp.dot(table, pick, preferred_element_type=F32)
        mine = iota((lines, cells.shape[1]), 0) == lax.shift_right_logical(cells, power(axial))
        for f in range(nfield):
            part = jnp.where(mine, got[f * lines : (f + 1) * lines], 0.0)
            part = jnp.sum(part, 0, keepdims=True)
            samp_ref[f : f + 1, span] = jnp.log2(part) * (1.0 / FINE)

    ones = []
    for c in range(chunks):
        ones.append((iota((npitch, LANES), 0) == dest_ref[c : c + 1, :]).astype(F32))
    stacked = jnp.concatenate(ones, 0)
    before = (iota((LANES, LANES), 0) < iota((LANES, LANES), 1)).astype(F32).astype(BF16)
    prefix = jnp.dot(stacked.astype(BF16), before, preferred_element_type=F32)
    carry = jnp.zeros((npitch, 1), F32)
    for c in range(chunks):
        rank = prefix[c * npitch : (c + 1) * npitch] + carry
        slot = jnp.sum(rank * ones[c], 0, keepdims=True).astype(jnp.int32)
        span = slice(c * LANES, (c + 1) * LANES)
        width = place_ref.shape[0]
        place_ref[:, span] = one_hot(width, slot & (width - 1))
        groups = 2 * chunks * LANES // npitch // width
        key_ref[:, span] = dest_ref[c : c + 1, :] * groups + lax.shift_right_logical(slot, power(width))
        carry = carry + jnp.sum(ones[c], 1, keepdims=True)


def slab(core, extra):
    return [extra, core, extra]


def near(stator, parts):
    turned = jnp.concatenate(parts, 0).T
    return (
        jnp.where(stator, turned[LANES - 1 : LANES], turned[0:1]),
        jnp.where(stator, turned[LANES - 2 : LANES - 1], turned[1:2]),
    )


def dispatch(
    npitch,
    nspan,
    f_ref,
    k_ref,
    kern_ref,
    tv_ref,
    cell_ref,
    map_ref,
    samp_ref,
    place_ref,
    key_ref,
    pick_ref,
    *refs,
):
    nfield, pitch, radial, axial = f_ref.shape
    planes = nfield + 1
    edge = planes * pitch
    if nspan == 2:
        sent_ref, got_ref = refs[:2]
        refs = refs[2:]
    else:
        low_ref, high_ref, all_ref = refs[:3]
        refs = refs[3:]
    buf_ref, speed_ref, face_ref, kern_s, upd_s, lhs_s, acc_s, face_s, near_s = refs
    s = lax.axis_index("span")
    q = lax.axis_index("row")

    total = kern_ref.shape[0]
    kern_s[...] = kern_ref[...].astype(F32)
    main = kern_s[pl.ds(pl.multiple_of(s * radial, 8), radial), :]
    above = kern_s[pl.ds(pl.multiple_of(jnp.minimum((s + 1) * radial, total - 8), 8), 8), :]
    below = kern_s[pl.ds(pl.multiple_of(jnp.maximum(s * radial - 8, 0), 8), 8), :]
    wide = jnp.concatenate([main, jnp.where(iota((EXTRA, total), 0) < 4, above, below)], 0).astype(BF16)
    smoothed = []
    for c in range(2):
        if nspan == 2:
            at = slice(c * radial, (c + 1) * radial)
            own, other = sent_ref[at, :].astype(F32), got_ref[at, :].astype(F32)
            rows = [jnp.where(s == 0, own, other), jnp.where(s == 0, other, own)]
        else:
            rows = [all_ref[n, c * radial : (c + 1) * radial, :].astype(F32) for n in range(nspan)]
        smoothed.append(
            jnp.dot(wide, jnp.concatenate(rows, 0).astype(BF16), preferred_element_type=F32)
        )
    sa = AXIAL_SPEED * (1.0 + 0.5 * jnp.tanh(smoothed[0]))
    sp = PITCH_SPEED * jnp.tanh(smoothed[1])
    speed_ref[0] = sa
    speed_ref[1] = sp

    chunks = cell_ref.shape[0]
    values, tracers = tv_ref.shape
    capacity = 2 * tracers // npitch
    count = nfield + 2
    table = jnp.concatenate(split(jnp.concatenate([sa[:radial], sp[:radial]], 0)), 0)

    @pl.loop(0, chunks // 2, unroll=True)
    def _(c):
        cells, span = tracer_chunk(cell_ref, c)
        line = lax.shift_right_logical(cells, power(axial)) & (radial - 1)
        got = jnp.dot(table, pick_ref[:, span], preferred_element_type=F32)
        got = got[: 2 * radial] + got[2 * radial :]
        mine = iota((radial, cells.shape[1]), 0) == line
        sampled = [samp_ref[f : f + 1, span] for f in range(nfield)]
        for n in range(2):
            part = jnp.where(mine, got[n * radial : (n + 1) * radial], 0.0)
            sampled.append(jnp.sum(part, 0, keepdims=True))
        for v, value in enumerate(sampled):
            head = tv_ref[v : v + 1, span]
            upd_s[v : v + 1, span] = head + 0.5 * (value - head)
            upd_s[count + v : count + v + 1, span] = tv_ref[count + v : count + v + 1, span] + 0.8 * value

    width = place_ref.shape[0]
    groups = capacity // width
    keys = npitch * groups
    coded = jnp.exp2(CODE * upd_s[:values])
    mine = iota((keys, tracers), 0) == key_ref[...]
    for v in range(values):
        lhs_s[v * keys : (v + 1) * keys, :] = jnp.where(mine, coded[v : v + 1], 0.0).astype(BF16)
    acc_s[...] = lax.dot_general(
        lhs_s[...], place_ref[...], (((1,), (1,)), ((), ())), preferred_element_type=F32
    ).reshape(acc_s.shape)
    room = buf_ref.shape[2] - values * capacity // LANES
    filler = [jnp.zeros((room, LANES), F32)] if room else []
    for d in range(npitch):
        pieces = []
        for g in range(groups):
            for n in range(width // LANES):
                pieces.append(acc_s[:, d * groups + g, n * LANES : (n + 1) * LANES])
        buf_ref[d, 0] = jnp.concatenate(pieces + filler, 0).astype(BF16)

    if nspan == 2:
        near_s[0, : edge // 2] = got_ref[2 * radial :, :LANES].astype(F32)
        near_s[0, edge // 2 :] = got_ref[2 * radial :, LANES : 2 * LANES].astype(F32)
        near_s[1] = near_s[0]
    else:
        near_s[0] = high_ref[...].astype(F32)
        near_s[1] = low_ref[...].astype(F32)
    sub = iota((EXTRA, LANES), 0)

    def beside(n):
        return jnp.where(
            sub == 0, near_s[0, n : n + 1], jnp.where(sub == 7, near_s[1, n : n + 1], 0.0)
        )

    stator = q == 0
    tile = pl.ds(pl.multiple_of((1 - q) * (axial - LANES), LANES), LANES)
    face_s[...] = jnp.zeros(face_s.shape, F32)

    for i in range(pitch):
        parts = []
        for f in range(planes):
            core = f_ref[f, i, :, tile] if f < nfield else k_ref[i, :, tile]
            parts += slab(core, beside(f * pitch + i))
        first, second = near(stator, parts)
        face_s[i : i + 1] = first
        face_s[pitch + i : pitch + i + 1] = second

    parts = []
    for n in range(2):
        speed = speed_ref[n, :, tile]
        parts += slab(speed[:radial], speed[radial:])
    first, second = near(stator, parts + [jnp.zeros((LANES - 2 * SLAB, LANES), F32)])
    face_s[2 * pitch : 2 * pitch + 1] = first
    face_s[2 * pitch + 1 : 2 * pitch + 2] = second
    face = face_s[...]
    face_ref[...] = face
    offset = map_ref[...].astype(F32)
    face_ref[2 * pitch + 2 : 2 * pitch + 3] = jnp.broadcast_to(offset[:, :1], (1, LANES))
    face = face.astype(BF16)

    @pl.loop(0, npitch, unroll=True)
    def _(d):
        buf_ref[d, 1] = face


def halos(low_ref, high_ref, f_ref, k_ref, halo_ref, up_ref, down_ref, near_s):
    nfield, pitch, radial, axial = f_ref.shape
    planes = nfield + 1
    edge = planes * pitch
    sub = iota((EXTRA, axial), 0)
    near_s[0] = high_ref[: 2 * edge].astype(F32)
    near_s[1] = low_ref[: 2 * edge].astype(F32)

    @pl.loop(0, edge, unroll=True)
    def _(n):
        tile = jnp.where(sub == 0, near_s[0, pl.ds(n, 1), :], 0.0)
        tile = jnp.where(sub == 1, near_s[0, pl.ds(edge + n, 1), :], tile)
        tile = jnp.where(sub == 6, near_s[1, pl.ds(n, 1), :], tile)
        halo_ref[n] = jnp.where(sub == 7, near_s[1, pl.ds(edge + n, 1), :], tile)

    def layers(ref, top):
        rows = []
        for f in range(planes):
            for n in range(2):
                i = top * (pitch - 2) + n
                rows.append(f_ref[f, i] if f < nfield else k_ref[i])
        for f in range(planes):
            corner = halo_ref[f * pitch + top * (pitch - 1)]
            rows += [corner[0:1], corner[7:8]]
        rows.append(jnp.zeros((8, axial), F32))
        ref[...] = jnp.concatenate(rows, 0).astype(BF16)

    layers(up_ref, 1)
    layers(down_ref, 0)


class Faces:
    def __init__(self, nspan, speed_ref, radial):
        self.rows, self.lanes = speed_ref.shape[1:]
        shape = (self.rows, self.lanes)
        s = lax.axis_index("span")
        stator = lax.axis_index("row") == 0
        lane, radius = iota(shape, 1), iota(shape, 0)
        sa = TIME_STEP * speed_ref[0]
        sp = TIME_STEP * speed_ref[1]
        wa = 0.5 * (sa + pltpu.roll(sa, self.lanes - 1, 1))
        self.first, self.last = lane == 0, lane == self.lanes - 1
        up, dn = jnp.maximum(wa, 0.0), jnp.minimum(wa, 0.0)
        self.axial = (
            jnp.where(self.last, 0.0, up),
            jnp.where(self.last, 0.0, dn),
            pltpu.roll(jnp.where(self.last, 0.0, up), 1, 1),
            pltpu.roll(jnp.where(self.last, 0.0, dn), 1, 1),
        )
        self.pitch_up, self.pitch_dn = jnp.maximum(sp, 0.0), jnp.minimum(sp, 0.0)
        top, bottom = s == nspan - 1, s == 0
        end = self.rows - 1
        self.wall_up = ((radius == radial - 1) & top) | ((radius == end) & bottom)
        self.wall_dn = ((radius == radial) & top) | ((radius == 0) & bottom)
        inlet = jnp.where(stator & self.first, sa, 0.0)
        keep = 1.0 + inlet - jnp.where(jnp.logical_not(stator) & self.last, sa, 0.0)
        self.keep = keep - self.axial[0] + self.axial[3] - self.pitch_up + self.pitch_dn

    def weights(self, k_before, k, k_after):
        half = 0.5 * TIME_STEP
        k = half * k
        k_up = jnp.where(self.last, 0.0, k + pltpu.roll(k, self.lanes - 1, 1))
        k_dn = jnp.where(self.first, 0.0, k + pltpu.roll(k, 1, 1))
        r_up = jnp.where(self.wall_up, 0.0, k + pltpu.roll(k, self.rows - 1, 0))
        r_dn = jnp.where(self.wall_dn, 0.0, k + pltpu.roll(k, 1, 0))
        p_up, p_dn = k + half * k_after, k + half * k_before
        return (
            self.keep - (k_up + k_dn) - (r_up + r_dn) - (p_up + p_dn),
            k_up - self.axial[1],
            k_dn + self.axial[2],
            r_up,
            r_dn,
            p_up - self.pitch_dn,
            p_dn + self.pitch_up,
        )

    def step(self, w, before, v, after):
        a = w[0] * v + w[1] * pltpu.roll(v, self.lanes - 1, 1)
        b = w[2] * pltpu.roll(v, 1, 1) + w[3] * pltpu.roll(v, self.rows - 1, 0)
        c = w[4] * pltpu.roll(v, 1, 0) + w[5] * after
        return (a + b) + (c + w[6] * before)


def middle(nspan, f_ref, k_ref, speed_ref, halo_ref, out_ref, o_ref, y2_ref, part_ref, outer_ref, row_ref, y_s, w_s, sem):
    nfield, pitch, radial, axial = f_ref.shape
    stator = lax.axis_index("row") == 0
    faces = Faces(nspan, speed_ref, radial)

    def state(f, i):
        return jnp.concatenate([f_ref[f, i], halo_ref[f * pitch + i]], 0)

    def kappa(i):
        return jnp.concatenate([k_ref[i], halo_ref[nfield * pitch + i]], 0)

    @pl.loop(1, pitch - 1, unroll=True)
    def _(i):
        w = faces.weights(kappa(i - 1), kappa(i), kappa(i + 1))
        for n, value in enumerate(w):
            w_s[n, i] = value
        for f in range(nfield):
            y_s[f, i] = faces.step(w, state(f, i - 1), state(f, i), state(f, i + 1))

    @pl.loop(2, pitch - 2, unroll=True)
    def _(i):
        w = [w_s[n, i] for n in range(7)]
        for f in range(nfield):
            o_ref[f, i - 2] = faces.step(w, y_s[f, i - 1], y_s[f, i], y_s[f, i + 1])[:radial]

    copies = []
    if axial > LANES:
        rest = pl.ds(pl.multiple_of(lax.axis_index("row") * LANES, LANES), axial - LANES)
        copies.append(
            pltpu.make_async_copy(
                o_ref.at[:, :, :, rest], out_ref.at[:, 2 : pitch - 2, :, rest], sem.at[0]
            )
        )
        copies[-1].start()
    k = [kappa(i) for i in (0, 1, pitch - 2, pitch - 1)]
    ends = faces.weights(-k[0], k[0], k[1]), faces.weights(k[2], k[3], -k[3])
    for n, value in enumerate(ends[0]):
        outer_ref[0, n] = value
    for n, value in enumerate(ends[1]):
        outer_ref[1, n] = value
    outer_ref[0, 7] = w_s[6, 1]
    outer_ref[1, 7] = w_s[5, pitch - 2]
    none = jnp.zeros((faces.rows, axial), F32)
    inner = [[w_s[n, i] for n in range(7)] for i in (1, pitch - 2)]
    for f in range(nfield):
        y2_ref[f, 0], y2_ref[f, 1] = y_s[f, 1], y_s[f, pitch - 2]
        part_ref[f, 0] = faces.step(ends[0], none, state(f, 0), state(f, 1))
        part_ref[f, 1] = faces.step(ends[1], state(f, pitch - 2), state(f, pitch - 1), none)
        part_ref[f, 2, :radial] = faces.step(inner[0], none, y_s[f, 1], y_s[f, 2])[:radial]
        part_ref[f, 3, :radial] = faces.step(inner[1], y_s[f, pitch - 3], y_s[f, pitch - 2], none)[:radial]
    row_ref[...] = jnp.zeros(row_ref.shape, F32)
    q = lax.axis_index("row")
    tile = pl.ds(pl.multiple_of((1 - q) * (axial - LANES), LANES), LANES)
    blank = jnp.zeros((SLAB, LANES), F32)

    @pl.loop(1, pitch - 1, unroll=True)
    def _(i):
        parts = []
        for f in range(nfield):
            parts += slab(y_s[f, i, :radial, tile], y_s[f, i, radial:, tile])
        row_ref[pl.ds(i, 1), :] = near(stator, parts + [blank])[0]

    for copy in copies:
        copy.wait()


def contribution(nspan, pitch, radial, face_ref, beyond, new_rows, window_ref):
    planes = LANES // SLAB
    nfield = planes - 1
    s = lax.axis_index("span")
    stator = lax.axis_index("row") == 0
    count = window_ref.shape[1]
    ghost, farther = window_ref[0], window_ref[1]
    tail = jnp.zeros((count - pitch - 2, LANES), F32)
    own = jnp.concatenate([beyond[0], face_ref[:pitch], beyond[1], tail], 0)
    top = jnp.zeros((1, LANES), F32)
    own_k1 = jnp.concatenate([top, face_ref[pitch : 2 * pitch], top, tail], 0)
    own_new = jnp.concatenate([top, new_rows, top, tail], 0)
    at = 2 * pitch

    def groups(row, g):
        out = row
        for f in range(planes):
            if f != g:
                out = jnp.where(iota(row.shape, 1) // SLAB == f, pltpu.roll(row, (f - g) * SLAB % LANES, 1), out)
        return out

    def speeds(rows):
        rows = TIME_STEP * rows
        return groups(rows[0:1], 0), groups(rows[1:2], 0), groups(rows[0:1], 1)

    sa0, sa1, sp0 = speeds(face_ref[at : at + 2])
    ga0, ga1, gp0 = speeds(window_ref[2, :2])
    shape = (count, LANES)
    lane = iota(shape, 1)
    group = lax.shift_right_logical(lane, power(SLAB))
    radius = lane & (SLAB - 1)

    def spread(x):
        out = x
        for f in range(nfield):
            out = jnp.where(group == f, pltpu.roll(x, (f + 1) * SLAB, 1), out)
        return out

    half = 0.5 * TIME_STEP
    k0, k1, g0, g1 = spread(own), spread(own_k1), spread(ghost), spread(farther)
    wall = ((radius == 7 + radial) & (s == nspan - 1)) | ((radius == 7) & (s == 0))

    def ahead(x):
        return pltpu.roll(x, count - 1, 0)

    def outward(x):
        return pltpu.roll(x, LANES - 1, 1)

    def change(v, k, speed):
        kappa = half * (k + ahead(k))
        up, dn = jnp.maximum(speed, 0.0), jnp.minimum(speed, 0.0)
        along = (up + kappa) * v + (dn - kappa) * ahead(v)
        kappa = jnp.where(wall, 0.0, half * (k + outward(k)))
        across = kappa * (v - outward(v))
        return along - pltpu.roll(along, 1, 0) + across - pltpu.roll(across, 1, 1)

    def face(first, second, speed, kappa):
        lower = jnp.where(stator, first, second)
        upper = jnp.where(stator, second, first)
        return (jnp.maximum(speed, 0.0) + kappa) * lower + (jnp.minimum(speed, 0.0) - kappa) * upper

    sign = jnp.where(stator, 1.0, -1.0)
    speed = 0.5 * (sa0 + ga0)
    kappa = half * (k0 + g0)
    flux = sign * face(own, ghost, speed, kappa)
    shift = -flux
    ghost_new = (
        ghost
        + flux
        - sign * face(ghost, farther, 0.5 * (ga0 + ga1), half * (g0 + g1))
        - change(ghost, g0, gp0)
    )
    flux = sign * face(own_new + shift, ghost_new, speed, kappa)
    inner = 0.5 * (sa0 + sa1)
    kappa = half * (k0 + k1)
    inner = sign * jnp.where(
        stator, jnp.minimum(inner, 0.0) - kappa, jnp.maximum(inner, 0.0) + kappa
    ) * shift
    add0 = shift - change(shift, k0, sp0) + inner - flux
    add1 = -inner
    return add0, add1


def column(stator, adds, i):
    row = iota((LANES, LANES), 0)
    near_row = jnp.where(stator, LANES - 1, 0)
    far_row = jnp.where(stator, LANES - 2, 1)
    far = jnp.where(row == far_row, adds[1][i + 1 : i + 2], 0.0)
    return jnp.where(row == near_row, adds[0][i + 1 : i + 2], far).T


def unpack(npitch, buf_ref, arr_out, arr_ref, sem):
    values = arr_ref.shape[0]
    capacity = arr_ref.shape[1] // npitch
    for p in range(npitch):
        coded = buf_ref[p, 0].astype(F32)
        plain = jnp.where(coded > 0.0, jnp.log2(coded) * (1.0 / CODE), 0.0)
        for j in range(capacity // LANES):
            at = p * capacity + j * LANES
            arr_ref[:, at : at + LANES] = plain[j * values : (j + 1) * values]
    copy = pltpu.make_async_copy(arr_ref, arr_out, sem.at[0])
    copy.start()
    copy.wait()


def extract(npitch, pitch, buf_ref, face_ref, window_ref, ring_s):
    whole = npitch * pitch
    count = window_ref.shape[1]
    for p in range(npitch):
        both = buf_ref[p, 1].astype(F32)
        ring_s[0, p * pitch : (p + 1) * pitch] = both[:pitch]
        ring_s[1, p * pitch : (p + 1) * pitch] = both[pitch : 2 * pitch]
        if p == 0:
            window_ref[2, :8] = both[2 * pitch : 2 * pitch + 8]
    for n in range(2):
        ring_s[n, whole : whole + pitch] = ring_s[n, :pitch]
        ring_s[n, whole + pitch :] = ring_s[n, pitch:count]
    facing = jnp.max(face_ref[2 * pitch + 2 : 2 * pitch + 3]).astype(jnp.int32)
    begin = 2 * pitch * lax.axis_index("pitch") - facing - 1 + 2 * whole
    begin = begin & (whole - 1)
    window_ref[0] = ring_s[0, pl.ds(begin, count), :]
    window_ref[1] = ring_s[1, pl.ds(begin, count), :]


def edges(
    nspan,
    _,
    f_ref,
    k_ref,
    speed_ref,
    halo_ref,
    lower_ref,
    upper_ref,
    y2_ref,
    part_ref,
    outer_ref,
    row_ref,
    o_ref,
    rows_ref,
    beyond_ref,
):
    nfield, pitch, radial, axial = f_ref.shape
    planes = nfield + 1
    stator = lax.axis_index("row") == 0
    faces = Faces(nspan, speed_ref, radial)
    ext = {-1: lower_ref[...].astype(F32), 1: upper_ref[...].astype(F32)}
    sub = iota((EXTRA, axial), 0)
    corner_at = 2 * planes * radial

    def state(f, i):
        if 0 <= i < pitch:
            core = f_ref[f, i] if f < nfield else k_ref[i]
            return jnp.concatenate([core, halo_ref[f * pitch + i]], 0)
        side = ext[-1 if i < 0 else 1]
        at = (2 * f + (i + 2 if i < 0 else i - pitch)) * radial
        extra = jnp.zeros((EXTRA, axial), F32)
        if i in (-1, pitch):
            corner = corner_at + 2 * f
            extra = jnp.where(sub == 0, side[corner : corner + 1], 0.0)
            extra = jnp.where(sub == 7, side[corner + 1 : corner + 2], extra)
        return jnp.concatenate([side[at : at + radial], extra], 0)

    beyond, ends = [], []

    def edge_lanes(value):
        return jnp.where(stator, value[:, axial - LANES :], value[:, :LANES])

    blank = jnp.zeros((SLAB, LANES), F32)
    for side in range(2):
        inside, outside, beyond_it = ((0, -1, -2), (pitch - 1, pitch, pitch + 1))[side]

        def ordered(far, centre, near):
            return (far, centre, near) if side == 0 else (near, centre, far)

        k_in, k_out = state(nfield, inside), state(nfield, outside)
        w_out = faces.weights(*ordered(state(nfield, beyond_it), k_out, k_in))
        kappa = 0.5 * TIME_STEP * (k_in + k_out)
        w_in = [outer_ref[side, n] for n in range(7)]
        w_in[0] = w_in[0] - kappa
        w_in[6 - side] = w_in[6 - side] + kappa
        wind = faces.pitch_up if side == 0 else -faces.pitch_dn
        updated = []
        for f in range(nfield):
            x_in, x_out = state(f, inside), state(f, outside)
            y_out = faces.step(w_out, *ordered(state(f, beyond_it), x_out, x_in))
            y_in = part_ref[f, side] + kappa * (x_out - x_in) + wind * x_out
            new_in = faces.step(w_in, *ordered(y_out, y_in, y2_ref[f, side]))[:radial]
            new_next = part_ref[f, 2 + side, :radial] + (outer_ref[side, 7] * y_in)[:radial]
            o_ref[f, 3 * side] = new_in
            o_ref[f, 1 + side] = new_next
            value = edge_lanes(y_in)
            updated += slab(value[:radial], value[radial:])
        ends.append(near(stator, updated + [blank])[0])
        parts = []
        for f in range(planes):
            value = edge_lanes(state(f, -1 if side == 0 else pitch))
            parts += slab(value[:radial], value[radial:])
        beyond.append(near(stator, parts)[0])
    rows = row_ref[...]
    index = iota(rows.shape, 0)
    rows_ref[...] = jnp.where(index == 0, ends[0], jnp.where(index == pitch - 1, ends[1], rows))
    beyond_ref[...] = jnp.zeros(beyond_ref.shape, F32)
    beyond_ref[0:1] = beyond[0]
    beyond_ref[1:2] = beyond[1]


def finish(nspan, _, mid_ref, edge_ref, face_ref, rows_ref, beyond_ref, window_ref, out_ref, tile_s, sems):
    nfield, pitch, radial, axial = out_ref.shape
    q = lax.axis_index("row")
    near_tile = pl.ds(pl.multiple_of((1 - q) * (axial - LANES), LANES), LANES)
    copies = []
    if axial > LANES:
        rest = pl.ds(pl.multiple_of(q * LANES, LANES), axial - LANES)
        for side in range(2):
            copies.append(
                pltpu.make_async_copy(
                    edge_ref.at[:, 2 * side : 2 * side + 2, :, rest],
                    out_ref.at[:, side * (pitch - 2) : side * (pitch - 2) + 2, :, rest],
                    sems.at[side],
                )
            )
            copies[-1].start()
    beyond = beyond_ref[0:1], beyond_ref[1:2]
    adds = contribution(nspan, pitch, radial, face_ref, beyond, rows_ref[...], window_ref)
    part = pitch // 8
    for n in range(8):
        for i in range(n * part, (n + 1) * part):
            block = column(q == 0, adds, i)
            for f in range(nfield):
                if 2 <= i < pitch - 2:
                    old = mid_ref[f, i - 2, :, near_tile]
                else:
                    old = edge_ref[f, i if i < 2 else i - pitch + 4, :, near_tile]
                tile_s[f, i] = old + block[f * SLAB + 8 : f * SLAB + 8 + radial]
        done = slice(n * part, (n + 1) * part)
        copies.append(
            pltpu.make_async_copy(
                tile_s.at[:, done], out_ref.at[:, done, :, near_tile], sems.at[2 + n]
            )
        )
        copies[-1].start()
    for copy in copies:
        copy.wait()


def local(
    fields,
    diffusivity,
    mean_flow,
    radial_kernel,
    tracer_values,
    tracer_cells,
    tracer_dest,
    interface_map,
):
    npitch = lax.axis_size("pitch")
    nspan = lax.axis_size("span")
    nfield, pitch, radial, axial = fields.shape
    planes = nfield + 1
    values, tracers = tracer_values.shape
    chunks = tracers // LANES
    capacity = 2 * tracers // npitch
    edge = planes * pitch
    cells = tracer_cells.reshape(chunks, LANES)
    dest = tracer_dest.reshape(chunks, LANES)

    mean_rows = 2 * radial
    if nspan == 2:
        outs = [((mean_rows + edge // 2, axial), BF16), ((2 * edge, axial), BF16)]
    else:
        outs = [((2 * edge, axial), BF16)] * 2 + [((edge, LANES), BF16)] * 2
        outs += [((mean_rows, axial), BF16)]
    inputs = [fields, diffusivity, radial_kernel, tracer_values, cells, dest, interface_map, mean_flow]
    *packed, fields, diffusivity, radial_kernel, tracer_values, cells, dest, interface_map = call(
        lambda *refs: pack_span(nspan, len(inputs), *refs),
        outs + [(x.shape, x.dtype) for x in inputs[:-1]],
        [pltpu.with_memory_space_constraint(x, pltpu.HBM) for x in inputs],
        [HBM] * len(inputs),
        [
            pltpu.VMEM(mean_flow.shape, mean_flow.dtype),
            pltpu.SemaphoreType.DMA((len(inputs) + 2,)),
        ],
        nbytes=2**20,
        fixed=True,
    )
    if nspan == 2:
        swap = [(0, 1), (1, 0)]
        span_got = (packed[0], lax.ppermute(packed[0], "span", swap))
        low = high = lax.ppermute(packed[1], "span", swap)
    else:
        upward = [(n, n + 1) for n in range(nspan - 1)]
        downward = [(n + 1, n) for n in range(nspan - 1)]
        low, high = lax.ppermute(packed[0], "span", upward), lax.ppermute(packed[1], "span", downward)
        span_got = (
            lax.ppermute(packed[2], "span", upward),
            lax.ppermute(packed[3], "span", downward),
            lax.all_gather(packed[4], "span"),
        )

    width = min(2 * LANES, capacity)
    sampled = call(
        lambda *refs: sample_fields(npitch, *refs),
        [
            ((8, tracers), F32),
            ((width, tracers), BF16),
            ((1, tracers), jnp.int32),
            ((axial, tracers), BF16),
        ],
        (fields, cells, dest),
        [VMEM] * 3,
        [pltpu.VMEM((nfield, pitch * radial, axial), BF16)],
        flops=4 * nfield * pitch * radial * axial * tracers,
        nbytes=2**20,
    )

    rows = radial + EXTRA
    per_slot = max(values * capacity // LANES, 2 * pitch + 3)
    per_slot = -(-per_slot // 8) * 8
    halo_rows = 2 * planes * radial + 16
    buf, speeds, face = call(
        lambda *refs: dispatch(npitch, nspan, *refs),
        [
            ((npitch, 2, per_slot, LANES), BF16),
            ((2, rows, axial), F32),
            ((per_slot, LANES), F32),
        ],
        (
            fields,
            diffusivity,
            radial_kernel,
            tracer_values,
            cells,
            interface_map,
        )
        + tuple(sampled)
        + span_got,
        [VMEM] * (10 + len(span_got)),
        [
            pltpu.VMEM(radial_kernel.shape, F32),
            pltpu.VMEM((16, tracers), F32),
            pltpu.VMEM((values * npitch * capacity // width, tracers), BF16),
            pltpu.VMEM((values, npitch * capacity // width, width), F32),
            pltpu.VMEM((per_slot, LANES), F32),
            pltpu.VMEM((2, edge, LANES), F32),
        ],
        flops=2 * npitch * values * tracers * capacity,
        nbytes=2**21,
    )
    buf, halo, up, down = call(
        lambda *refs: halos(*refs[1:5], *refs[6:]),
        [((npitch, 2, per_slot, LANES), BF16), ((edge, EXTRA, axial), F32)]
        + [((halo_rows, axial), BF16)] * 2,
        (buf, low, high, fields, diffusivity),
        [ANY] + [VMEM] * 4,
        [pltpu.VMEM((2, 2 * edge, axial), F32)],
        nbytes=2**18,
        place=(ANY, VMEM, VMEM, VMEM),
        passed={0: 0},
    )
    buf = lax.all_to_all(buf, "pitch", 0, 0)
    ring = [(n, (n + 1) % npitch) for n in range(npitch)]
    lower = lax.ppermute(up, "pitch", ring)
    upper = lax.ppermute(down, "pitch", [(b, a) for a, b in ring])

    moved, mid, near_edge, part, outer, new_rows = call(
        lambda *refs: middle(nspan, *refs),
        [
            (fields.shape, F32),
            ((nfield, pitch - 4, radial, axial), F32),
            ((nfield, 2, rows, axial), F32),
            ((nfield, 4, rows, axial), F32),
            ((2, 8, rows, axial), F32),
            ((pitch, LANES), F32),
        ],
        (fields, diffusivity, speeds, halo),
        [VMEM] * 4,
        [
            pltpu.VMEM((nfield, pitch, rows, axial), F32),
            pltpu.VMEM((7, pitch, rows, axial), F32),
            pltpu.SemaphoreType.DMA((1,)),
        ],
        flops=2**24,
        nbytes=2**22,
        place=(ANY,) + (VMEM,) * 5,
    )
    (window,) = call(
        lambda *refs: extract(npitch, pitch, *refs[1:]),
        [((3, pitch + 8, LANES), F32)],
        (new_rows, buf, face),
        [VMEM] * 3,
        [pltpu.VMEM((2, npitch * pitch + pitch + 8, LANES), F32)],
        nbytes=2**18,
    )
    (arrived,) = call(
        lambda *refs: unpack(npitch, *refs[1:]),
        [((values, npitch * capacity), F32)],
        (window, buf),
        [VMEM] * 2,
        [pltpu.VMEM((values, npitch * capacity), F32), pltpu.SemaphoreType.DMA((1,))],
        nbytes=2**20,
        place=ANY,
    )
    near_edge, new_rows, beyond = call(
        lambda *refs: edges(nspan, *refs),
        [
            ((nfield, 4, radial, axial), F32),
            ((pitch, LANES), F32),
            ((8, LANES), F32),
        ],
        (
            window,
            fields,
            diffusivity,
            speeds,
            halo,
            lower,
            upper,
            near_edge,
            part,
            outer,
            new_rows,
        ),
        [VMEM] * 11,
        flops=2**23,
        nbytes=2**21,
    )
    window = lax.ppermute(window, "row", [(0, 1), (1, 0)])
    (moved,) = call(
        lambda *refs: finish(nspan, *refs),
        [(fields.shape, F32)],
        (moved, mid, near_edge, face, new_rows, beyond, window),
        [ANY] + [VMEM] * 6,
        [
            pltpu.VMEM((nfield, pitch, radial, LANES), F32),
            pltpu.SemaphoreType.DMA((10,)),
        ],
        flops=2**22,
        nbytes=2**21,
        place=ANY,
        passed={0: 0},
    )
    return moved, arrived


def solution(mesh):
    placed = (
        P(None, "pitch", "span", "row"),
        P("pitch", "span", "row"),
        P("span", None, "row"),
        P(),
        P(None, ("pitch", "span", "row")),
        P(("pitch", "span", "row")),
        P(("pitch", "span", "row"), None),
        P("row", "pitch"),
    )
    return jax.shard_map(
        local,
        mesh=mesh,
        in_specs=placed,
        out_specs=(P(None, "pitch", "span", "row"), P(None, ("pitch", "span", "row"))),
        check_vma=False,
    )
```
